32 devices in a mesh: dp: 8 (over z, x), mp: 4 (over y, core).
Axes of the slice: x: 2, y: 2, z: 4, core: 2. Of those that a mesh axis runs over, the one named last changes fastest.
Arguments:
- tokens: bfloat16 [16, 664, 768], P('dp'), may hold values from -6 to 6
- cotangent: bfloat16 [16, 664, 768], P('dp'), may hold values from -6 to 6
- step_counts: int32 [16], P('dp'), may hold values from 1 to 2, as said below
- wrist_flags: int32 [16], P('dp'), may hold values 0 or 1
- inward_weight: float32 [3, 768, 768], P(None, 'dp', 'mp'), may hold values from -0.3125 to 0.3125
- outward_weight: float32 [768, 768], P('mp', 'dp'), may hold values from -0.875 to 0.875
- upward_weight: float32 [768, 3072], P('dp', 'mp')
- downward_weight: float32 [3072, 768], P('mp', 'dp'), may hold values from -0.109375 to 0.109375
- norm_table: float32 [4, 768], replicated
- momentum_inward: float32 [3, 768, 768], P(None, 'dp', 'mp'), may hold values from -0.00061035156 to 0.00061035156
- momentum_outward: float32 [768, 768], P('mp', 'dp'), may hold values from -0.00061035156 to 0.00061035156
- momentum_upward: float32 [768, 3072], P('dp', 'mp'), may hold values from -0.00061035156 to 0.00061035156
- momentum_downward: float32 [3072, 768], P('mp', 'dp'), may hold values from -0.00061035156 to 0.00061035156
- momentum_norms: float32 [4, 768], P(None, 'dp'), may hold values from -0.001953125 to 0.001953125
- variance_inward: float32 [3, 768, 768], P(None, 'dp', 'mp'), may hold values from 7.064254e-11 to 1.1302806e-09
- variance_outward: float32 [768, 768], P('mp', 'dp'), may hold values from 7.064254e-11 to 1.1302806e-09
- variance_upward: float32 [768, 3072], P('dp', 'mp'), may hold values from 7.064254e-11 to 1.1302806e-09
- variance_downward: float32 [3072, 768], P('mp', 'dp'), may hold values from 7.064254e-11 to 1.1302806e-09
- variance_norms: float32 [4, 768], P(None, 'dp'), may hold values from 6.3578287e-10 to 1.0172526e-08
Outputs:
- output: bfloat16 [16, 664, 768], P('dp')
- input_grad: float32 [16, 664, 768], P('dp')
- grad_norm: float32 [], replicated
- first_inward: float32 [3, 768, 768], P(None, 'dp', 'mp')
- second_inward: float32 [3, 768, 768], P(None, 'dp', 'mp')
- master_inward: float32 [3, 768, 768], P(None, 'dp', 'mp')
- first_outward: float32 [768, 768], P('mp', 'dp')
- second_outward: float32 [768, 768], P('mp', 'dp')
- master_outward: float32 [768, 768], P('mp', 'dp')
- first_upward: float32 [768, 3072], P('dp', 'mp')
- second_upward: float32 [768, 3072], P('dp', 'mp')
- master_upward: float32 [768, 3072], P('dp', 'mp')
- first_downward: float32 [3072, 768], P('mp', 'dp')
- second_downward: float32 [3072, 768], P('mp', 'dp')
- master_downward: float32 [3072, 768], P('mp', 'dp')
- first_norms: float32 [4, 768], P(None, 'dp')
- second_norms: float32 [4, 768], P(None, 'dp')
- master_norms: float32 [4, 768], P(None, 'dp')
The draws below stay inside these ranges and needn't reach their ends.
Inputs may be any that keep to these rules, and one draw needn't show every extreme that they name: `step_counts`: some item has 2 timesteps and some item has 1.
All inputs are finite; a program needn't handle non-finite values. No bound on the sum of `wrist_flags` on one device may be relied on, other than what follows from the above.
Results may differ from the reference program's by a relative error of at most 0.012.
The reference program's roundings to bfloat16 on the way count: a program that leaves them out, or rounds other values in their place, can miss the bound.
Values may be sent and summed in bfloat16 or wider, within the bound.
A program may use at most 128 MiB of HBM per device.

```python
import math
from functools import partial
import jax
import jax.numpy as jnp
from jax import lax

D = 768
HEADS = 12
FF = 3072
HEAD_DIM = 64
TASK = 16
PRIMARY = 256
WRIST = 64
READOUT = 4
TIMESTEPS = 2
SLOTS = 664
ITEMS = 16
STEP = 10


def draw_step_counts(key, part):
    key = jax.random.fold_in(key, 13)
    key_one, key_two = jax.random.split(key)
    counts = jax.random.randint(key_one, (ITEMS,), 1, TIMESTEPS + 1)
    chosen = jax.random.randint(key_two, (), 0, ITEMS)
    counts = counts.at[chosen].set(TIMESTEPS)
    counts = counts.at[(chosen + 1) % ITEMS].set(1)
    return counts.astype(jnp.int32)


def draw_upward_weight(key, part):
    key = jax.random.fold_in(key, 11)
    key_one, key_two = jax.random.split(key)
    column = jnp.arange(FF, dtype=jnp.float32) / FF
    values = jax.random.normal(key_one, (D, FF), jnp.float32)
    rising = 0.5 + column
    jitter = jax.random.uniform(key_two, (1, FF), jnp.float32, 0.8, 1.2)
    return values * (rising[None, :] * jitter) * D ** (-0.5)


def draw_norm_table(key, part):
    key = jax.random.fold_in(key, 12)
    key_one, key_two = jax.random.split(key)
    column = jnp.arange(D, dtype=jnp.float32) / D
    rising = 0.5 + column
    shifts = 0.3 * jax.random.normal(key_two, (2, D), jnp.float32)
    gains = rising[None, :] * jax.random.uniform(key_one, (2, D), jnp.float32, 0.8, 1.2)
    return jnp.stack([gains[0], shifts[0], gains[1], shifts[1]])


def with_ends(drawn, key, low, top_value):
    dims = drawn.shape
    spot = [jax.random.randint(jax.random.fold_in(key, axis), (), 0, dims[axis]) for axis in range(len(dims))]
    drawn = drawn.at[tuple(spot)].set(low)
    longest = dims.index(max(dims))
    spot[longest] = (spot[longest] + 1) % dims[longest]
    return drawn.at[tuple(spot)].set(top_value)


def level_of(own_key, extent, shards, low, high):
    gain = 1.0
    for dim, blocks in shards:
        draws = jax.random.uniform(jax.random.fold_in(jax.random.fold_in(own_key, 6), dim), (blocks,), jnp.float32, low / len(shards), high / len(shards))
        gain = gain * jnp.repeat(jnp.exp(draws), extent[dim] // blocks).reshape((-1,) + (1,) * (len(extent) - 1 - dim))
    return gain


def scatter_about(own_key, shape, scale, most, cuts=(), kind=jnp.bfloat16):
    values = jax.random.normal(own_key, shape, jnp.float32) * scale
    if len(cuts) > 0:
        values = level_of(own_key, shape, cuts, -0.22, 0.18) * values
    return jnp.clip(values, min=-most, max=most).astype(kind)


def setup_inputs(seed: int = 0) -> dict:
    streams_of = jax.random.split(jax.random.key(seed), 20)
    return {
        "tokens": scatter_about(streams_of[0], (ITEMS, SLOTS, D), 1.0, 6.0, ((0, 8),)),
        "cotangent": scatter_about(streams_of[1], (ITEMS, SLOTS, D), 1.0, 6.0, ((0, 8),)),
        "step_counts": draw_step_counts(jax.random.fold_in(streams_of[19], 71), 0),
        "wrist_flags": with_ends((jax.random.randint(streams_of[3], (ITEMS,), 0, 2) < 1).astype(jnp.int32), jax.random.fold_in(streams_of[3], 1), 0, 1),
        "inward_weight": scatter_about(streams_of[4], (3, D, D), (D // 2) ** -0.5, 0.3125, ((1, 8), (2, 4)), jnp.float32),
        "outward_weight": scatter_about(streams_of[5], (D, D), (D // 16) ** -0.5, 0.875, ((0, 4), (1, 8)), jnp.float32),
        "upward_weight": draw_upward_weight(jax.random.fold_in(streams_of[19], 71), 0),
        "downward_weight": scatter_about(streams_of[7], (FF, D), FF ** -0.5, 0.109375, ((0, 4), (1, 8)), jnp.float32),
        "norm_table": draw_norm_table(jax.random.fold_in(streams_of[19], 71), 0),
        "momentum_inward": scatter_about(streams_of[9], (3, D, D), (0.111 * (4 * D * D + 2 * D * FF) ** -0.5), 0.00061035156, ((1, 8), (2, 4)), jnp.float32),
        "momentum_outward": scatter_about(streams_of[10], (D, D), (0.111 * (4 * D * D + 2 * D * FF) ** -0.5), 0.00061035156, ((0, 4), (1, 8)), jnp.float32),
        "momentum_upward": scatter_about(streams_of[11], (D, FF), (0.111 * (4 * D * D + 2 * D * FF) ** -0.5), 0.00061035156, ((0, 8), (1, 4)), jnp.float32),
        "momentum_downward": scatter_about(streams_of[12], (FF, D), (0.111 * (4 * D * D + 2 * D * FF) ** -0.5), 0.00061035156, ((0, 4), (1, 8)), jnp.float32),
        "momentum_norms": scatter_about(streams_of[13], (4, D), (0.333 * (4 * D * D + 2 * D * FF) ** -0.5), 0.001953125, ((1, 8),), jnp.float32),
        "variance_inward": jnp.clip(jnp.exp(math.log(1.130280646854942e-09) - 2.7725887 * jax.random.uniform(streams_of[14], (3, D, D), jnp.float32) ** level_of(streams_of[14], (3, D, D), ((1, 8), (2, 4)), -0.2, 0.2)), 7.064254042843388e-11, 1.130280646854942e-09),
        "variance_outward": jnp.clip(jnp.exp(math.log(1.130280646854942e-09) - 2.7725887 * jax.random.uniform(streams_of[15], (D, D), jnp.float32) ** level_of(streams_of[15], (D, D), ((0, 4), (1, 8)), -0.2, 0.2)), 7.064254042843388e-11, 1.130280646854942e-09),
        "variance_upward": jnp.clip(jnp.exp(math.log(1.130280646854942e-09) - 2.7725887 * jax.random.uniform(streams_of[16], (D, FF), jnp.float32) ** level_of(streams_of[16], (D, FF), ((0, 8), (1, 4)), -0.2, 0.2)), 7.064254042843388e-11, 1.130280646854942e-09),
        "variance_downward": jnp.clip(jnp.exp(math.log(1.130280646854942e-09) - 2.7725887 * jax.random.uniform(streams_of[17], (FF, D), jnp.float32) ** level_of(streams_of[17], (FF, D), ((0, 4), (1, 8)), -0.2, 0.2)), 7.064254042843388e-11, 1.130280646854942e-09),
        "variance_norms": jnp.clip(jnp.exp(math.log(1.017252593271678e-08) - 2.7725887 * jax.random.uniform(streams_of[18], (4, D), jnp.float32) ** level_of(streams_of[18], (4, D), ((1, 8),), -0.2, 0.2)), 6.357828707947988e-10, 1.017252593271678e-08),
    }


NORM_EPSILON = 1e-06
CLIP_NORM = 1.0
BETA_ONE = 0.9
BETA_TWO = 0.999
ADAM_EPSILON = 1e-08
WEIGHT_DECAY = 0.1
NEGATIVE = -1e+30
RATE_INWARD = 0.05
RATE_OUTWARD = 0.15
RATE_UPWARD = 0.04
RATE_DOWNWARD = 0.02
RATE_NORMS = 0.5

@jax.custom_vjp
def low(v):
    return lax.optimization_barrier(v.astype(jnp.bfloat16)).astype(jnp.float32)

@jax.custom_vjp
def low_back(v):
    return v

def low_keep(v):
    return (low(v), None)

def low_pass(kept, grad):
    return (grad,)

def back_keep(v):
    return (v, None)

def back_low(kept, grad):
    return (low(grad),)
low.defvjp(low_keep, low_pass)
low_back.defvjp(back_keep, back_low)

def slot_mask(live_steps, has_wrist):
    position = jnp.arange(SLOTS, dtype=jnp.int32)
    relative = position - TASK
    period = PRIMARY + WRIST + READOUT
    is_task = relative < 0
    forward_pos = jnp.maximum(relative, 0)
    stepno = forward_pos // period
    offset = forward_pos % period
    not_task = jnp.logical_not(is_task)
    is_read = jnp.logical_and(not_task, offset >= PRIMARY + WRIST)
    is_obs = jnp.logical_and(not_task, jnp.logical_not(is_read))
    is_wrist = jnp.logical_and(is_obs, offset >= PRIMARY)
    present = jnp.logical_or(is_task, jnp.logical_and(stepno < live_steps, jnp.logical_or(jnp.logical_not(is_wrist), has_wrist == 1)))
    see_obs = is_obs[None, :] & not_task[:, None] & (stepno[None, :] <= stepno[:, None])
    see_read = is_read[None, :] & is_read[:, None] & (stepno[None, :] == stepno[:, None])
    return present[None, :] & (is_task[None, :] | see_obs | see_read)

def layer_norm(values, gain_row, shift_row):
    centre = values - lax.optimization_barrier(jnp.mean(values, axis=-1, keepdims=True))
    spread = lax.optimization_barrier(jnp.mean(centre * centre, axis=-1, keepdims=True))
    return centre * lax.rsqrt(spread + NORM_EPSILON) * gain_row + shift_row

def gelu_tanh(values):
    return 0.5 * values * (1.0 + jnp.tanh(0.7978845608028654 * (values + 0.044715 * values * values * values)))

def product(left_side, right_side):
    return jnp.dot(left_side, right_side, precision=lax.Precision.HIGHEST, preferred_element_type=jnp.float32)

def forward(tokens, inward, outward, upward, downward, norm_rows, allowed):
    normed = low(layer_norm(tokens, norm_rows[0], norm_rows[1]))
    inward_low = low(inward)
    queries = low(low_back(product(normed, inward_low[0])))
    key_rows = low(low_back(product(normed, inward_low[1])))
    value_rows = low(low_back(product(normed, inward_low[2])))
    query_heads = queries.reshape(SLOTS, HEADS, HEAD_DIM)
    key_heads = key_rows.reshape(SLOTS, HEADS, HEAD_DIM)
    value_heads = value_rows.reshape(SLOTS, HEADS, HEAD_DIM)
    dotted = jnp.einsum('qhd,khd->hqk', query_heads, key_heads, precision=lax.Precision.HIGHEST) * HEAD_DIM ** (-0.5)
    scores = jnp.where(allowed[None], low_back(dotted), NEGATIVE)
    highest = lax.optimization_barrier(jnp.max(scores, axis=-1, keepdims=True))
    spread = jnp.exp(scores - highest)
    attention = spread / lax.optimization_barrier(jnp.sum(spread, axis=-1, keepdims=True))
    mixed_heads = jnp.einsum('hqk,khd->qhd', low(attention), value_heads, precision=lax.Precision.HIGHEST)
    context = low(low_back(mixed_heads.reshape(SLOTS, D)))
    middle = tokens + low_back(product(context, low(outward)))
    normed_two = low(layer_norm(middle, norm_rows[2], norm_rows[3]))
    upper_pre = low_back(product(normed_two, low(upward)))
    hidden = low(gelu_tanh(upper_pre))
    return middle + low_back(product(hidden, low(downward)))

def adam_update(master, momentum, variance, gradient, clip_scale, step_rate, decay_rate):
    clipped = gradient * clip_scale
    moment_one = BETA_ONE * momentum + (1.0 - BETA_ONE) * clipped
    moment_two = BETA_TWO * variance + (1.0 - BETA_TWO) * clipped * clipped
    first_hat = moment_one / (1.0 - BETA_ONE ** STEP)
    second_hat = moment_two / (1.0 - BETA_TWO ** STEP)
    updated = master - step_rate * (first_hat / (jnp.sqrt(second_hat) + ADAM_EPSILON) + decay_rate * master)
    return (moment_one, moment_two, updated)

def reference(tokens, cotangent, step_counts, wrist_flags, inward_weight, outward_weight, upward_weight, downward_weight, norm_table, momentum_inward, momentum_outward, momentum_upward, momentum_downward, momentum_norms, variance_inward, variance_outward, variance_upward, variance_downward, variance_norms):
    masters = (inward_weight, outward_weight, upward_weight, downward_weight, norm_table)

    def one_item(running, packed):
        item_tokens, item_back, live_steps, has_wrist = packed
        allowed = slot_mask(live_steps, has_wrist)
        result, pullback = jax.vjp(partial(forward, allowed=allowed), item_tokens.astype(jnp.float32), inward_weight, outward_weight, upward_weight, downward_weight, norm_table)
        gradients = pullback(item_back.astype(jnp.float32))
        running = tuple((former + update for former, update in zip(running, gradients[1:])))
        return (running, (result.astype(jnp.bfloat16), gradients[0]))
    empty_sums = tuple((jnp.zeros_like(master) for master in masters))
    totals, (output, input_grad) = lax.scan(one_item, empty_sums, (tokens, cotangent, step_counts, wrist_flags))
    squares = sum((jnp.sum(piece * piece) for piece in totals))
    grad_norm = jnp.sqrt(squares)
    clip_scale = jnp.minimum(1.0, CLIP_NORM / (grad_norm + 1e-06))
    inward_new = adam_update(inward_weight, momentum_inward, variance_inward, totals[0], clip_scale, RATE_INWARD, WEIGHT_DECAY)
    outward_new = adam_update(outward_weight, momentum_outward, variance_outward, totals[1], clip_scale, RATE_OUTWARD, WEIGHT_DECAY)
    upward_new = adam_update(upward_weight, momentum_upward, variance_upward, totals[2], clip_scale, RATE_UPWARD, WEIGHT_DECAY)
    downward_new = adam_update(downward_weight, momentum_downward, variance_downward, totals[3], clip_scale, RATE_DOWNWARD, WEIGHT_DECAY)
    norms_new = adam_update(norm_table, momentum_norms, variance_norms, totals[4], clip_scale, RATE_NORMS, 0.0)
    return (output, input_grad, grad_norm, inward_new[0], inward_new[1], inward_new[2], outward_new[0], outward_new[1], outward_new[2], upward_new[0], upward_new[1], upward_new[2], downward_new[0], downward_new[1], downward_new[2], norms_new[0], norms_new[1], norms_new[2])
```

```python
import jax
import jax.numpy as jnp
from jax import lax
from jax.experimental import pallas as pl
from jax.experimental.pallas import tpu as pltpu
from jax.sharding import PartitionSpec as P

HEAD_DIM = 64
TASK = 16
PRIMARY = 256
WRIST = 64
READOUT = 4
SLOTS = 664
MB = 2
STEP = 10


NORM_EPSILON = 1e-06
CLIP_NORM = 1.0
BETA_ONE = 0.9
BETA_TWO = 0.999
ADAM_EPSILON = 1e-08
WEIGHT_DECAY = 0.1
NEGATIVE = -1e30
RATE_INWARD = 0.05
RATE_OUTWARD = 0.15
RATE_UPWARD = 0.04
RATE_DOWNWARD = 0.02
RATE_NORMS = 0.5


def slot_mask(live_steps, has_wrist):
    position = jnp.arange(SLOTS, dtype=jnp.int32)
    relative = position - TASK
    period = PRIMARY + WRIST + READOUT
    is_task = relative < 0
    forward_pos = jnp.maximum(relative, 0)
    stepno = forward_pos // period
    offset = forward_pos % period
    not_task = jnp.logical_not(is_task)
    is_read = jnp.logical_and(not_task, offset >= PRIMARY + WRIST)
    is_obs = jnp.logical_and(not_task, jnp.logical_not(is_read))
    is_wrist = jnp.logical_and(is_obs, offset >= PRIMARY)
    present = jnp.logical_or(
        is_task,
        jnp.logical_and(
            stepno < live_steps, jnp.logical_or(jnp.logical_not(is_wrist), has_wrist == 1)
        ),
    )
    see_obs = is_obs[None, :] & not_task[:, None] & (stepno[None, :] <= stepno[:, None])
    see_read = is_read[None, :] & is_read[:, None] & (stepno[None, :] == stepno[:, None])
    return present[None, :] & (is_task[None, :] | see_obs | see_read)


def layer_stats(values):
    centre = values - jnp.mean(values, axis=-1, keepdims=True)
    inverse = lax.rsqrt(jnp.mean(centre * centre, axis=-1, keepdims=True) + NORM_EPSILON)
    return (centre * inverse, inverse)


def layer_back(grad_result, normal, inverse, gain_row):
    scaled = grad_result * gain_row
    return inverse * (
        scaled
        - jnp.mean(scaled, axis=-1, keepdims=True)
        - normal * jnp.mean(scaled * normal, axis=-1, keepdims=True)
    )


def gelu_tanh(values):
    return (
        0.5
        * values
        * (1.0 + jnp.tanh(0.7978845608028654 * (values + 0.044715 * values * values * values)))
    )


def attention_scores(queries, key_heads, allowed, score_scale):
    dotted = (
        jnp.einsum("nqhd,nkhd->nhqk", queries, key_heads, preferred_element_type=jnp.float32)
        * score_scale
    )
    return jnp.where(allowed, dotted, NEGATIVE)


def adam_update(master, momentum, variance, gradient, clip_scale, step_rate, decay_rate):
    clipped = gradient * clip_scale
    moment_one = BETA_ONE * momentum + (1.0 - BETA_ONE) * clipped
    moment_two = BETA_TWO * variance + (1.0 - BETA_TWO) * clipped * clipped
    first_hat = moment_one / (1.0 - BETA_ONE**STEP)
    second_hat = moment_two / (1.0 - BETA_TWO**STEP)
    updated = master - step_rate * (
        first_hat / (jnp.sqrt(second_hat) + ADAM_EPSILON) + decay_rate * master
    )
    return (moment_one, moment_two, updated)


def body(
    tokens,
    cotangent,
    step_counts,
    wrist_flags,
    inward_weight,
    outward_weight,
    upward_weight,
    downward_weight,
    norm_table,
    momentum_inward,
    momentum_outward,
    momentum_upward,
    momentum_downward,
    momentum_norms,
    variance_inward,
    variance_outward,
    variance_upward,
    variance_downward,
    variance_norms,
):
    full_inward, full_outward, full_upward, full_downward = (
        lax.all_gather(inward_weight.astype(jnp.bfloat16), "dp", axis=1, tiled=True),
        lax.all_gather(outward_weight.astype(jnp.bfloat16), "dp", axis=1, tiled=True),
        lax.all_gather(upward_weight.astype(jnp.bfloat16), "dp", axis=0, tiled=True),
        lax.all_gather(downward_weight.astype(jnp.bfloat16), "dp", axis=1, tiled=True),
    )
    model_width = norm_table.shape[1]
    local_heads = full_inward.shape[2] // HEAD_DIM
    score_scale = HEAD_DIM ** (-0.5)
    per_batch = tokens.shape[0] // MB
    row_count = per_batch * SLOTS
    share_rows = row_count // lax.axis_size("mp")
    share_start = lax.axis_index("mp") * share_rows
    results = []
    input_grads = []
    local_sums = None
    for batch_index in range(MB):
        start_item = batch_index * per_batch
        block_tokens = (
            tokens[start_item : start_item + per_batch]
            .astype(jnp.float32)
            .reshape(row_count, model_width)
        )
        block_back = (
            cotangent[start_item : start_item + per_batch]
            .astype(jnp.float32)
            .reshape(row_count, model_width)
        )
        allowed = jax.vmap(slot_mask)(
            step_counts[start_item : start_item + per_batch],
            wrist_flags[start_item : start_item + per_batch],
        )[:, None]
        normal_one, inverse_one = layer_stats(block_tokens)
        normed_one = (normal_one * norm_table[0] + norm_table[1]).astype(jnp.bfloat16)
        projected = jnp.einsum(
            "rd,cdm->crm", normed_one, full_inward, preferred_element_type=jnp.float32
        ).astype(jnp.bfloat16)
        triple = projected.reshape(3, per_batch, SLOTS, local_heads, HEAD_DIM)
        queries = triple[0]
        key_heads = triple[1]
        value_heads = triple[2]
        scores = attention_scores(queries, key_heads, allowed, score_scale)
        highest = jnp.max(scores, axis=-1, keepdims=True)
        log_total = highest + jnp.log(jnp.sum(jnp.exp(scores - highest), axis=-1, keepdims=True))
        attention_low = jnp.exp(scores - log_total).astype(jnp.bfloat16)
        context = (
            jnp.einsum(
                "nhqk,nkhd->nqhd", attention_low, value_heads, preferred_element_type=jnp.float32
            )
            .astype(jnp.bfloat16)
            .reshape(row_count, -1)
        )
        attn_terms = jnp.dot(context, full_outward, preferred_element_type=jnp.float32)
        tokens_share = lax.dynamic_slice_in_dim(block_tokens, share_start, share_rows, 0)
        back_share = lax.dynamic_slice_in_dim(block_back, share_start, share_rows, 0)
        middle_share = tokens_share + lax.psum_scatter(
            attn_terms, "mp", scatter_dimension=0, tiled=True
        )
        normal_two, inverse_two = layer_stats(middle_share)
        normed_share = (normal_two * norm_table[2] + norm_table[3]).astype(jnp.bfloat16)
        normed_two = lax.all_gather(normed_share, "mp", axis=0, tiled=True)
        upper_pre = jnp.dot(normed_two, full_upward, preferred_element_type=jnp.float32)
        hidden = gelu_tanh(upper_pre).astype(jnp.bfloat16)
        lowered_share = lax.psum_scatter(
            jnp.dot(hidden, full_downward, preferred_element_type=jnp.float32).astype(jnp.bfloat16),
            "mp",
            scatter_dimension=0,
            tiled=True,
        ).astype(jnp.float32)
        output_share = (middle_share + lowered_share).astype(jnp.bfloat16)
        back_rows = block_back.astype(jnp.bfloat16)
        grad_down = jnp.einsum("rf,rd->fd", hidden, back_rows, preferred_element_type=jnp.float32)
        grad_hidden = jnp.einsum(
            "rd,fd->rf", back_rows, full_downward, preferred_element_type=jnp.float32
        )
        upper_pull = jax.vjp(gelu_tanh, upper_pre)[1]
        grad_upper = upper_pull(grad_hidden)[0].astype(jnp.bfloat16)
        grad_up = jnp.einsum(
            "rd,rf->df", normed_two, grad_upper, preferred_element_type=jnp.float32
        )
        normed_terms = jnp.einsum(
            "rf,df->rd", grad_upper, full_upward, preferred_element_type=jnp.float32
        )
        grad_normed_two = lax.psum_scatter(normed_terms, "mp", scatter_dimension=0, tiled=True)
        gain_two = jnp.sum(grad_normed_two * normal_two, axis=0)
        shift_two = jnp.sum(grad_normed_two, axis=0)
        grad_middle_share = back_share + layer_back(
            grad_normed_two, normal_two, inverse_two, norm_table[2]
        )
        middle_low, output_rows = (
            lax.all_gather(grad_middle_share.astype(jnp.bfloat16), "mp", axis=0, tiled=True),
            lax.all_gather(output_share, "mp", axis=0, tiled=True),
        )
        results.append(output_rows.reshape(per_batch, SLOTS, model_width))
        grad_out = jnp.einsum("rm,rd->md", context, middle_low, preferred_element_type=jnp.float32)
        grad_context = (
            jnp.einsum("rd,md->rm", middle_low, full_outward, preferred_element_type=jnp.float32)
            .astype(jnp.bfloat16)
            .reshape(per_batch, SLOTS, local_heads, HEAD_DIM)
        )
        scores_again = attention_scores(queries, key_heads, allowed, score_scale)
        attention_full = jnp.exp(scores_again - log_total)
        attention_again = attention_full.astype(jnp.bfloat16)
        grad_values = jnp.einsum(
            "nhqk,nqhd->nkhd", attention_again, grad_context, preferred_element_type=jnp.float32
        ).astype(jnp.bfloat16)
        grad_weights = jnp.einsum(
            "nqhd,nkhd->nhqk", grad_context, value_heads, preferred_element_type=jnp.float32
        )
        grad_scores = (
            attention_full
            * (grad_weights - jnp.sum(grad_weights * attention_full, axis=-1, keepdims=True))
        ).astype(jnp.bfloat16)
        grad_queries = (
            jnp.einsum(
                "nhqk,nkhd->nqhd", grad_scores, key_heads, preferred_element_type=jnp.float32
            )
            * score_scale
        ).astype(jnp.bfloat16)
        grad_keys = (
            jnp.einsum("nhqk,nqhd->nkhd", grad_scores, queries, preferred_element_type=jnp.float32)
            * score_scale
        ).astype(jnp.bfloat16)
        grad_triple = jnp.stack([grad_queries, grad_keys, grad_values]).reshape(3, row_count, -1)
        grad_in = jnp.einsum(
            "rd,crm->cdm", normed_one, grad_triple, preferred_element_type=jnp.float32
        )
        first_terms = jnp.einsum(
            "crm,cdm->rd", grad_triple, full_inward, preferred_element_type=jnp.float32
        )
        grad_normed_one = lax.psum_scatter(first_terms, "mp", scatter_dimension=0, tiled=True)
        normal_share = lax.dynamic_slice_in_dim(normal_one, share_start, share_rows, 0)
        inverse_share = lax.dynamic_slice_in_dim(inverse_one, share_start, share_rows, 0)
        gain_one = jnp.sum(grad_normed_one * normal_share, axis=0)
        shift_one = jnp.sum(grad_normed_one, axis=0)
        tokens_grad_share = grad_middle_share + layer_back(
            grad_normed_one, normal_share, inverse_share, norm_table[0]
        )
        table_terms = jnp.stack([gain_one, shift_one, gain_two, shift_two])[None]
        grad_tokens, gathered_tables = (
            lax.all_gather(tokens_grad_share, "mp", axis=0, tiled=True),
            lax.all_gather(table_terms, "mp", axis=0, tiled=True),
        )
        grad_table = jnp.sum(gathered_tables, axis=0)
        input_grads.append(grad_tokens.reshape(per_batch, SLOTS, model_width))
        batch_grads = (grad_in, grad_out, grad_up, grad_down, grad_table)
        if local_sums is None:
            local_sums = batch_grads
        else:
            local_sums = tuple((former + latter for former, latter in zip(local_sums, batch_grads)))
    shards = (
        lax.psum_scatter(local_sums[0], "dp", scatter_dimension=1, tiled=True),
        lax.psum_scatter(local_sums[1], "dp", scatter_dimension=1, tiled=True),
        lax.psum_scatter(local_sums[2], "dp", scatter_dimension=0, tiled=True),
        lax.psum_scatter(local_sums[3], "dp", scatter_dimension=1, tiled=True),
        lax.psum_scatter(local_sums[4], "dp", scatter_dimension=1, tiled=True),
    )
    mp_count = lax.axis_size("mp")
    squares = (
        sum((jnp.sum(piece * piece) for piece in shards[:4]))
        + jnp.sum(shards[4] * shards[4]) / mp_count
    )
    grad_norm = jnp.sqrt(lax.psum(squares, ("dp", "mp")))
    clip_scale = jnp.minimum(1.0, CLIP_NORM / (grad_norm + 1e-06))
    shard_width = shards[4].shape[1]
    own_table = lax.dynamic_slice_in_dim(
        norm_table, lax.axis_index("dp") * shard_width, shard_width, 1
    )
    inward_new = adam_update(
        inward_weight,
        momentum_inward,
        variance_inward,
        shards[0],
        clip_scale,
        RATE_INWARD,
        WEIGHT_DECAY,
    )
    outward_new = adam_update(
        outward_weight,
        momentum_outward,
        variance_outward,
        shards[1],
        clip_scale,
        RATE_OUTWARD,
        WEIGHT_DECAY,
    )
    upward_new = adam_update(
        upward_weight,
        momentum_upward,
        variance_upward,
        shards[2],
        clip_scale,
        RATE_UPWARD,
        WEIGHT_DECAY,
    )
    downward_new = adam_update(
        downward_weight,
        momentum_downward,
        variance_downward,
        shards[3],
        clip_scale,
        RATE_DOWNWARD,
        WEIGHT_DECAY,
    )
    norms_new = adam_update(
        own_table, momentum_norms, variance_norms, shards[4], clip_scale, RATE_NORMS, 0.0
    )
    output = jnp.concatenate(results, axis=0)
    input_grad = jnp.concatenate(input_grads, axis=0)
    return (
        output,
        input_grad,
        grad_norm,
        inward_new[0],
        inward_new[1],
        inward_new[2],
        outward_new[0],
        outward_new[1],
        outward_new[2],
        upward_new[0],
        upward_new[1],
        upward_new[2],
        downward_new[0],
        downward_new[1],
        downward_new[2],
        norms_new[0],
        norms_new[1],
        norms_new[2],
    )


def whole_program(mesh, function):
    placed = (
        P("dp", None, None),
        P("dp", None, None),
        P("dp"),
        P("dp"),
        P(None, "dp", "mp"),
        P("mp", "dp"),
        P("dp", "mp"),
        P("mp", "dp"),
        P(),
        P(None, "dp", "mp"),
        P("mp", "dp"),
        P("dp", "mp"),
        P("mp", "dp"),
        P(None, "dp"),
        P(None, "dp", "mp"),
        P("mp", "dp"),
        P("dp", "mp"),
        P("mp", "dp"),
        P(None, "dp"),
    )
    return jax.shard_map(
        function,
        mesh=mesh,
        in_specs=placed,
        out_specs=(
            P("dp", None, None),
            P("dp", None, None),
            P(),
            P(None, "dp", "mp"),
            P(None, "dp", "mp"),
            P(None, "dp", "mp"),
            P("mp", "dp"),
            P("mp", "dp"),
            P("mp", "dp"),
            P("dp", "mp"),
            P("dp", "mp"),
            P("dp", "mp"),
            P("mp", "dp"),
            P("mp", "dp"),
            P("mp", "dp"),
            P(None, "dp"),
            P(None, "dp"),
            P(None, "dp"),
        ),
        check_vma=False,
    )


NN = (((1,), (0,)), ((), ()))
NT = (((1,), (1,)), ((), ()))
TN = (((0,), (0,)), ((), ()))
MESH = pl.DeviceIdType.MESH
F32 = jnp.float32
BF16 = jnp.bfloat16
ROWS = 672
HALF = ROWS // 2
KEYS = 768
NEAR_KEYS = 384
PERIOD = PRIMARY + WRIST + READOUT


def dot(left, right, dims=NN):
    return lax.dot_general(left, right, dims, preferred_element_type=F32)


def gelu_both(values):
    square = values * values
    inner = 0.7978845608028654 * values * (1.0 + 0.044715 * square)
    bend = jnp.tanh(inner)
    half_up = 0.5 + 0.5 * bend
    slope = half_up + 0.5 * values * (1.0 - bend * bend) * (
        0.7978845608028654 * (1.0 + 0.134145 * square)
    )
    return values * half_up, slope


def key_bits(live_steps, has_wrist):
    place = lax.broadcasted_iota(jnp.int32, (1, KEYS), 1)
    relative = place - TASK
    is_task = relative < 0
    later = relative >= PERIOD
    offset = jnp.where(later, relative - PERIOD, relative)
    is_read = offset >= PRIMARY + WRIST
    is_wrist = jnp.logical_and(offset >= PRIMARY, offset < PRIMARY + WRIST)
    step_of = jnp.where(later, 1, 0)
    alive = jnp.logical_and(
        step_of < live_steps, jnp.logical_or(jnp.logical_not(is_wrist), has_wrist == 1)
    )
    bits = jnp.where(is_read, jnp.where(later, 16, 8), jnp.where(later, 4, 2))
    bits = jnp.where(alive, bits, 0)
    bits = jnp.where(is_task, 1, bits)
    return jnp.where(place < SLOTS, bits, 0)


def query_bits(first):
    place = lax.broadcasted_iota(jnp.int32, (HALF, 1), 0) + first
    relative = place - TASK
    is_task = relative < 0
    later = relative >= PERIOD
    offset = jnp.where(later, relative - PERIOD, relative)
    is_read = offset >= PRIMARY + WRIST
    bits = jnp.where(later, 7, 3) + jnp.where(is_read, jnp.where(later, 16, 8), 0)
    return jnp.where(is_task, 1, bits)


class Sems:
    def __init__(self):
        self.count = 0

    def take(self):
        self.count += 1
        return self.count - 1


N_REMOTE = 64
VMEM_BYTES = 64 * 1024 * 1024 - 65536


def fused_kernel(
    steps, flags, shard_h, tokens_h, back_h, norms,
    output_h, grad_h, shards_out, table_out,
    weights, tokens, back, normed_one, queries, keys, values, probs, heads, context,
    middle, normed_two, hidden, grad_upper, middle_low, out_rows, grad_rows,
    keep, keep_low, send_a, send_b, ysend_a, ysend_b,
    recv_attn, recv_low, recv_mid, recv_first,
    yrecv_attn, yrecv_low, yrecv_mid, yrecv_first,
    grad_mid, grad_triple, total, x_send, x_recv, z_send, z_recv,
    table_mine, table_recv,
    send_sems, recv_sems, local_sems,
):
    dp = lax.axis_index("dp")
    mp = lax.axis_index("mp")
    z, x = dp // 2, dp % 2
    y, c = mp // 2, mp % 2
    core_peer = (dp, y * 2 + 1 - c)
    y_peer = (dp, (1 - y) * 2 + c)
    x_peer = (z * 2 + 1 - x, mp)
    z_peers = [(((z + k) % 4) * 2 + x, mp) for k in (1, 2, 3)]
    all_peers = [core_peer, y_peer, x_peer] + z_peers
    far = 1 - y
    block = weights.shape[1] // 8

    sems = Sems()
    pending = []

    def send(src, dst, peer):
        index = sems.take()
        copy = pltpu.make_async_remote_copy(
            src_ref=src, dst_ref=dst, send_sem=send_sems.at[index], recv_sem=recv_sems.at[index],
            device_id=peer, device_id_type=MESH,
        )
        copy.start()
        pending.append(copy)
        return copy

    def done_sending(copy):
        copy.wait_send()
        pending[:] = [other for other in pending if other is not copy]

    def block_rows(index):
        return pl.ds(pl.multiple_of(index * block, 32), block)

    def half_rows(half):
        return pl.ds(pl.multiple_of(half * HALF, 16), HALF)

    own_block = block_rows(dp)
    loads = [
        pltpu.make_async_copy(shard_h.at[i], weights.at[i, own_block], local_sems.at[i])
        for i in range(3)
    ]
    loads.append(pltpu.make_async_copy(tokens_h, tokens, local_sems.at[3]))
    loads.append(pltpu.make_async_copy(back_h, back, local_sems.at[4]))
    for load in loads:
        load.start()

    barrier = pltpu.get_barrier_semaphore()
    for peer in all_peers:
        pl.semaphore_signal(barrier, inc=1, device_id=peer, device_id_type=MESH)
    pl.semaphore_wait(barrier, len(all_peers))

    z_copies = {}
    x_copies = {}

    def weights_out(mat):
        loads[mat].wait()
        rows = weights.at[mat, own_block]
        for k in (1, 2, 3):
            z_copies[mat, k] = send(rows, rows, z_peers[k - 1])
        x_copies[mat, 0] = send(rows, rows, x_peer)

    def weights_on(mat):
        for k in (1, 3, 2):
            z_copies[mat, k].wait_recv()
            rows = weights.at[mat, block_rows(((z + 4 - k) % 4) * 2 + x)]
            x_copies[mat, k] = send(rows, rows, x_peer)

    def weights_in(mat):
        for k in (0, 1, 3, 2):
            x_copies[mat, k].wait_recv()

    def norm_stats(rows):
        centre = rows - jnp.mean(rows, axis=-1, keepdims=True)
        inverse = lax.rsqrt(jnp.mean(centre * centre, axis=-1, keepdims=True) + NORM_EPSILON)
        return centre * inverse, inverse

    def norm_back(grad_result, normal, inverse, gain_row):
        scaled = grad_result * gain_row
        return inverse * (
            scaled
            - jnp.mean(scaled, axis=-1, keepdims=True)
            - normal * jnp.mean(scaled * normal, axis=-1, keepdims=True)
        )

    def first_norm(item):
        @pl.loop(0, ROWS // 112)
        def _(index):
            rows = pl.ds(pl.multiple_of(index * 112, 16), 112)
            normal, _ = norm_stats(tokens[item, rows, :].astype(F32))
            normed_one[item, rows, :] = (normal * norms[0:1, :] + norms[1:2, :]).astype(BF16)

    weights_out(0)
    loads[3].wait()
    first_norm(far)
    weights_on(0)
    weights_out(1)
    weights_out(2)
    first_norm(y)
    loads[4].wait()
    zero_rows = jnp.zeros((KEYS - ROWS, HEAD_DIM), BF16)
    for i in range(6):
        keys[i, ROWS:KEYS, :] = zero_rows
        values[i, ROWS:KEYS, :] = zero_rows
    weights_in(0)

    def project(item):
        @pl.loop(0, 2)
        def _(half):
            rows = half_rows(half)
            joined = dot(normed_one[item, rows, :], weights[0, :, 0:576])
            for head in range(3):
                low = head * HEAD_DIM
                queries[item * 3 + head, rows, :] = (
                    joined[:, low : low + HEAD_DIM].astype(BF16) * HEAD_DIM ** (-0.5)
                ).astype(BF16)
                low += 192
                keys[item * 3 + head, rows, :] = joined[:, low : low + HEAD_DIM].astype(BF16)
                low += 192
                values[item * 3 + head, rows, :] = joined[:, low : low + HEAD_DIM].astype(BF16)

    def attend(item):
        bits = key_bits(steps[item], flags[item])

        @pl.loop(0, 3)
        def _(head):
            at = item * 3 + head
            for half, extent in ((0, NEAR_KEYS), (1, KEYS)):
                first = half * HALF
                scores = dot(queries[at, first : first + HALF, :], keys[at, 0:extent, :], NT)
                seen = jnp.bitwise_and(bits[:, 0:extent], query_bits(first)) != 0
                scores = jnp.where(seen, scores, NEGATIVE)
                spread = jnp.exp(scores - jnp.max(scores, axis=-1, keepdims=True))
                scale = 1.0 / jnp.sum(spread, axis=-1, keepdims=True)
                low = (spread * scale).astype(BF16)
                probs[at, first : first + HALF, 0:extent] = low
                heads[at, first : first + HALF, :] = dot(low, values[at, 0:extent, :]).astype(BF16)

    def join_heads(source, item, half):
        rows = half_rows(half)
        return jnp.concatenate([source[item * 3 + head, rows, :] for head in range(3)], axis=1)

    def attention_out(item, slot):
        for half in (0, 1):
            context[item, half * HALF : (half + 1) * HALF, :] = join_heads(heads, item, half)
        outward = weights[0, :, 576:768]
        send_a[slot] = dot(context[item, half_rows(1 - c), :], outward, NT).astype(BF16)
        copy = send(send_a.at[slot], recv_attn.at[slot], core_peer)
        keep[slot] = dot(context[item, half_rows(c), :], outward, NT)
        return copy

    project(far)
    attend(far)
    attn_far = attention_out(far, 0)
    project(y)
    attn_far.wait_recv()
    ysend_a[...] = (keep[0] + recv_attn[0].astype(F32)).astype(BF16)
    attn_y = send(ysend_a, yrecv_attn, y_peer)
    weights_on(1)
    attend(y)
    weights_on(2)
    attn_near = attention_out(y, 1)
    attn_near.wait_recv()
    attn_y.wait_recv()
    mine = half_rows(c)
    middle[...] = (
        tokens[y, mine, :].astype(F32)
        + keep[1]
        + recv_attn[1].astype(F32)
        + yrecv_attn[...].astype(F32)
    )
    normal_two, _ = norm_stats(middle[...])
    normed_two[y, mine, :] = (normal_two * norms[2:3, :] + norms[3:4, :]).astype(BF16)

    def share_rows(buffer):
        rows = buffer.at[y, mine]
        return send(rows, rows, core_peer), send(rows, rows, y_peer)

    def pass_on(buffer, copy):
        copy.wait_recv()
        rows = buffer.at[far, mine]
        return send(rows, rows, core_peer)

    two_core, two_y = share_rows(normed_two)
    weights_in(1)
    weights_in(2)
    done_sending(attn_far)
    done_sending(attn_near)
    done_sending(attn_y)

    def feed_forward(item, half, keep_slot, send_slot):
        rows = half_rows(half)
        upper = dot(normed_two[item, rows, :], weights[1])
        grown, slope = gelu_both(upper)
        grown = grown.astype(BF16)
        hidden[item, rows, :] = grown
        pull = (dot(back[item, rows, :], weights[2]) * slope).astype(BF16)
        grad_upper[item, rows, :] = pull
        terms = dot(pull, weights[1], NT)
        lowered = dot(grown, weights[2], NT)
        if keep_slot is not None:
            keep[keep_slot] = terms
            keep_low[keep_slot] = lowered
            return None
        send_a[send_slot] = terms.astype(BF16)
        first = send(send_a.at[send_slot], recv_mid.at[send_slot], core_peer)
        send_b[send_slot] = lowered.astype(BF16)
        return first, send(send_b.at[send_slot], recv_low.at[send_slot], core_peer)

    feed_forward(y, c, 1, None)
    two_core.wait_recv()
    mid_near, low_near = feed_forward(y, 1 - c, None, 1)
    two_on = pass_on(normed_two, two_y)
    feed_forward(far, c, 0, None)
    two_on.wait_recv()
    mid_far, low_far = feed_forward(far, 1 - c, None, 0)
    mid_far.wait_recv()
    ysend_a[...] = (keep[0] + recv_mid[0].astype(F32)).astype(BF16)
    mid_y = send(ysend_a, yrecv_mid, y_peer)
    low_far.wait_recv()
    ysend_b[...] = (keep_low[0] + recv_low[0].astype(F32)).astype(BF16)
    low_y = send(ysend_b, yrecv_low, y_peer)

    def band_grad(slot, first, width, left_of, right_of):
        total[slot, :, first : first + width] = dot(left_of(0), right_of(0), TN) + dot(
            left_of(1), right_of(1), TN
        )

    def grads_out(mat, slot):
        for k in range(4):
            x_send[mat, k] = total[slot, block_rows(2 * k + 1 - x), :].astype(BF16)
        return send(x_send.at[mat], x_recv.at[mat], x_peer)

    def grads_on(mat, slot, copy):
        copy.wait_recv()
        sent = []
        for k in (2, 1, 3):
            other = (z + k) % 4
            z_send[mat, k - 1] = (
                total[slot, block_rows(2 * other + x), :] + x_recv[mat, other].astype(F32)
            ).astype(BF16)
            sent.append(send(z_send.at[mat, k - 1], z_recv.at[mat, k - 1], z_peers[k - 1]))
        shards_out[mat] = total[slot, own_block, :] + x_recv[mat, z].astype(F32)
        return sent

    def grads_in(mat, sent):
        for copy in sent:
            copy.wait_recv()
        summed = shards_out[mat]
        for k in range(3):
            summed += z_recv[mat, k].astype(F32)
        shards_out[mat] = summed
        return jnp.sum(summed * summed)

    for first in (0, 256, 512):
        band_grad(
            0, first, 256,
            lambda i: back[i], lambda i, f=first: hidden[i, :, f : f + 256],
        )
    down_x = grads_out(2, 0)
    for first in (0, 256, 512):
        band_grad(
            1, first, 256,
            lambda i: normed_two[i], lambda i, f=first: grad_upper[i, :, f : f + 256],
        )
    up_x = grads_out(1, 1)

    mid_near.wait_recv()
    mid_y.wait_recv()
    grad_two = keep[1] + recv_mid[1].astype(F32) + yrecv_mid[...].astype(F32)
    normal_two, inverse_two = norm_stats(middle[...])
    table_mine[2:3, :] = jnp.sum(grad_two * normal_two, axis=0, keepdims=True)
    table_mine[3:4, :] = jnp.sum(grad_two, axis=0, keepdims=True)
    grad_mid[...] = back[y, mine, :].astype(F32) + norm_back(
        grad_two, normal_two, inverse_two, norms[2:3, :]
    )
    middle_low[y, mine, :] = grad_mid[...].astype(BF16)
    ml_core, ml_y = share_rows(middle_low)

    low_near.wait_recv()
    low_y.wait_recv()
    out_rows[y, mine, :] = (
        middle[...] + keep_low[1] + recv_low[1].astype(F32) + yrecv_low[...].astype(F32)
    ).astype(BF16)
    out_core, out_y = share_rows(out_rows)
    done_sending(mid_near)
    done_sending(mid_far)
    done_sending(mid_y)
    down_z = grads_on(2, 0, down_x)

    def attend_back(item):
        for half in (0, 1):
            rows = half_rows(half)
            pulled = dot(middle_low[item, rows, :], weights[0, :, 576:768]).astype(BF16)
            for head in range(3):
                heads[item * 3 + head, rows, :] = pulled[:, head * HEAD_DIM : (head + 1) * HEAD_DIM]

        @pl.loop(0, 3)
        def _(head):
            at = item * 3 + head
            grad_key = None
            grad_value = None
            key_rows = keys[at]
            value_rows = values[at]
            for half, extent in ((1, KEYS), (0, NEAR_KEYS)):
                first = half * HALF
                rows = slice(first, first + HALF)
                pulled = heads[at, rows, :]
                weight = dot(pulled, value_rows[0:extent], NT)
                low = probs[at, rows, 0:extent]
                wide = low.astype(F32)
                weight = wide * weight
                moved = (weight - wide * jnp.sum(weight, axis=-1, keepdims=True)).astype(BF16)
                asked = queries[at, rows, :]
                part_key = dot(moved, asked, TN)
                part_value = dot(low, pulled, TN)
                queries[at, rows, :] = (
                    dot(moved, key_rows[0:extent]) * HEAD_DIM ** (-0.5)
                ).astype(BF16)
                if grad_key is None:
                    grad_key, grad_value = part_key, part_value
                else:
                    keys[at, 0:extent, :] = (grad_key[0:extent] + part_key).astype(BF16)
                    values[at, 0:extent, :] = (grad_value[0:extent] + part_value).astype(BF16)
                    keys[at, extent:KEYS, :] = grad_key[extent:KEYS].astype(BF16)
                    values[at, extent:KEYS, :] = grad_value[extent:KEYS].astype(BF16)

        for half in (0, 1):
            rows = slice(half * HALF, (half + 1) * HALF)
            grad_triple[item, rows, :] = jnp.concatenate(
                [
                    source[item * 3 + head, rows, :]
                    for source in (queries, keys, values)
                    for head in range(3)
                ],
                axis=1,
            )

    def first_terms(item, slot):
        inward = weights[0, :, 0:576]
        send_a[slot] = dot(grad_triple[item, half_rows(1 - c), :], inward, NT).astype(BF16)
        copy = send(send_a.at[slot], recv_first.at[slot], core_peer)
        keep[slot] = dot(grad_triple[item, half_rows(c), :], inward, NT)
        return copy

    ml_on = pass_on(middle_low, ml_y)
    ml_on.wait_recv()
    attend_back(far)
    first_far = first_terms(far, 0)
    up_z = grads_on(1, 1, up_x)
    out_on = pass_on(out_rows, out_y)
    first_far.wait_recv()
    ysend_a[...] = (keep[0] + recv_first[0].astype(F32)).astype(BF16)
    first_y = send(ysend_a, yrecv_first, y_peer)
    ml_core.wait_recv()
    attend_back(y)
    first_near = first_terms(y, 1)
    for first, width in ((0, 256), (256, 256), (512, 64)):
        band_grad(
            0, first, width,
            lambda i: normed_one[i], lambda i, f=first, w=width: grad_triple[i, :, f : f + w],
        )
    band_grad(0, 576, 192, lambda i: middle_low[i], lambda i: context[i])
    in_x = grads_out(0, 0)

    first_near.wait_recv()
    first_y.wait_recv()
    grad_one = keep[1] + recv_first[1].astype(F32) + yrecv_first[...].astype(F32)
    normal_one, inverse_one = norm_stats(tokens[y, mine, :].astype(F32))
    table_mine[0:1, :] = jnp.sum(grad_one * normal_one, axis=0, keepdims=True)
    table_mine[1:2, :] = jnp.sum(grad_one, axis=0, keepdims=True)
    grad_rows[y, mine, :] = (
        grad_mid[...] + norm_back(grad_one, normal_one, inverse_one, norms[0:1, :])
    ).astype(BF16)
    rows_core, rows_y = share_rows(grad_rows)

    out_core.wait_recv()
    out_on.wait_recv()
    store_out = pltpu.make_async_copy(out_rows, output_h, local_sems.at[5])
    store_out.start()
    in_z = grads_on(0, 0, in_x)
    squares = grads_in(2, down_z) + grads_in(1, up_z)
    rows_on = pass_on(grad_rows, rows_y)
    squares += grads_in(0, in_z)
    table_mine[4:8, :] = jnp.broadcast_to(squares, (4, table_mine.shape[1]))

    rows_core.wait_recv()
    rows_on.wait_recv()
    store_rows = pltpu.make_async_copy(grad_rows, grad_h, local_sems.at[6])
    store_rows.start()

    at_hop = 0
    for peer in (core_peer, y_peer, x_peer):
        hop = send(table_mine, table_recv.at[at_hop], peer)
        hop.wait_recv()
        done_sending(hop)
        table_mine[...] = table_mine[...] + table_recv[at_hop]
        at_hop += 1
    hops = []
    for k in (1, 2, 3):
        hops.append(send(table_mine, table_recv.at[2 + k], z_peers[k - 1]))
    for hop in hops:
        hop.wait_recv()
    parts = [table_mine[...], table_recv[3], table_recv[4], table_recv[5]]
    ordered = None
    for level in range(4):
        piece = parts[0]
        for k in (1, 2, 3):
            piece = jnp.where((level + k) % 4 == z, parts[k], piece)
        ordered = piece if ordered is None else ordered + piece
    table_out[...] = ordered

    store_out.wait()
    store_rows.wait()
    for copy in list(pending):
        copy.wait_send()


def fused_body(
    tokens, cotangent, step_counts, wrist_flags,
    inward_weight, outward_weight, upward_weight, downward_weight, norm_table,
    momentum_inward, momentum_outward, momentum_upward, momentum_downward, momentum_norms,
    variance_inward, variance_outward, variance_upward, variance_downward, variance_norms,
):
    width = norm_table.shape[1]
    block = upward_weight.shape[0]
    shard = jnp.stack(
        [
            jnp.concatenate(
                [inward_weight[0], inward_weight[1], inward_weight[2], outward_weight.T], axis=1
            ),
            upward_weight,
            downward_weight.T,
        ]
    ).astype(BF16)
    padding = ((0, 0), (0, ROWS - SLOTS), (0, 0))
    any_spec = pl.BlockSpec(memory_space=pl.ANY)
    vmem = pl.BlockSpec(memory_space=pltpu.VMEM)
    smem = pl.BlockSpec(memory_space=pltpu.SMEM)
    rows = pltpu.VMEM((2, ROWS, width), BF16)
    halves = pltpu.VMEM((2, HALF, width), BF16)
    half = pltpu.VMEM((HALF, width), BF16)
    keep = pltpu.VMEM((2, HALF, width), F32)
    output, grads, shards, table = pl.pallas_call(
        fused_kernel,
        out_shape=(
            jax.ShapeDtypeStruct((2, ROWS, width), BF16),
            jax.ShapeDtypeStruct((2, ROWS, width), BF16),
            jax.ShapeDtypeStruct((3, block, width), F32),
            jax.ShapeDtypeStruct((8, width), F32),
        ),
        in_specs=[smem, smem, any_spec, any_spec, any_spec, vmem],
        out_specs=(any_spec, any_spec, vmem, vmem),
        scratch_shapes=[
            pltpu.VMEM((3, width, width), BF16),
            rows,
            rows,
            rows,
            pltpu.VMEM((6, ROWS, HEAD_DIM), BF16),
            pltpu.VMEM((6, KEYS, HEAD_DIM), BF16),
            pltpu.VMEM((6, KEYS, HEAD_DIM), BF16),
            pltpu.VMEM((6, ROWS, KEYS), BF16),
            pltpu.VMEM((6, ROWS, HEAD_DIM), BF16),
            pltpu.VMEM((2, ROWS, 192), BF16),
            pltpu.VMEM((HALF, width), F32),
            rows,
            rows,
            rows,
            rows,
            rows,
            rows,
            keep,
            keep,
            halves,
            halves,
            half,
            half,
            halves,
            halves,
            halves,
            halves,
            half,
            half,
            half,
            half,
            pltpu.VMEM((HALF, width), F32),
            pltpu.VMEM((2, ROWS, 576), BF16),
            pltpu.VMEM((2, width, width), F32),
            pltpu.VMEM((3, 4, block, width), BF16),
            pltpu.VMEM((3, 4, block, width), BF16),
            pltpu.VMEM((3, 3, block, width), BF16),
            pltpu.VMEM((3, 3, block, width), BF16),
            pltpu.VMEM((8, width), F32),
            pltpu.VMEM((6, 8, width), F32),
            pltpu.SemaphoreType.DMA((N_REMOTE,)),
            pltpu.SemaphoreType.DMA((N_REMOTE,)),
            pltpu.SemaphoreType.DMA((7,)),
        ],
        compiler_params=pltpu.CompilerParams(
            collective_id=0, has_side_effects=True, vmem_limit_bytes=VMEM_BYTES
        ),
        name="block_step",
    )(
        step_counts,
        wrist_flags,
        shard,
        jnp.pad(tokens, padding),
        jnp.pad(cotangent, padding),
        norm_table,
    )
    part = inward_weight.shape[2]
    grad_inward = jnp.stack([shards[0, :, i * part : (i + 1) * part] for i in range(3)])
    grad_outward = shards[0, :, 3 * part :].T
    table_sums = table[:4]
    grad_norm = jnp.sqrt(table[4, 0] + jnp.sum(table_sums * table_sums))
    clip_scale = jnp.minimum(1.0, CLIP_NORM / (grad_norm + 1e-06))
    shard_width = momentum_norms.shape[1]
    start = lax.axis_index("dp") * shard_width
    own_table = lax.dynamic_slice_in_dim(norm_table, start, shard_width, 1)
    own_sums = lax.dynamic_slice_in_dim(table_sums, start, shard_width, 1)
    updated = []
    for master, momentum, variance, gradient, rate, decay in (
        (inward_weight, momentum_inward, variance_inward, grad_inward, RATE_INWARD, WEIGHT_DECAY),
        (outward_weight, momentum_outward, variance_outward, grad_outward, RATE_OUTWARD, WEIGHT_DECAY),
        (upward_weight, momentum_upward, variance_upward, shards[1], RATE_UPWARD, WEIGHT_DECAY),
        (downward_weight, momentum_downward, variance_downward, shards[2].T, RATE_DOWNWARD, WEIGHT_DECAY),
        (own_table, momentum_norms, variance_norms, own_sums, RATE_NORMS, 0.0),
    ):
        updated.extend(adam_update(master, momentum, variance, gradient, clip_scale, rate, decay))
    return (
        output[:, :SLOTS],
        grads[:, :SLOTS].astype(F32),
        grad_norm,
        *updated,
    )


def solution(mesh):
    fits = mesh.shape["dp"] == 8 and mesh.shape["mp"] == 4
    return whole_program(mesh, fused_body if fits else body)
```

```python
import jax
import jax.numpy as jnp
from jax import lax
from jax.experimental import pallas as pl
from jax.experimental.pallas import tpu as pltpu
from jax.sharding import PartitionSpec as P

HEAD_DIM = 64
TASK = 16
PRIMARY = 256
WRIST = 64
READOUT = 4
SLOTS = 664
MB = 2
STEP = 10


NORM_EPSILON = 1e-06
CLIP_NORM = 1.0
BETA_ONE = 0.9
BETA_TWO = 0.999
ADAM_EPSILON = 1e-08
WEIGHT_DECAY = 0.1
NEGATIVE = -1e30
RATE_INWARD = 0.05
RATE_OUTWARD = 0.15
RATE_UPWARD = 0.04
RATE_DOWNWARD = 0.02
RATE_NORMS = 0.5


def slot_mask(live_steps, has_wrist):
    position = jnp.arange(SLOTS, dtype=jnp.int32)
    relative = position - TASK
    period = PRIMARY + WRIST + READOUT
    is_task = relative < 0
    forward_pos = jnp.maximum(relative, 0)
    stepno = forward_pos // period
    offset = forward_pos % period
    not_task = jnp.logical_not(is_task)
    is_read = jnp.logical_and(not_task, offset >= PRIMARY + WRIST)
    is_obs = jnp.logical_and(not_task, jnp.logical_not(is_read))
    is_wrist = jnp.logical_and(is_obs, offset >= PRIMARY)
    present = jnp.logical_or(
        is_task,
        jnp.logical_and(
            stepno < live_steps, jnp.logical_or(jnp.logical_not(is_wrist), has_wrist == 1)
        ),
    )
    see_obs = is_obs[None, :] & not_task[:, None] & (stepno[None, :] <= stepno[:, None])
    see_read = is_read[None, :] & is_read[:, None] & (stepno[None, :] == stepno[:, None])
    return present[None, :] & (is_task[None, :] | see_obs | see_read)


def layer_stats(values):
    centre = values - jnp.mean(values, axis=-1, keepdims=True)
    inverse = lax.rsqrt(jnp.mean(centre * centre, axis=-1, keepdims=True) + NORM_EPSILON)
    return (centre * inverse, inverse)


def layer_back(grad_result, normal, inverse, gain_row):
    scaled = grad_result * gain_row
    return inverse * (
        scaled
        - jnp.mean(scaled, axis=-1, keepdims=True)
        - normal * jnp.mean(scaled * normal, axis=-1, keepdims=True)
    )


def gelu_tanh(values):
    return (
        0.5
        * values
        * (1.0 + jnp.tanh(0.7978845608028654 * (values + 0.044715 * values * values * values)))
    )


def attention_scores(queries, key_heads, allowed, score_scale):
    dotted = (
        jnp.einsum("nqhd,nkhd->nhqk", queries, key_heads, preferred_element_type=jnp.float32)
        * score_scale
    )
    return jnp.where(allowed, dotted, NEGATIVE)


def adam_update(master, momentum, variance, gradient, clip_scale, step_rate, decay_rate):
    clipped = gradient * clip_scale
    moment_one = BETA_ONE * momentum + (1.0 - BETA_ONE) * clipped
    moment_two = BETA_TWO * variance + (1.0 - BETA_TWO) * clipped * clipped
    first_hat = moment_one / (1.0 - BETA_ONE**STEP)
    second_hat = moment_two / (1.0 - BETA_TWO**STEP)
    updated = master - step_rate * (
        first_hat / (jnp.sqrt(second_hat) + ADAM_EPSILON) + decay_rate * master
    )
    return (moment_one, moment_two, updated)


def body(
    tokens,
    cotangent,
    step_counts,
    wrist_flags,
    inward_weight,
    outward_weight,
    upward_weight,
    downward_weight,
    norm_table,
    momentum_inward,
    momentum_outward,
    momentum_upward,
    momentum_downward,
    momentum_norms,
    variance_inward,
    variance_outward,
    variance_upward,
    variance_downward,
    variance_norms,
):
    full_inward, full_outward, full_upward, full_downward = (
        lax.all_gather(inward_weight.astype(jnp.bfloat16), "dp", axis=1, tiled=True),
        lax.all_gather(outward_weight.astype(jnp.bfloat16), "dp", axis=1, tiled=True),
        lax.all_gather(upward_weight.astype(jnp.bfloat16), "dp", axis=0, tiled=True),
        lax.all_gather(downward_weight.astype(jnp.bfloat16), "dp", axis=1, tiled=True),
    )
    model_width = norm_table.shape[1]
    local_heads = full_inward.shape[2] // HEAD_DIM
    score_scale = HEAD_DIM ** (-0.5)
    per_batch = tokens.shape[0] // MB
    row_count = per_batch * SLOTS
    share_rows = row_count // lax.axis_size("mp")
    share_start = lax.axis_index("mp") * share_rows
    results = []
    input_grads = []
    local_sums = None
    for batch_index in range(MB):
        start_item = batch_index * per_batch
        block_tokens = (
            tokens[start_item : start_item + per_batch]
            .astype(jnp.float32)
            .reshape(row_count, model_width)
        )
        block_back = (
            cotangent[start_item : start_item + per_batch]
            .astype(jnp.float32)
            .reshape(row_count, model_width)
        )
        allowed = jax.vmap(slot_mask)(
            step_counts[start_item : start_item + per_batch],
            wrist_flags[start_item : start_item + per_batch],
        )[:, None]
        normal_one, inverse_one = layer_stats(block_tokens)
        normed_one = (normal_one * norm_table[0] + norm_table[1]).astype(jnp.bfloat16)
        projected = jnp.einsum(
            "rd,cdm->crm", normed_one, full_inward, preferred_element_type=jnp.float32
        ).astype(jnp.bfloat16)
        triple = projected.reshape(3, per_batch, SLOTS, local_heads, HEAD_DIM)
        queries = triple[0]
        key_heads = triple[1]
        value_heads = triple[2]
        scores = attention_scores(queries, key_heads, allowed, score_scale)
        highest = jnp.max(scores, axis=-1, keepdims=True)
        log_total = highest + jnp.log(jnp.sum(jnp.exp(scores - highest), axis=-1, keepdims=True))
        attention_low = jnp.exp(scores - log_total).astype(jnp.bfloat16)
        context = (
            jnp.einsum(
                "nhqk,nkhd->nqhd", attention_low, value_heads, preferred_element_type=jnp.float32
            )
            .astype(jnp.bfloat16)
            .reshape(row_count, -1)
        )
        attn_terms = jnp.dot(context, full_outward, preferred_element_type=jnp.float32)
        tokens_share = lax.dynamic_slice_in_dim(block_tokens, share_start, share_rows, 0)
        back_share = lax.dynamic_slice_in_dim(block_back, share_start, share_rows, 0)
        middle_share = tokens_share + lax.psum_scatter(
            attn_terms, "mp", scatter_dimension=0, tiled=True
        )
        normal_two, inverse_two = layer_stats(middle_share)
        normed_share = (normal_two * norm_table[2] + norm_table[3]).astype(jnp.bfloat16)
        normed_two = lax.all_gather(normed_share, "mp", axis=0, tiled=True)
        upper_pre = jnp.dot(normed_two, full_upward, preferred_element_type=jnp.float32)
        hidden = gelu_tanh(upper_pre).astype(jnp.bfloat16)
        lowered_share = lax.psum_scatter(
            jnp.dot(hidden, full_downward, preferred_element_type=jnp.float32).astype(jnp.bfloat16),
            "mp",
            scatter_dimension=0,
            tiled=True,
        ).astype(jnp.float32)
        output_share = (middle_share + lowered_share).astype(jnp.bfloat16)
        back_rows = block_back.astype(jnp.bfloat16)
        grad_down = jnp.einsum("rf,rd->fd", hidden, back_rows, preferred_element_type=jnp.float32)
        grad_hidden = jnp.einsum(
            "rd,fd->rf", back_rows, full_downward, preferred_element_type=jnp.float32
        )
        upper_pull = jax.vjp(gelu_tanh, upper_pre)[1]
        grad_upper = upper_pull(grad_hidden)[0].astype(jnp.bfloat16)
        grad_up = jnp.einsum(
            "rd,rf->df", normed_two, grad_upper, preferred_element_type=jnp.float32
        )
        normed_terms = jnp.einsum(
            "rf,df->rd", grad_upper, full_upward, preferred_element_type=jnp.float32
        )
        grad_normed_two = lax.psum_scatter(normed_terms, "mp", scatter_dimension=0, tiled=True)
        gain_two = jnp.sum(grad_normed_two * normal_two, axis=0)
        shift_two = jnp.sum(grad_normed_two, axis=0)
        grad_middle_share = back_share + layer_back(
            grad_normed_two, normal_two, inverse_two, norm_table[2]
        )
        middle_low, output_rows = (
            lax.all_gather(grad_middle_share.astype(jnp.bfloat16), "mp", axis=0, tiled=True),
            lax.all_gather(output_share, "mp", axis=0, tiled=True),
        )
        results.append(output_rows.reshape(per_batch, SLOTS, model_width))
        grad_out = jnp.einsum("rm,rd->md", context, middle_low, preferred_element_type=jnp.float32)
        grad_context = (
            jnp.einsum("rd,md->rm", middle_low, full_outward, preferred_element_type=jnp.float32)
            .astype(jnp.bfloat16)
            .reshape(per_batch, SLOTS, local_heads, HEAD_DIM)
        )
        scores_again = attention_scores(queries, key_heads, allowed, score_scale)
        attention_full = jnp.exp(scores_again - log_total)
        attention_again = attention_full.astype(jnp.bfloat16)
        grad_values = jnp.einsum(
            "nhqk,nqhd->nkhd", attention_again, grad_context, preferred_element_type=jnp.float32
        ).astype(jnp.bfloat16)
        grad_weights = jnp.einsum(
            "nqhd,nkhd->nhqk", grad_context, value_heads, preferred_element_type=jnp.float32
        )
        grad_scores = (
            attention_full
            * (grad_weights - jnp.sum(grad_weights * attention_full, axis=-1, keepdims=True))
        ).astype(jnp.bfloat16)
        grad_queries = (
            jnp.einsum(
                "nhqk,nkhd->nqhd", grad_scores, key_heads, preferred_element_type=jnp.float32
            )
            * score_scale
        ).astype(jnp.bfloat16)
        grad_keys = (
            jnp.einsum("nhqk,nqhd->nkhd", grad_scores, queries, preferred_element_type=jnp.float32)
            * score_scale
        ).astype(jnp.bfloat16)
        grad_triple = jnp.stack([grad_queries, grad_keys, grad_values]).reshape(3, row_count, -1)
        grad_in = jnp.einsum(
            "rd,crm->cdm", normed_one, grad_triple, preferred_element_type=jnp.float32
        )
        first_terms = jnp.einsum(
            "crm,cdm->rd", grad_triple, full_inward, preferred_element_type=jnp.float32
        )
        grad_normed_one = lax.psum_scatter(first_terms, "mp", scatter_dimension=0, tiled=True)
        normal_share = lax.dynamic_slice_in_dim(normal_one, share_start, share_rows, 0)
        inverse_share = lax.dynamic_slice_in_dim(inverse_one, share_start, share_rows, 0)
        gain_one = jnp.sum(grad_normed_one * normal_share, axis=0)
        shift_one = jnp.sum(grad_normed_one, axis=0)
        tokens_grad_share = grad_middle_share + layer_back(
            grad_normed_one, normal_share, inverse_share, norm_table[0]
        )
        table_terms = jnp.stack([gain_one, shift_one, gain_two, shift_two])[None]
        grad_tokens, gathered_tables = (
            lax.all_gather(tokens_grad_share, "mp", axis=0, tiled=True),
            lax.all_gather(table_terms, "mp", axis=0, tiled=True),
        )
        grad_table = jnp.sum(gathered_tables, axis=0)
        input_grads.append(grad_tokens.reshape(per_batch, SLOTS, model_width))
        batch_grads = (grad_in, grad_out, grad_up, grad_down, grad_table)
        if local_sums is None:
            local_sums = batch_grads
        else:
            local_sums = tuple((former + latter for former, latter in zip(local_sums, batch_grads)))
    shards = (
        lax.psum_scatter(local_sums[0], "dp", scatter_dimension=1, tiled=True),
        lax.psum_scatter(local_sums[1], "dp", scatter_dimension=1, tiled=True),
        lax.psum_scatter(local_sums[2], "dp", scatter_dimension=0, tiled=True),
        lax.psum_scatter(local_sums[3], "dp", scatter_dimension=1, tiled=True),
        lax.psum_scatter(local_sums[4], "dp", scatter_dimension=1, tiled=True),
    )
    mp_count = lax.axis_size("mp")
    squares = (
        sum((jnp.sum(piece * piece) for piece in shards[:4]))
        + jnp.sum(shards[4] * shards[4]) / mp_count
    )
    grad_norm = jnp.sqrt(lax.psum(squares, ("dp", "mp")))
    clip_scale = jnp.minimum(1.0, CLIP_NORM / (grad_norm + 1e-06))
    shard_width = shards[4].shape[1]
    own_table = lax.dynamic_slice_in_dim(
        norm_table, lax.axis_index("dp") * shard_width, shard_width, 1
    )
    inward_new = adam_update(
        inward_weight,
        momentum_inward,
        variance_inward,
        shards[0],
        clip_scale,
        RATE_INWARD,
        WEIGHT_DECAY,
    )
    outward_new = adam_update(
        outward_weight,
        momentum_outward,
        variance_outward,
        shards[1],
        clip_scale,
        RATE_OUTWARD,
        WEIGHT_DECAY,
    )
    upward_new = adam_update(
        upward_weight,
        momentum_upward,
        variance_upward,
        shards[2],
        clip_scale,
        RATE_UPWARD,
        WEIGHT_DECAY,
    )
    downward_new = adam_update(
        downward_weight,
        momentum_downward,
        variance_downward,
        shards[3],
        clip_scale,
        RATE_DOWNWARD,
        WEIGHT_DECAY,
    )
    norms_new = adam_update(
        own_table, momentum_norms, variance_norms, shards[4], clip_scale, RATE_NORMS, 0.0
    )
    output = jnp.concatenate(results, axis=0)
    input_grad = jnp.concatenate(input_grads, axis=0)
    return (
        output,
        input_grad,
        grad_norm,
        inward_new[0],
        inward_new[1],
        inward_new[2],
        outward_new[0],
        outward_new[1],
        outward_new[2],
        upward_new[0],
        upward_new[1],
        upward_new[2],
        downward_new[0],
        downward_new[1],
        downward_new[2],
        norms_new[0],
        norms_new[1],
        norms_new[2],
    )


def whole_program(mesh, function):
    placed = (
        P("dp", None, None),
        P("dp", None, None),
        P("dp"),
        P("dp"),
        P(None, "dp", "mp"),
        P("mp", "dp"),
        P("dp", "mp"),
        P("mp", "dp"),
        P(),
        P(None, "dp", "mp"),
        P("mp", "dp"),
        P("dp", "mp"),
        P("mp", "dp"),
        P(None, "dp"),
        P(None, "dp", "mp"),
        P("mp", "dp"),
        P("dp", "mp"),
        P("mp", "dp"),
        P(None, "dp"),
    )
    return jax.shard_map(
        function,
        mesh=mesh,
        in_specs=placed,
        out_specs=(
            P("dp", None, None),
            P("dp", None, None),
            P(),
            P(None, "dp", "mp"),
            P(None, "dp", "mp"),
            P(None, "dp", "mp"),
            P("mp", "dp"),
            P("mp", "dp"),
            P("mp", "dp"),
            P("dp", "mp"),
            P("dp", "mp"),
            P("dp", "mp"),
            P("mp", "dp"),
            P("mp", "dp"),
            P("mp", "dp"),
            P(None, "dp"),
            P(None, "dp"),
            P(None, "dp"),
        ),
        check_vma=False,
    )


NN = (((1,), (0,)), ((), ()))
NT = (((1,), (1,)), ((), ()))
TN = (((0,), (0,)), ((), ()))
MESH = pl.DeviceIdType.MESH
F32 = jnp.float32
BF16 = jnp.bfloat16
ROWS = 672
HALF = ROWS // 2
KEYS = 768
NEAR_KEYS = 384
PERIOD = PRIMARY + WRIST + READOUT


def dot(left, right, dims=NN):
    return lax.dot_general(left, right, dims, preferred_element_type=F32)


def gelu_both(values):
    square = values * values
    inner = 0.7978845608028654 * values * (1.0 + 0.044715 * square)
    bend = jnp.tanh(inner)
    half_up = 0.5 + 0.5 * bend
    slope = half_up + 0.5 * values * (1.0 - bend * bend) * (
        0.7978845608028654 * (1.0 + 0.134145 * square)
    )
    return values * half_up, slope


def key_bits(live_steps, has_wrist):
    place = lax.broadcasted_iota(jnp.int32, (1, KEYS), 1)
    relative = place - TASK
    is_task = relative < 0
    later = relative >= PERIOD
    offset = jnp.where(later, relative - PERIOD, relative)
    is_read = offset >= PRIMARY + WRIST
    is_wrist = jnp.logical_and(offset >= PRIMARY, offset < PRIMARY + WRIST)
    step_of = jnp.where(later, 1, 0)
    alive = jnp.logical_and(
        step_of < live_steps, jnp.logical_or(jnp.logical_not(is_wrist), has_wrist == 1)
    )
    bits = jnp.where(is_read, jnp.where(later, 16, 8), jnp.where(later, 4, 2))
    bits = jnp.where(alive, bits, 0)
    bits = jnp.where(is_task, 1, bits)
    return jnp.where(place < SLOTS, bits, 0)


def query_bits(first):
    place = lax.broadcasted_iota(jnp.int32, (HALF, 1), 0) + first
    relative = place - TASK
    is_task = relative < 0
    later = relative >= PERIOD
    offset = jnp.where(later, relative - PERIOD, relative)
    is_read = offset >= PRIMARY + WRIST
    bits = jnp.where(later, 7, 3) + jnp.where(is_read, jnp.where(later, 16, 8), 0)
    return jnp.where(is_task, 1, bits)


N_REMOTE = 128
VMEM_BYTES = 64 * 1024 * 1024 - 65536


def fused_kernel(
    steps, flags, shard_h, tokens_h, back_h, norms,
    output_h, grad_h, shards_out, table_out,
    weights, tokens, back, normed_one, queries, keys, values, probs, heads, context,
    middle, normed_two, hidden, grad_upper, middle_low, out_half, grad_half,
    keep, keep_low, send_a, send_b,
    recv_one, recv_mid, recv_low, swapped_one, swapped_mid, swapped_low,
    grad_mid, grad_triple, total, x_send, x_recv, z_send, z_recv,
    table_mine, table_recv,
    send_sems, recv_sems, local_sems,
):
    dp = lax.axis_index("dp")
    mp = lax.axis_index("mp")
    z, x = dp // 2, dp % 2
    y, c = mp // 2, mp % 2
    core_peer = (dp, y * 2 + 1 - c)
    y_peer = (dp, (1 - y) * 2 + c)
    x_peer = (z * 2 + 1 - x, mp)
    z_peers = [(((z + k) % 4) * 2 + x, mp) for k in (1, 2, 3)]
    all_peers = [core_peer, y_peer, x_peer] + z_peers
    block = weights.shape[1] // 8
    used = []
    pending = []

    def describe(index, src, dst, peer):
        return pltpu.make_async_remote_copy(
            src_ref=src, dst_ref=dst, send_sem=send_sems.at[index], recv_sem=recv_sems.at[index],
            device_id=peer, device_id_type=MESH,
        )

    def send(src, dst, peer):
        used.append(0)
        copy = describe(len(used) - 1, src, dst, peer)
        copy.start()
        pending.append(copy)
        return copy

    def done_sending(*copies):
        for copy in copies:
            copy.wait_send()
            pending[:] = [other for other in pending if other is not copy]

    def block_rows(index):
        return pl.ds(pl.multiple_of(index * block, 32), block)

    def half_rows(half):
        return pl.ds(pl.multiple_of(half * HALF, 16), HALF)

    mine = half_rows(c)
    own_block = block_rows(dp)
    loads = [
        pltpu.make_async_copy(shard_h.at[i], weights.at[i, own_block], local_sems.at[i])
        for i in range(3)
    ]
    loads.append(pltpu.make_async_copy(tokens_h, tokens, local_sems.at[3]))
    loads.append(pltpu.make_async_copy(back_h, back, local_sems.at[4]))
    for load in loads:
        load.start()

    barrier = pltpu.get_barrier_semaphore()
    for peer in all_peers:
        pl.semaphore_signal(barrier, inc=1, device_id=peer, device_id_type=MESH)
    pl.semaphore_wait(barrier, len(all_peers))

    later = []
    z_index = {}
    for mat in range(3):
        for sign in (1, -1):
            for j in (1, 2, 3):
                z_index[mat, sign, j] = len(used)
                used.append(0)
                z_index[mat, sign, j, "x"] = len(used)
                used.append(0)
    own_x = {}

    def z_send_block(mat, sign, j):
        origin = z - sign * (j - 1)
        rows = weights.at[mat, block_rows(origin * 2 + x)]
        there = ((z + sign) * 2 + x, mp)
        copy = describe(z_index[mat, sign, j], rows, rows, there)
        wanted = jnp.logical_and(
            jnp.logical_and(origin >= 0, origin <= 3), z < 3 if sign == 1 else z > 0
        )

        @pl.when(wanted)
        def _():
            copy.start()

        later.append((wanted, copy))

    def weights_out(mat):
        loads[mat].wait()
        for sign in (1, -1):
            z_send_block(mat, sign, 1)
        rows = weights.at[mat, own_block]
        own_x[mat] = send(rows, rows, x_peer)

    def arrives(sign, j):
        return z >= j if sign == 1 else z <= 3 - j

    def block_at(mat, sign, j):
        return weights.at[mat, block_rows((z - sign * j) * 2 + x)]

    def weights_on(mat, j):
        for sign in (1, -1):
            here = arrives(sign, j)
            rows = block_at(mat, sign, j)
            onward = describe(z_index[mat, sign, j, "x"], rows, rows, x_peer)

            @pl.when(here)
            def _():
                describe(z_index[mat, sign, j], rows, rows, x_peer).wait_recv()

            if j < 3:
                z_send_block(mat, sign, j + 1)

            @pl.when(here)
            def _():
                onward.start()

            later.append((here, onward))

    def weights_in(mat):
        own_x[mat].wait_recv()
        for j in (1, 2, 3):
            for sign in (1, -1):
                rows = block_at(mat, sign, j)

                @pl.when(arrives(sign, j))
                def _():
                    describe(z_index[mat, sign, j, "x"], rows, rows, x_peer).wait_recv()

    def norm_stats(rows):
        centre = rows - jnp.mean(rows, axis=-1, keepdims=True)
        inverse = lax.rsqrt(jnp.mean(centre * centre, axis=-1, keepdims=True) + NORM_EPSILON)
        return centre * inverse, inverse

    def norm_back(grad_result, normal, inverse, gain_row):
        scaled = grad_result * gain_row
        return inverse * (
            scaled
            - jnp.mean(scaled, axis=-1, keepdims=True)
            - normal * jnp.mean(scaled * normal, axis=-1, keepdims=True)
        )

    def first_norm(item, low, high):
        @pl.loop(low, high)
        def _(index):
            rows = pl.ds(pl.multiple_of(index * 112, 16), 112)
            normal, _ = norm_stats(tokens[item, rows, :].astype(F32))
            normed_one[item, rows, :] = (normal * norms[0:1, :] + norms[1:2, :]).astype(BF16)

    weights_out(0)
    loads[3].wait()
    first_norm(0, 0, 4)
    weights_on(0, 1)
    first_norm(0, 4, 6)
    first_norm(1, 0, 2)
    weights_on(0, 2)
    first_norm(1, 2, 6)
    weights_on(0, 3)
    weights_out(1)
    loads[4].wait()
    zero_rows = jnp.zeros((KEYS - ROWS, HEAD_DIM), BF16)
    for i in range(6):
        keys[i, ROWS:KEYS, :] = zero_rows
        values[i, ROWS:KEYS, :] = zero_rows
    weights_in(0)

    def project(item):
        @pl.loop(0, 2)
        def _(half):
            rows = half_rows(half)
            joined = dot(normed_one[item, rows, :], weights[0, :, 0:576])
            for head in range(3):
                low = head * HEAD_DIM
                queries[item * 3 + head, rows, :] = (
                    joined[:, low : low + HEAD_DIM].astype(BF16) * HEAD_DIM ** (-0.5)
                ).astype(BF16)
                low += 192
                keys[item * 3 + head, rows, :] = joined[:, low : low + HEAD_DIM].astype(BF16)
                low += 192
                values[item * 3 + head, rows, :] = joined[:, low : low + HEAD_DIM].astype(BF16)

    def attend(item):
        bits = key_bits(steps[item], flags[item])

        @pl.loop(0, 3)
        def _(head):
            at = item * 3 + head
            for half, extent in ((0, NEAR_KEYS), (1, KEYS)):
                first = half * HALF
                scores = dot(queries[at, first : first + HALF, :], keys[at, 0:extent, :], NT)
                seen = jnp.bitwise_and(bits[:, 0:extent], query_bits(first)) != 0
                scores = jnp.where(seen, scores, NEGATIVE)
                spread = jnp.exp(scores - jnp.max(scores, axis=-1, keepdims=True))
                scale = 1.0 / jnp.sum(spread, axis=-1, keepdims=True)
                low = (spread * scale).astype(BF16)
                probs[at, first : first + HALF, 0:extent] = low
                heads[at, first : first + HALF, :] = dot(low, values[at, 0:extent, :]).astype(BF16)

    def to_core(kind, item, source):
        return send(source.at[item], kind.at[item], core_peer)

    def to_swap(copy, kept, received, staged, swapped, item):
        done_sending(copy)
        copy.wait_recv()
        staged[item] = (kept[item] + received[item].astype(F32)).astype(BF16)
        return send(staged.at[item], swapped.at[item], y_peer)

    def both(copy, staged, swapped, item):
        copy.wait_recv()
        return staged[item].astype(F32) + swapped[item].astype(F32)

    def attention_out(item):
        for half in (0, 1):
            rows = slice(half * HALF, (half + 1) * HALF)
            context[item, rows, :] = jnp.concatenate(
                [heads[item * 3 + head, rows, :] for head in range(3)], axis=1
            )
        outward = weights[0, :, 576:768]
        send_a[item] = dot(context[item, half_rows(1 - c), :], outward, NT).astype(BF16)
        copy = to_core(recv_one, item, send_a)
        keep[item] = dot(context[item, mine, :], outward, NT)
        return copy

    project(0)
    weights_on(1, 1)
    attend(0)
    weights_on(1, 2)
    attn_0 = attention_out(0)
    weights_on(1, 3)
    weights_out(2)
    project(1)
    swap_0 = to_swap(attn_0, keep, recv_one, send_a, swapped_one, 0)
    weights_on(2, 1)
    attend(1)
    weights_on(2, 2)
    attn_1 = attention_out(1)
    weights_on(2, 3)
    swap_1 = to_swap(attn_1, keep, recv_one, send_a, swapped_one, 1)

    def share_rows(buffer, item):
        rows = buffer.at[item, mine]
        return send(rows, rows, core_peer)

    def second_norm(copy, item):
        rows = tokens[item, mine, :].astype(F32) + both(copy, send_a, swapped_one, item)
        middle[item] = rows
        normal, _ = norm_stats(rows)
        normed_two[item, mine, :] = (normal * norms[2:3, :] + norms[3:4, :]).astype(BF16)
        return share_rows(normed_two, item)

    def feed_forward(item, half, keeps):
        rows = half_rows(half)
        upper = dot(normed_two[item, rows, :], weights[1])
        grown, slope = gelu_both(upper)
        grown = grown.astype(BF16)
        hidden[item, rows, :] = grown
        pull = (dot(back[item, rows, :], weights[2]) * slope).astype(BF16)
        grad_upper[item, rows, :] = pull
        terms = dot(pull, weights[1], NT)
        lowered = dot(grown, weights[2], NT)
        if keeps:
            keep[item] = terms
            keep_low[item] = lowered
            return None
        send_a[item] = terms.astype(BF16)
        first = to_core(recv_mid, item, send_a)
        send_b[item] = lowered.astype(BF16)
        return first, to_core(recv_low, item, send_b)

    two_0 = second_norm(swap_0, 0)
    done_sending(swap_0)
    weights_in(1)
    weights_in(2)
    feed_forward(0, c, True)
    two_0.wait_recv()
    mid_0, low_0 = feed_forward(0, 1 - c, False)
    two_1 = second_norm(swap_1, 1)
    done_sending(swap_1)
    swap_mid_0 = to_swap(mid_0, keep, recv_mid, send_a, swapped_mid, 0)
    feed_forward(1, c, True)
    two_1.wait_recv()
    mid_1, low_1 = feed_forward(1, 1 - c, False)

    def band_grad(slot, first, width, left_of, right_of):
        total[slot, :, first : first + width] = dot(left_of(0), right_of(0), TN) + dot(
            left_of(1), right_of(1), TN
        )

    x_copies = {}
    z_copies = {}

    def grads_out(mat, slot):
        for k in (2, 1, 3, 0):
            x_send[mat, k] = total[slot, block_rows(2 * ((z + k) % 4) + 1 - x), :].astype(BF16)
            x_copies[mat, k] = send(x_send.at[mat, k], x_recv.at[mat, k], x_peer)

    def grads_on(mat, slot):
        for k in (2, 1, 3):
            x_copies[mat, k].wait_recv()
            z_send[mat, k - 1] = (
                total[slot, block_rows(2 * ((z + k) % 4) + x), :] + x_recv[mat, k].astype(F32)
            ).astype(BF16)
            z_copies[mat, k] = send(z_send.at[mat, k - 1], z_recv.at[mat, k - 1], z_peers[k - 1])
        x_copies[mat, 0].wait_recv()
        shards_out[mat] = total[slot, own_block, :] + x_recv[mat, 0].astype(F32)

    def grads_in(mat):
        summed = shards_out[mat]
        for k in (1, 3, 2):
            z_copies[mat, k].wait_recv()
            summed += z_recv[mat, k - 1].astype(F32)
        shards_out[mat] = summed
        return jnp.sum(summed * summed)

    for first in (0, 256, 512):
        band_grad(
            0, first, 256,
            lambda i: back[i], lambda i, f=first: hidden[i, :, f : f + 256],
        )
        if first == 0:
            swap_mid_1 = to_swap(mid_1, keep, recv_mid, send_a, swapped_mid, 1)
    grads_out(2, 0)
    for first in (0, 256, 512):
        band_grad(
            1, first, 256,
            lambda i: normed_two[i], lambda i, f=first: grad_upper[i, :, f : f + 256],
        )
    grads_out(1, 1)

    def middle_back(copy, item):
        grad_two = both(copy, send_a, swapped_mid, item)
        normal, inverse = norm_stats(middle[item])
        sums = (
            jnp.sum(grad_two * normal, axis=0, keepdims=True),
            jnp.sum(grad_two, axis=0, keepdims=True),
        )
        for row, part in zip((2, 3), sums):
            table_mine[row : row + 1, :] = part if item == 0 else table_mine[row : row + 1, :] + part
        pulled = back[item, mine, :].astype(F32) + norm_back(
            grad_two, normal, inverse, norms[2:3, :]
        )
        grad_mid[item] = pulled
        middle_low[item, mine, :] = pulled.astype(BF16)
        return share_rows(middle_low, item)

    def attend_back(item):
        for half in (0, 1):
            rows = half_rows(half)
            pulled = dot(middle_low[item, rows, :], weights[0, :, 576:768]).astype(BF16)
            for head in range(3):
                heads[item * 3 + head, rows, :] = pulled[:, head * HEAD_DIM : (head + 1) * HEAD_DIM]

        @pl.loop(0, 3)
        def _(head):
            at = item * 3 + head
            grad_key = None
            grad_value = None
            key_rows = keys[at]
            value_rows = values[at]
            for half, extent in ((1, KEYS), (0, NEAR_KEYS)):
                first = half * HALF
                rows = slice(first, first + HALF)
                pulled = heads[at, rows, :]
                weight = dot(pulled, value_rows[0:extent], NT)
                low = probs[at, rows, 0:extent]
                wide = low.astype(F32)
                weight = wide * weight
                moved = (weight - wide * jnp.sum(weight, axis=-1, keepdims=True)).astype(BF16)
                asked = queries[at, rows, :]
                part_key = dot(moved, asked, TN)
                part_value = dot(low, pulled, TN)
                queries[at, rows, :] = (
                    dot(moved, key_rows[0:extent]) * HEAD_DIM ** (-0.5)
                ).astype(BF16)
                if grad_key is None:
                    grad_key, grad_value = part_key, part_value
                else:
                    keys[at, 0:extent, :] = (grad_key[0:extent] + part_key).astype(BF16)
                    values[at, 0:extent, :] = (grad_value[0:extent] + part_value).astype(BF16)
                    keys[at, extent:KEYS, :] = grad_key[extent:KEYS].astype(BF16)
                    values[at, extent:KEYS, :] = grad_value[extent:KEYS].astype(BF16)

        for half in (0, 1):
            rows = slice(half * HALF, (half + 1) * HALF)
            grad_triple[item, rows, :] = jnp.concatenate(
                [
                    source[item * 3 + head, rows, :]
                    for source in (queries, keys, values)
                    for head in range(3)
                ],
                axis=1,
            )

    def first_terms(item):
        inward = weights[0, :, 0:576]
        send_a[item] = dot(grad_triple[item, half_rows(1 - c), :], inward, NT).astype(BF16)
        copy = to_core(recv_one, item, send_a)
        keep[item] = dot(grad_triple[item, mine, :], inward, NT)
        return copy

    low_swap_0 = low_swap_1 = None
    ml_0 = middle_back(swap_mid_0, 0)
    done_sending(swap_mid_0)
    ml_0.wait_recv()
    attend_back(0)
    first_0 = first_terms(0)
    ml_1 = middle_back(swap_mid_1, 1)
    done_sending(swap_mid_1)
    first_swap_0 = to_swap(first_0, keep, recv_one, send_a, swapped_one, 0)
    grads_on(2, 0)
    ml_1.wait_recv()
    attend_back(1)
    first_1 = first_terms(1)
    for first, width in ((0, 256), (256, 256), (512, 64)):
        band_grad(
            0, first, width,
            lambda i: normed_one[i], lambda i, f=first, w=width: grad_triple[i, :, f : f + w],
        )
        if first == 0:
            first_swap_1 = to_swap(first_1, keep, recv_one, send_a, swapped_one, 1)
            low_swap_0 = to_swap(low_0, keep_low, recv_low, send_b, swapped_low, 0)
            low_swap_1 = to_swap(low_1, keep_low, recv_low, send_b, swapped_low, 1)
    band_grad(0, 576, 192, lambda i: middle_low[i], lambda i: context[i])
    grads_out(0, 0)
    grads_on(1, 1)

    stores = []

    def give(half_buffer, result, item):
        here = result.at[item, mine]
        store = pltpu.make_async_copy(half_buffer.at[item], here, local_sems.at[5 + len(stores)])
        store.start()
        stores.append(store)
        return send(half_buffer.at[item], here, core_peer)

    def first_back(copy, item):
        grad_one = both(copy, send_a, swapped_one, item)
        normal, inverse = norm_stats(tokens[item, mine, :].astype(F32))
        sums = (
            jnp.sum(grad_one * normal, axis=0, keepdims=True),
            jnp.sum(grad_one, axis=0, keepdims=True),
        )
        for row, part in zip((0, 1), sums):
            table_mine[row : row + 1, :] = part if item == 0 else table_mine[row : row + 1, :] + part
        grad_half[item] = (
            grad_mid[item] + norm_back(grad_one, normal, inverse, norms[0:1, :])
        ).astype(BF16)
        return give(grad_half, grad_h, item)

    rows_0 = first_back(first_swap_0, 0)
    squares = grads_in(2)
    grads_on(0, 0)
    rows_1 = first_back(first_swap_1, 1)
    squares += grads_in(1)
    squares += grads_in(0)
    table_mine[4:8, :] = jnp.broadcast_to(squares, (4, table_mine.shape[1]))

    for hop_number, peer in enumerate((core_peer, y_peer, x_peer)):
        hop = send(table_mine, table_recv.at[hop_number], peer)
        hop.wait_recv()
        done_sending(hop)
        received = table_recv[hop_number]
        if hop_number == 1:
            table_mine[4:8, :] = table_mine[4:8, :] + received[4:8]
        else:
            table_mine[...] = table_mine[...] + received
    hops = [send(table_mine, table_recv.at[2 + k], z_peers[k - 1]) for k in (1, 2, 3)]
    for hop in hops:
        hop.wait_recv()
    parts = [table_mine[...], table_recv[3], table_recv[4], table_recv[5]]
    ordered = None
    for level in range(4):
        piece = parts[0]
        for k in (1, 2, 3):
            piece = jnp.where((level + k) % 4 == z, parts[k], piece)
        ordered = piece if ordered is None else ordered + piece
    table_out[...] = ordered

    given = [rows_0, rows_1]
    for item, copy in ((0, low_swap_0), (1, low_swap_1)):
        out_half[item] = (middle[item] + both(copy, send_b, swapped_low, item)).astype(BF16)
        given.append(give(out_half, output_h, item))
    for copy in given:
        copy.wait_recv()
    for store in stores:
        store.wait()
    for copy in list(pending):
        copy.wait_send()
    for wanted, copy in later:

        @pl.when(wanted)
        def _():
            copy.wait_send()


def fused_body(
    tokens, cotangent, step_counts, wrist_flags,
    inward_weight, outward_weight, upward_weight, downward_weight, norm_table,
    momentum_inward, momentum_outward, momentum_upward, momentum_downward, momentum_norms,
    variance_inward, variance_outward, variance_upward, variance_downward, variance_norms,
):
    width = norm_table.shape[1]
    block = upward_weight.shape[0]
    shard = jnp.stack(
        [
            jnp.concatenate(
                [inward_weight[0], inward_weight[1], inward_weight[2], outward_weight.T], axis=1
            ),
            upward_weight,
            downward_weight.T,
        ]
    ).astype(BF16)
    padding = ((0, 0), (0, ROWS - SLOTS), (0, 0))
    any_spec = pl.BlockSpec(memory_space=pl.ANY)
    vmem = pl.BlockSpec(memory_space=pltpu.VMEM)
    smem = pl.BlockSpec(memory_space=pltpu.SMEM)
    rows = pltpu.VMEM((2, ROWS, width), BF16)
    halves = pltpu.VMEM((2, HALF, width), BF16)
    keep = pltpu.VMEM((2, HALF, width), F32)
    output, grads, shards, table = pl.pallas_call(
        fused_kernel,
        out_shape=(
            jax.ShapeDtypeStruct((2, ROWS, width), BF16),
            jax.ShapeDtypeStruct((2, ROWS, width), BF16),
            jax.ShapeDtypeStruct((3, block, width), F32),
            jax.ShapeDtypeStruct((8, width), F32),
        ),
        in_specs=[smem, smem, any_spec, any_spec, any_spec, vmem],
        out_specs=(any_spec, any_spec, vmem, vmem),
        scratch_shapes=[
            pltpu.VMEM((3, width, width), BF16),
            rows,
            rows,
            rows,
            pltpu.VMEM((6, ROWS, HEAD_DIM), BF16),
            pltpu.VMEM((6, KEYS, HEAD_DIM), BF16),
            pltpu.VMEM((6, KEYS, HEAD_DIM), BF16),
            pltpu.VMEM((6, ROWS, KEYS), BF16),
            pltpu.VMEM((6, ROWS, HEAD_DIM), BF16),
            pltpu.VMEM((2, ROWS, 192), BF16),
            keep,
            rows,
            rows,
            rows,
            rows,
            halves,
            halves,
            keep,
            keep,
            halves,
            halves,
            halves,
            halves,
            halves,
            halves,
            halves,
            halves,
            keep,
            pltpu.VMEM((2, ROWS, 576), BF16),
            pltpu.VMEM((2, width, width), F32),
            pltpu.VMEM((3, 4, block, width), BF16),
            pltpu.VMEM((3, 4, block, width), BF16),
            pltpu.VMEM((3, 3, block, width), BF16),
            pltpu.VMEM((3, 3, block, width), BF16),
            pltpu.VMEM((8, width), F32),
            pltpu.VMEM((6, 8, width), F32),
            pltpu.SemaphoreType.DMA((N_REMOTE,)),
            pltpu.SemaphoreType.DMA((N_REMOTE,)),
            pltpu.SemaphoreType.DMA((9,)),
        ],
        compiler_params=pltpu.CompilerParams(
            collective_id=0, has_side_effects=True, vmem_limit_bytes=VMEM_BYTES
        ),
        name="block_step",
    )(
        step_counts,
        wrist_flags,
        shard,
        jnp.pad(tokens, padding),
        jnp.pad(cotangent, padding),
        norm_table,
    )
    part = inward_weight.shape[2]
    grad_inward = jnp.stack([shards[0, :, i * part : (i + 1) * part] for i in range(3)])
    grad_outward = shards[0, :, 3 * part :].T
    table_sums = table[:4]
    grad_norm = jnp.sqrt(table[4, 0] + jnp.sum(table_sums * table_sums))
    clip_scale = jnp.minimum(1.0, CLIP_NORM / (grad_norm + 1e-06))
    shard_width = momentum_norms.shape[1]
    start = lax.axis_index("dp") * shard_width
    own_table = lax.dynamic_slice_in_dim(norm_table, start, shard_width, 1)
    own_sums = lax.dynamic_slice_in_dim(table_sums, start, shard_width, 1)
    updated = []
    for master, momentum, variance, gradient, rate, decay in (
        (inward_weight, momentum_inward, variance_inward, grad_inward, RATE_INWARD, WEIGHT_DECAY),
        (outward_weight, momentum_outward, variance_outward, grad_outward, RATE_OUTWARD, WEIGHT_DECAY),
        (upward_weight, momentum_upward, variance_upward, shards[1], RATE_UPWARD, WEIGHT_DECAY),
        (downward_weight, momentum_downward, variance_downward, shards[2].T, RATE_DOWNWARD, WEIGHT_DECAY),
        (own_table, momentum_norms, variance_norms, own_sums, RATE_NORMS, 0.0),
    ):
        updated.extend(adam_update(master, momentum, variance, gradient, clip_scale, rate, decay))
    return (
        output[:, :SLOTS],
        grads[:, :SLOTS].astype(F32),
        grad_norm,
        *updated,
    )


def solution(mesh):
    fits = mesh.shape["dp"] == 8 and mesh.shape["mp"] == 4
    return whole_program(mesh, fused_body if fits else body)
```

```python
import jax
import jax.numpy as jnp
from jax import lax
from jax.experimental import pallas as pl
from jax.experimental.pallas import tpu as pltpu
from jax.sharding import PartitionSpec as P

HEAD_DIM = 64
TASK = 16
PRIMARY = 256
WRIST = 64
READOUT = 4
SLOTS = 664
MB = 2
STEP = 10


NORM_EPSILON = 1e-06
CLIP_NORM = 1.0
BETA_ONE = 0.9
BETA_TWO = 0.999
ADAM_EPSILON = 1e-08
WEIGHT_DECAY = 0.1
NEGATIVE = -1e30
RATE_INWARD = 0.05
RATE_OUTWARD = 0.15
RATE_UPWARD = 0.04
RATE_DOWNWARD = 0.02
RATE_NORMS = 0.5


def slot_mask(live_steps, has_wrist):
    position = jnp.arange(SLOTS, dtype=jnp.int32)
    relative = position - TASK
    period = PRIMARY + WRIST + READOUT
    is_task = relative < 0
    forward_pos = jnp.maximum(relative, 0)
    stepno = forward_pos // period
    offset = forward_pos % period
    not_task = jnp.logical_not(is_task)
    is_read = jnp.logical_and(not_task, offset >= PRIMARY + WRIST)
    is_obs = jnp.logical_and(not_task, jnp.logical_not(is_read))
    is_wrist = jnp.logical_and(is_obs, offset >= PRIMARY)
    present = jnp.logical_or(
        is_task,
        jnp.logical_and(
            stepno < live_steps, jnp.logical_or(jnp.logical_not(is_wrist), has_wrist == 1)
        ),
    )
    see_obs = is_obs[None, :] & not_task[:, None] & (stepno[None, :] <= stepno[:, None])
    see_read = is_read[None, :] & is_read[:, None] & (stepno[None, :] == stepno[:, None])
    return present[None, :] & (is_task[None, :] | see_obs | see_read)


def layer_stats(values):
    centre = values - jnp.mean(values, axis=-1, keepdims=True)
    inverse = lax.rsqrt(jnp.mean(centre * centre, axis=-1, keepdims=True) + NORM_EPSILON)
    return (centre * inverse, inverse)


def layer_back(grad_result, normal, inverse, gain_row):
    scaled = grad_result * gain_row
    return inverse * (
        scaled
        - jnp.mean(scaled, axis=-1, keepdims=True)
        - normal * jnp.mean(scaled * normal, axis=-1, keepdims=True)
    )


def gelu_tanh(values):
    return (
        0.5
        * values
        * (1.0 + jnp.tanh(0.7978845608028654 * (values + 0.044715 * values * values * values)))
    )


def attention_scores(queries, key_heads, allowed, score_scale):
    dotted = (
        jnp.einsum("nqhd,nkhd->nhqk", queries, key_heads, preferred_element_type=jnp.float32)
        * score_scale
    )
    return jnp.where(allowed, dotted, NEGATIVE)


def adam_update(master, momentum, variance, gradient, clip_scale, step_rate, decay_rate):
    clipped = gradient * clip_scale
    moment_one = BETA_ONE * momentum + (1.0 - BETA_ONE) * clipped
    moment_two = BETA_TWO * variance + (1.0 - BETA_TWO) * clipped * clipped
    first_hat = moment_one / (1.0 - BETA_ONE**STEP)
    second_hat = moment_two / (1.0 - BETA_TWO**STEP)
    updated = master - step_rate * (
        first_hat / (jnp.sqrt(second_hat) + ADAM_EPSILON) + decay_rate * master
    )
    return (moment_one, moment_two, updated)


def body(
    tokens,
    cotangent,
    step_counts,
    wrist_flags,
    inward_weight,
    outward_weight,
    upward_weight,
    downward_weight,
    norm_table,
    momentum_inward,
    momentum_outward,
    momentum_upward,
    momentum_downward,
    momentum_norms,
    variance_inward,
    variance_outward,
    variance_upward,
    variance_downward,
    variance_norms,
):
    full_inward, full_outward, full_upward, full_downward = (
        lax.all_gather(inward_weight.astype(jnp.bfloat16), "dp", axis=1, tiled=True),
        lax.all_gather(outward_weight.astype(jnp.bfloat16), "dp", axis=1, tiled=True),
        lax.all_gather(upward_weight.astype(jnp.bfloat16), "dp", axis=0, tiled=True),
        lax.all_gather(downward_weight.astype(jnp.bfloat16), "dp", axis=1, tiled=True),
    )
    model_width = norm_table.shape[1]
    local_heads = full_inward.shape[2] // HEAD_DIM
    score_scale = HEAD_DIM ** (-0.5)
    per_batch = tokens.shape[0] // MB
    row_count = per_batch * SLOTS
    share_rows = row_count // lax.axis_size("mp")
    share_start = lax.axis_index("mp") * share_rows
    results = []
    input_grads = []
    local_sums = None
    for batch_index in range(MB):
        start_item = batch_index * per_batch
        block_tokens = (
            tokens[start_item : start_item + per_batch]
            .astype(jnp.float32)
            .reshape(row_count, model_width)
        )
        block_back = (
            cotangent[start_item : start_item + per_batch]
            .astype(jnp.float32)
            .reshape(row_count, model_width)
        )
        allowed = jax.vmap(slot_mask)(
            step_counts[start_item : start_item + per_batch],
            wrist_flags[start_item : start_item + per_batch],
        )[:, None]
        normal_one, inverse_one = layer_stats(block_tokens)
        normed_one = (normal_one * norm_table[0] + norm_table[1]).astype(jnp.bfloat16)
        projected = jnp.einsum(
            "rd,cdm->crm", normed_one, full_inward, preferred_element_type=jnp.float32
        ).astype(jnp.bfloat16)
        triple = projected.reshape(3, per_batch, SLOTS, local_heads, HEAD_DIM)
        queries = triple[0]
        key_heads = triple[1]
        value_heads = triple[2]
        scores = attention_scores(queries, key_heads, allowed, score_scale)
        highest = jnp.max(scores, axis=-1, keepdims=True)
        log_total = highest + jnp.log(jnp.sum(jnp.exp(scores - highest), axis=-1, keepdims=True))
        attention_low = jnp.exp(scores - log_total).astype(jnp.bfloat16)
        context = (
            jnp.einsum(
                "nhqk,nkhd->nqhd", attention_low, value_heads, preferred_element_type=jnp.float32
            )
            .astype(jnp.bfloat16)
            .reshape(row_count, -1)
        )
        attn_terms = jnp.dot(context, full_outward, preferred_element_type=jnp.float32)
        tokens_share = lax.dynamic_slice_in_dim(block_tokens, share_start, share_rows, 0)
        back_share = lax.dynamic_slice_in_dim(block_back, share_start, share_rows, 0)
        middle_share = tokens_share + lax.psum_scatter(
            attn_terms, "mp", scatter_dimension=0, tiled=True
        )
        normal_two, inverse_two = layer_stats(middle_share)
        normed_share = (normal_two * norm_table[2] + norm_table[3]).astype(jnp.bfloat16)
        normed_two = lax.all_gather(normed_share, "mp", axis=0, tiled=True)
        upper_pre = jnp.dot(normed_two, full_upward, preferred_element_type=jnp.float32)
        hidden = gelu_tanh(upper_pre).astype(jnp.bfloat16)
        lowered_share = lax.psum_scatter(
            jnp.dot(hidden, full_downward, preferred_element_type=jnp.float32).astype(jnp.bfloat16),
            "mp",
            scatter_dimension=0,
            tiled=True,
        ).astype(jnp.float32)
        output_share = (middle_share + lowered_share).astype(jnp.bfloat16)
        back_rows = block_back.astype(jnp.bfloat16)
        grad_down = jnp.einsum("rf,rd->fd", hidden, back_rows, preferred_element_type=jnp.float32)
        grad_hidden = jnp.einsum(
            "rd,fd->rf", back_rows, full_downward, preferred_element_type=jnp.float32
        )
        upper_pull = jax.vjp(gelu_tanh, upper_pre)[1]
        grad_upper = upper_pull(grad_hidden)[0].astype(jnp.bfloat16)
        grad_up = jnp.einsum(
            "rd,rf->df", normed_two, grad_upper, preferred_element_type=jnp.float32
        )
        normed_terms = jnp.einsum(
            "rf,df->rd", grad_upper, full_upward, preferred_element_type=jnp.float32
        )
        grad_normed_two = lax.psum_scatter(normed_terms, "mp", scatter_dimension=0, tiled=True)
        gain_two = jnp.sum(grad_normed_two * normal_two, axis=0)
        shift_two = jnp.sum(grad_normed_two, axis=0)
        grad_middle_share = back_share + layer_back(
            grad_normed_two, normal_two, inverse_two, norm_table[2]
        )
        middle_low, output_rows = (
            lax.all_gather(grad_middle_share.astype(jnp.bfloat16), "mp", axis=0, tiled=True),
            lax.all_gather(output_share, "mp", axis=0, tiled=True),
        )
        results.append(output_rows.reshape(per_batch, SLOTS, model_width))
        grad_out = jnp.einsum("rm,rd->md", context, middle_low, preferred_element_type=jnp.float32)
        grad_context = (
            jnp.einsum("rd,md->rm", middle_low, full_outward, preferred_element_type=jnp.float32)
            .astype(jnp.bfloat16)
            .reshape(per_batch, SLOTS, local_heads, HEAD_DIM)
        )
        scores_again = attention_scores(queries, key_heads, allowed, score_scale)
        attention_full = jnp.exp(scores_again - log_total)
        attention_again = attention_full.astype(jnp.bfloat16)
        grad_values = jnp.einsum(
            "nhqk,nqhd->nkhd", attention_again, grad_context, preferred_element_type=jnp.float32
        ).astype(jnp.bfloat16)
        grad_weights = jnp.einsum(
            "nqhd,nkhd->nhqk", grad_context, value_heads, preferred_element_type=jnp.float32
        )
        grad_scores = (
            attention_full
            * (grad_weights - jnp.sum(grad_weights * attention_full, axis=-1, keepdims=True))
        ).astype(jnp.bfloat16)
        grad_queries = (
            jnp.einsum(
                "nhqk,nkhd->nqhd", grad_scores, key_heads, preferred_element_type=jnp.float32
            )
            * score_scale
        ).astype(jnp.bfloat16)
        grad_keys = (
            jnp.einsum("nhqk,nqhd->nkhd", grad_scores, queries, preferred_element_type=jnp.float32)
            * score_scale
        ).astype(jnp.bfloat16)
        grad_triple = jnp.stack([grad_queries, grad_keys, grad_values]).reshape(3, row_count, -1)
        grad_in = jnp.einsum(
            "rd,crm->cdm", normed_one, grad_triple, preferred_element_type=jnp.float32
        )
        first_terms = jnp.einsum(
            "crm,cdm->rd", grad_triple, full_inward, preferred_element_type=jnp.float32
        )
        grad_normed_one = lax.psum_scatter(first_terms, "mp", scatter_dimension=0, tiled=True)
        normal_share = lax.dynamic_slice_in_dim(normal_one, share_start, share_rows, 0)
        inverse_share = lax.dynamic_slice_in_dim(inverse_one, share_start, share_rows, 0)
        gain_one = jnp.sum(grad_normed_one * normal_share, axis=0)
        shift_one = jnp.sum(grad_normed_one, axis=0)
        tokens_grad_share = grad_middle_share + layer_back(
            grad_normed_one, normal_share, inverse_share, norm_table[0]
        )
        table_terms = jnp.stack([gain_one, shift_one, gain_two, shift_two])[None]
        grad_tokens, gathered_tables = (
            lax.all_gather(tokens_grad_share, "mp", axis=0, tiled=True),
            lax.all_gather(table_terms, "mp", axis=0, tiled=True),
        )
        grad_table = jnp.sum(gathered_tables, axis=0)
        input_grads.append(grad_tokens.reshape(per_batch, SLOTS, model_width))
        batch_grads = (grad_in, grad_out, grad_up, grad_down, grad_table)
        if local_sums is None:
            local_sums = batch_grads
        else:
            local_sums = tuple((former + latter for former, latter in zip(local_sums, batch_grads)))
    shards = (
        lax.psum_scatter(local_sums[0], "dp", scatter_dimension=1, tiled=True),
        lax.psum_scatter(local_sums[1], "dp", scatter_dimension=1, tiled=True),
        lax.psum_scatter(local_sums[2], "dp", scatter_dimension=0, tiled=True),
        lax.psum_scatter(local_sums[3], "dp", scatter_dimension=1, tiled=True),
        lax.psum_scatter(local_sums[4], "dp", scatter_dimension=1, tiled=True),
    )
    mp_count = lax.axis_size("mp")
    squares = (
        sum((jnp.sum(piece * piece) for piece in shards[:4]))
        + jnp.sum(shards[4] * shards[4]) / mp_count
    )
    grad_norm = jnp.sqrt(lax.psum(squares, ("dp", "mp")))
    clip_scale = jnp.minimum(1.0, CLIP_NORM / (grad_norm + 1e-06))
    shard_width = shards[4].shape[1]
    own_table = lax.dynamic_slice_in_dim(
        norm_table, lax.axis_index("dp") * shard_width, shard_width, 1
    )
    inward_new = adam_update(
        inward_weight,
        momentum_inward,
        variance_inward,
        shards[0],
        clip_scale,
        RATE_INWARD,
        WEIGHT_DECAY,
    )
    outward_new = adam_update(
        outward_weight,
        momentum_outward,
        variance_outward,
        shards[1],
        clip_scale,
        RATE_OUTWARD,
        WEIGHT_DECAY,
    )
    upward_new = adam_update(
        upward_weight,
        momentum_upward,
        variance_upward,
        shards[2],
        clip_scale,
        RATE_UPWARD,
        WEIGHT_DECAY,
    )
    downward_new = adam_update(
        downward_weight,
        momentum_downward,
        variance_downward,
        shards[3],
        clip_scale,
        RATE_DOWNWARD,
        WEIGHT_DECAY,
    )
    norms_new = adam_update(
        own_table, momentum_norms, variance_norms, shards[4], clip_scale, RATE_NORMS, 0.0
    )
    output = jnp.concatenate(results, axis=0)
    input_grad = jnp.concatenate(input_grads, axis=0)
    return (
        output,
        input_grad,
        grad_norm,
        inward_new[0],
        inward_new[1],
        inward_new[2],
        outward_new[0],
        outward_new[1],
        outward_new[2],
        upward_new[0],
        upward_new[1],
        upward_new[2],
        downward_new[0],
        downward_new[1],
        downward_new[2],
        norms_new[0],
        norms_new[1],
        norms_new[2],
    )


def whole_program(mesh, function):
    placed = (
        P("dp", None, None),
        P("dp", None, None),
        P("dp"),
        P("dp"),
        P(None, "dp", "mp"),
        P("mp", "dp"),
        P("dp", "mp"),
        P("mp", "dp"),
        P(),
        P(None, "dp", "mp"),
        P("mp", "dp"),
        P("dp", "mp"),
        P("mp", "dp"),
        P(None, "dp"),
        P(None, "dp", "mp"),
        P("mp", "dp"),
        P("dp", "mp"),
        P("mp", "dp"),
        P(None, "dp"),
    )
    return jax.shard_map(
        function,
        mesh=mesh,
        in_specs=placed,
        out_specs=(
            P("dp", None, None),
            P("dp", None, None),
            P(),
            P(None, "dp", "mp"),
            P(None, "dp", "mp"),
            P(None, "dp", "mp"),
            P("mp", "dp"),
            P("mp", "dp"),
            P("mp", "dp"),
            P("dp", "mp"),
            P("dp", "mp"),
            P("dp", "mp"),
            P("mp", "dp"),
            P("mp", "dp"),
            P("mp", "dp"),
            P(None, "dp"),
            P(None, "dp"),
            P(None, "dp"),
        ),
        check_vma=False,
    )


NN = (((1,), (0,)), ((), ()))
NT = (((1,), (1,)), ((), ()))
TN = (((0,), (0,)), ((), ()))
MESH = pl.DeviceIdType.MESH
F32 = jnp.float32
BF16 = jnp.bfloat16
ROWS = 672
HALF = ROWS // 2
KEYS = 768
NEAR_KEYS = 384
PERIOD = PRIMARY + WRIST + READOUT


def dot(left, right, dims=NN):
    return lax.dot_general(left, right, dims, preferred_element_type=F32)


def gelu_both(values):
    square = values * values
    inner = 0.7978845608028654 * values * (1.0 + 0.044715 * square)
    bend = jnp.tanh(inner)
    half_up = 0.5 + 0.5 * bend
    slope = half_up + 0.5 * values * (1.0 - bend * bend) * (
        0.7978845608028654 * (1.0 + 0.134145 * square)
    )
    return values * half_up, slope


def key_bits(live_steps, has_wrist):
    place = lax.broadcasted_iota(jnp.int32, (1, KEYS), 1)
    relative = place - TASK
    is_task = relative < 0
    later = relative >= PERIOD
    offset = jnp.where(later, relative - PERIOD, relative)
    is_read = offset >= PRIMARY + WRIST
    is_wrist = jnp.logical_and(offset >= PRIMARY, offset < PRIMARY + WRIST)
    step_of = jnp.where(later, 1, 0)
    alive = jnp.logical_and(
        step_of < live_steps, jnp.logical_or(jnp.logical_not(is_wrist), has_wrist == 1)
    )
    bits = jnp.where(is_read, jnp.where(later, 16, 8), jnp.where(later, 4, 2))
    bits = jnp.where(alive, bits, 0)
    bits = jnp.where(is_task, 1, bits)
    return jnp.where(place < SLOTS, bits, 0)


def query_bits(first):
    place = lax.broadcasted_iota(jnp.int32, (HALF, 1), 0) + first
    relative = place - TASK
    is_task = relative < 0
    later = relative >= PERIOD
    offset = jnp.where(later, relative - PERIOD, relative)
    is_read = offset >= PRIMARY + WRIST
    bits = jnp.where(later, 7, 3) + jnp.where(is_read, jnp.where(later, 16, 8), 0)
    return jnp.where(is_task, 1, bits)


N_REMOTE = 128
VMEM_BYTES = 64 * 1024 * 1024 - 65536


def fused_kernel(
    steps, flags, inward_h, outward_h, upward_h, downward_h, tokens_h, back_h, norms,
    output_h, grad_h, shards_out, table_out,
    weights, tokens, back, normed_one, queries, keys, values, probs, heads, context,
    middle, normed_two, hidden, grad_upper, middle_low, out_half, grad_half,
    keep, keep_low, send_a, send_b,
    recv_one, recv_mid, recv_low, swapped_one, swapped_mid, swapped_low,
    grad_mid, grad_triple, total, x_send, x_recv, z_recv,
    table_mine, table_recv, inward_f, outward_f, upward_f, downward_f,
    send_sems, recv_sems, local_sems,
):
    dp = lax.axis_index("dp")
    mp = lax.axis_index("mp")
    z, x = dp // 2, dp % 2
    y, c = mp // 2, mp % 2
    core_peer = (dp, y * 2 + 1 - c)
    y_peer = (dp, (1 - y) * 2 + c)
    x_peer = (z * 2 + 1 - x, mp)
    z_peers = [(((z + k) % 4) * 2 + x, mp) for k in (1, 2, 3)]
    all_peers = [core_peer, y_peer, x_peer] + z_peers
    block = weights.shape[1] // 8
    used = []
    pending = []

    def describe(index, src, dst, peer):
        return pltpu.make_async_remote_copy(
            src_ref=src, dst_ref=dst, send_sem=send_sems.at[index], recv_sem=recv_sems.at[index],
            device_id=peer, device_id_type=MESH,
        )

    def send(src, dst, peer):
        used.append(0)
        copy = describe(len(used) - 1, src, dst, peer)
        copy.start()
        pending.append(copy)
        return copy

    def done_sending(*copies):
        for copy in copies:
            copy.wait_send()
            pending[:] = [other for other in pending if other is not copy]

    def block_rows(index):
        return pl.ds(pl.multiple_of(index * block, 32), block)

    def half_rows(half):
        return pl.ds(pl.multiple_of(half * HALF, 16), HALF)

    mine = half_rows(c)
    own_block = block_rows(dp)
    loads = [
        pltpu.make_async_copy(source, target, local_sems.at[4 + i])
        for i, (source, target) in enumerate(
            (
                (inward_h, inward_f),
                (outward_h, outward_f),
                (upward_h, upward_f),
                (downward_h, downward_f),
                (tokens_h, tokens),
                (back_h, back),
            )
        )
    ]
    for load in loads:
        load.start()

    barrier = pltpu.get_barrier_semaphore()
    for peer in all_peers:
        pl.semaphore_signal(barrier, inc=1, device_id=peer, device_id_type=MESH)
    loads[0].wait()
    loads[1].wait()
    weights[0, own_block, :] = jnp.concatenate(
        [inward_f[0], inward_f[1], inward_f[2], outward_f[...].T], axis=1
    ).astype(BF16)
    pl.semaphore_wait(barrier, len(all_peers))

    later = []
    z_index = {}
    for mat in range(3):
        for sign in (1, -1):
            for j in (1, 2, 3):
                z_index[mat, sign, j] = len(used)
                used.append(0)
                z_index[mat, sign, j, "x"] = len(used)
                used.append(0)
    own_x = {}

    def z_send_block(mat, sign, j):
        origin = z - sign * (j - 1)
        rows = weights.at[mat, block_rows(origin * 2 + x)]
        there = ((z + sign) * 2 + x, mp)
        copy = describe(z_index[mat, sign, j], rows, rows, there)
        wanted = jnp.logical_and(
            jnp.logical_and(origin >= 0, origin <= 3), z < 3 if sign == 1 else z > 0
        )

        @pl.when(wanted)
        def _():
            copy.start()

        later.append((wanted, copy))

    def weights_out(mat):
        for sign in (1, -1):
            z_send_block(mat, sign, 1)
        rows = weights.at[mat, own_block]
        own_x[mat] = send(rows, rows, x_peer)

    def arrives(sign, j):
        return z >= j if sign == 1 else z <= 3 - j

    def block_at(mat, sign, j):
        return weights.at[mat, block_rows((z - sign * j) * 2 + x)]

    def weights_on(mat, j):
        for sign in (1, -1):
            here = arrives(sign, j)
            rows = block_at(mat, sign, j)
            onward = describe(z_index[mat, sign, j, "x"], rows, rows, x_peer)

            @pl.when(here)
            def _():
                describe(z_index[mat, sign, j], rows, rows, x_peer).wait_recv()

            if j < 3:
                z_send_block(mat, sign, j + 1)

            @pl.when(here)
            def _():
                onward.start()

            later.append((here, onward))

    def weights_in(mat):
        own_x[mat].wait_recv()
        for j in (1, 2, 3):
            for sign in (1, -1):
                rows = block_at(mat, sign, j)

                @pl.when(arrives(sign, j))
                def _():
                    describe(z_index[mat, sign, j, "x"], rows, rows, x_peer).wait_recv()

    def norm_stats(rows):
        centre = rows - jnp.mean(rows, axis=-1, keepdims=True)
        inverse = lax.rsqrt(jnp.mean(centre * centre, axis=-1, keepdims=True) + NORM_EPSILON)
        return centre * inverse, inverse

    def norm_back(grad_result, normal, inverse, gain_row):
        scaled = grad_result * gain_row
        return inverse * (
            scaled
            - jnp.mean(scaled, axis=-1, keepdims=True)
            - normal * jnp.mean(scaled * normal, axis=-1, keepdims=True)
        )

    def load_half(source, item, half):
        body = source[item, pl.ds(pl.multiple_of(half * HALF, 16), SLOTS - HALF), :].astype(F32)
        tail = source[item, SLOTS - HALF : HALF, :].astype(F32)
        return jnp.concatenate([body, jnp.where(half == 0, tail, 0.0)], axis=0)

    def first_norm(item, low, high):
        @pl.loop(low, min(high, 5))
        def _(index):
            rows = pl.ds(pl.multiple_of(index * 112, 16), 112)
            normal, _ = norm_stats(tokens[item, rows, :].astype(F32))
            normed_one[item, rows, :] = (normal * norms[0:1, :] + norms[1:2, :]).astype(BF16)

        if high == 6:
            normal, _ = norm_stats(tokens[item, 560:SLOTS, :].astype(F32))
            normed = normal * norms[0:1, :] + norms[1:2, :]
            none = jnp.zeros((ROWS - SLOTS, normed.shape[1]), F32)
            normed_one[item, 560:ROWS, :] = jnp.concatenate([normed, none], axis=0).astype(BF16)

    weights_out(0)
    loads[2].wait()
    loads[3].wait()
    weights[1, own_block, :] = upward_f[...].astype(BF16)
    weights[2, own_block, :] = downward_f[...].astype(BF16)
    loads[4].wait()
    first_norm(0, 0, 4)
    weights_on(0, 1)
    first_norm(0, 4, 6)
    first_norm(1, 0, 2)
    weights_on(0, 2)
    first_norm(1, 2, 6)
    weights_on(0, 3)
    weights_out(1)
    loads[5].wait()
    zero_rows = jnp.zeros((KEYS - ROWS, HEAD_DIM), BF16)
    for i in range(6):
        keys[i, ROWS:KEYS, :] = zero_rows
        values[i, ROWS:KEYS, :] = zero_rows
    weights_in(0)

    def project(item):
        @pl.loop(0, 2)
        def _(half):
            rows = half_rows(half)
            joined = dot(normed_one[item, rows, :], weights[0, :, 0:576])
            for head in range(3):
                low = head * HEAD_DIM
                queries[item * 3 + head, rows, :] = (
                    joined[:, low : low + HEAD_DIM].astype(BF16) * HEAD_DIM ** (-0.5)
                ).astype(BF16)
                low += 192
                keys[item * 3 + head, rows, :] = joined[:, low : low + HEAD_DIM].astype(BF16)
                low += 192
                values[item * 3 + head, rows, :] = joined[:, low : low + HEAD_DIM].astype(BF16)

    def attend(item):
        bits = key_bits(steps[item], flags[item])

        @pl.loop(0, 3)
        def _(head):
            at = item * 3 + head
            for half, extent in ((0, NEAR_KEYS), (1, KEYS)):
                first = half * HALF
                scores = dot(queries[at, first : first + HALF, :], keys[at, 0:extent, :], NT)
                seen = jnp.bitwise_and(bits[:, 0:extent], query_bits(first)) != 0
                scores = jnp.where(seen, scores, NEGATIVE)
                spread = jnp.exp(scores - jnp.max(scores, axis=-1, keepdims=True))
                scale = 1.0 / jnp.sum(spread, axis=-1, keepdims=True)
                low = (spread * scale).astype(BF16)
                probs[at, first : first + HALF, 0:extent] = low
                heads[at, first : first + HALF, :] = dot(low, values[at, 0:extent, :]).astype(BF16)

    def to_core(kind, item, source):
        return send(source.at[item], kind.at[item], core_peer)

    def to_swap(copy, kept, received, staged, swapped, item):
        done_sending(copy)
        copy.wait_recv()
        staged[item] = (kept[item] + received[item].astype(F32)).astype(BF16)
        return send(staged.at[item], swapped.at[item], y_peer)

    def both(copy, staged, swapped, item):
        copy.wait_recv()
        return staged[item].astype(F32) + swapped[item].astype(F32)

    def attention_out(item):
        for half in (0, 1):
            rows = slice(half * HALF, (half + 1) * HALF)
            context[item, rows, :] = jnp.concatenate(
                [heads[item * 3 + head, rows, :] for head in range(3)], axis=1
            )
        outward = weights[0, :, 576:768]
        send_a[item] = dot(context[item, half_rows(1 - c), :], outward, NT).astype(BF16)
        copy = to_core(recv_one, item, send_a)
        keep[item] = dot(context[item, mine, :], outward, NT)
        return copy

    project(0)
    weights_on(1, 1)
    attend(0)
    weights_on(1, 2)
    attn_0 = attention_out(0)
    weights_on(1, 3)
    weights_out(2)
    project(1)
    swap_0 = to_swap(attn_0, keep, recv_one, send_a, swapped_one, 0)
    weights_on(2, 1)
    attend(1)
    weights_on(2, 2)
    attn_1 = attention_out(1)
    weights_on(2, 3)
    swap_1 = to_swap(attn_1, keep, recv_one, send_a, swapped_one, 1)

    def share_rows(buffer, item):
        rows = buffer.at[item, mine]
        return send(rows, rows, core_peer)

    def second_norm(copy, item):
        rows = load_half(tokens, item, c) + both(copy, send_a, swapped_one, item)
        middle[item] = rows
        normal, _ = norm_stats(rows)
        normed_two[item, mine, :] = (normal * norms[2:3, :] + norms[3:4, :]).astype(BF16)
        return share_rows(normed_two, item)

    def feed_forward(item, half, keeps):
        rows = half_rows(half)
        upper = dot(normed_two[item, rows, :], weights[1])
        grown, slope = gelu_both(upper)
        grown = grown.astype(BF16)
        hidden[item, rows, :] = grown
        pull = (dot(load_half(back, item, half).astype(BF16), weights[2]) * slope).astype(BF16)
        grad_upper[item, rows, :] = pull
        terms = dot(pull, weights[1], NT)
        lowered = dot(grown, weights[2], NT)
        if keeps:
            keep[item] = terms
            keep_low[item] = lowered
            return None
        send_a[item] = terms.astype(BF16)
        first = to_core(recv_mid, item, send_a)
        send_b[item] = lowered.astype(BF16)
        return first, to_core(recv_low, item, send_b)

    two_0 = second_norm(swap_0, 0)
    done_sending(swap_0)
    weights_in(1)
    weights_in(2)
    feed_forward(0, c, True)
    two_0.wait_recv()
    mid_0, low_0 = feed_forward(0, 1 - c, False)
    two_1 = second_norm(swap_1, 1)
    done_sending(swap_1)
    swap_mid_0 = to_swap(mid_0, keep, recv_mid, send_a, swapped_mid, 0)
    feed_forward(1, c, True)
    two_1.wait_recv()
    mid_1, low_1 = feed_forward(1, 1 - c, False)

    def band_grad(slot, first, width, left_of, right_of):
        total[slot, :, first : first + width] = dot(left_of(0), right_of(0), TN) + dot(
            left_of(1), right_of(1), TN
        )

    x_copies = {}
    z_copies = {}

    def grads_out(mat, slot):
        for k in (2, 1, 3, 0):
            x_send[mat, k] = total[slot, block_rows(2 * ((z + k) % 4) + 1 - x), :].astype(BF16)
            x_copies[mat, k] = send(x_send.at[mat, k], x_recv.at[mat, k], x_peer)

    def grads_on(mat, slot):
        for k in (2, 1, 3):
            done_sending(x_copies[mat, k])
            x_copies[mat, k].wait_recv()
            x_send[mat, k] = (
                total[slot, block_rows(2 * ((z + k) % 4) + x), :] + x_recv[mat, k].astype(F32)
            ).astype(BF16)
            z_copies[mat, k] = send(x_send.at[mat, k], z_recv.at[mat, k - 1], z_peers[k - 1])
        x_copies[mat, 0].wait_recv()
        shards_out[mat] = total[slot, own_block, :] + x_recv[mat, 0].astype(F32)

    def grads_in(mat):
        summed = shards_out[mat]
        for k in (1, 3, 2):
            z_copies[mat, k].wait_recv()
            summed += z_recv[mat, k - 1].astype(F32)
        shards_out[mat] = summed
        return jnp.sum(summed * summed)

    for first in (0, 256, 512):
        band_grad(
            0, first, 256,
            lambda i: back[i], lambda i, f=first: hidden[i, 0:SLOTS, f : f + 256],
        )
        if first == 0:
            swap_mid_1 = to_swap(mid_1, keep, recv_mid, send_a, swapped_mid, 1)
    grads_out(2, 0)
    for first in (0, 256, 512):
        band_grad(
            1, first, 256,
            lambda i: normed_two[i], lambda i, f=first: grad_upper[i, :, f : f + 256],
        )
    grads_out(1, 1)

    def middle_back(copy, item):
        grad_two = both(copy, send_a, swapped_mid, item)
        normal, inverse = norm_stats(middle[item])
        sums = (
            jnp.sum(grad_two * normal, axis=0, keepdims=True),
            jnp.sum(grad_two, axis=0, keepdims=True),
        )
        for row, part in zip((2, 3), sums):
            table_mine[row : row + 1, :] = part if item == 0 else table_mine[row : row + 1, :] + part
        pulled = load_half(back, item, c) + norm_back(
            grad_two, normal, inverse, norms[2:3, :]
        )
        grad_mid[item] = pulled
        middle_low[item, mine, :] = pulled.astype(BF16)
        return share_rows(middle_low, item)

    def attend_back(item):
        for half in (0, 1):
            rows = half_rows(half)
            pulled = dot(middle_low[item, rows, :], weights[0, :, 576:768]).astype(BF16)
            for head in range(3):
                heads[item * 3 + head, rows, :] = pulled[:, head * HEAD_DIM : (head + 1) * HEAD_DIM]

        @pl.loop(0, 3)
        def _(head):
            at = item * 3 + head
            grad_key = None
            grad_value = None
            key_rows = keys[at]
            value_rows = values[at]
            for half, extent in ((1, KEYS), (0, NEAR_KEYS)):
                first = half * HALF
                rows = slice(first, first + HALF)
                pulled = heads[at, rows, :]
                weight = dot(pulled, value_rows[0:extent], NT)
                low = probs[at, rows, 0:extent]
                wide = low.astype(F32)
                weight = wide * weight
                moved = (weight - wide * jnp.sum(weight, axis=-1, keepdims=True)).astype(BF16)
                asked = queries[at, rows, :]
                part_key = dot(moved, asked, TN)
                part_value = dot(low, pulled, TN)
                queries[at, rows, :] = (
                    dot(moved, key_rows[0:extent]) * HEAD_DIM ** (-0.5)
                ).astype(BF16)
                if grad_key is None:
                    grad_key, grad_value = part_key, part_value
                else:
                    keys[at, 0:extent, :] = (grad_key[0:extent] + part_key).astype(BF16)
                    values[at, 0:extent, :] = (grad_value[0:extent] + part_value).astype(BF16)
                    keys[at, extent:KEYS, :] = grad_key[extent:KEYS].astype(BF16)
                    values[at, extent:KEYS, :] = grad_value[extent:KEYS].astype(BF16)

        for half in (0, 1):
            rows = slice(half * HALF, (half + 1) * HALF)
            grad_triple[item, rows, :] = jnp.concatenate(
                [
                    source[item * 3 + head, rows, :]
                    for source in (queries, keys, values)
                    for head in range(3)
                ],
                axis=1,
            )

    def first_terms(item):
        inward = weights[0, :, 0:576]
        send_a[item] = dot(grad_triple[item, half_rows(1 - c), :], inward, NT).astype(BF16)
        copy = to_core(recv_one, item, send_a)
        keep[item] = dot(grad_triple[item, mine, :], inward, NT)
        return copy

    low_swap_0 = low_swap_1 = None
    ml_0 = middle_back(swap_mid_0, 0)
    done_sending(swap_mid_0)
    ml_0.wait_recv()
    attend_back(0)
    first_0 = first_terms(0)
    ml_1 = middle_back(swap_mid_1, 1)
    done_sending(swap_mid_1)
    first_swap_0 = to_swap(first_0, keep, recv_one, send_a, swapped_one, 0)
    grads_on(2, 0)
    ml_1.wait_recv()
    attend_back(1)
    first_1 = first_terms(1)
    for first, width in ((0, 256), (256, 256), (512, 64)):
        band_grad(
            0, first, width,
            lambda i: normed_one[i], lambda i, f=first, w=width: grad_triple[i, :, f : f + w],
        )
        if first == 0:
            first_swap_1 = to_swap(first_1, keep, recv_one, send_a, swapped_one, 1)
            low_swap_0 = to_swap(low_0, keep_low, recv_low, send_b, swapped_low, 0)
            low_swap_1 = to_swap(low_1, keep_low, recv_low, send_b, swapped_low, 1)
    band_grad(0, 576, 192, lambda i: middle_low[i], lambda i: context[i])
    grads_out(0, 0)
    grads_on(1, 1)

    stores = []

    def give(half_buffer, result, item):
        here = result.at[item, mine]
        store = pltpu.make_async_copy(half_buffer.at[item], here, local_sems.at[len(stores)])
        store.start()
        stores.append(store)
        return send(half_buffer.at[item], here, core_peer)

    def first_back(copy, item):
        grad_one = both(copy, send_a, swapped_one, item)
        normal, inverse = norm_stats(load_half(tokens, item, c))
        sums = (
            jnp.sum(grad_one * normal, axis=0, keepdims=True),
            jnp.sum(grad_one, axis=0, keepdims=True),
        )
        for row, part in zip((0, 1), sums):
            table_mine[row : row + 1, :] = part if item == 0 else table_mine[row : row + 1, :] + part
        grad_half[item] = (
            grad_mid[item] + norm_back(grad_one, normal, inverse, norms[0:1, :])
        ).astype(BF16)
        return give(grad_half, grad_h, item)

    rows_0 = first_back(first_swap_0, 0)
    squares = grads_in(2)
    grads_on(0, 0)
    rows_1 = first_back(first_swap_1, 1)
    squares += grads_in(1)
    squares += grads_in(0)
    table_mine[4:8, :] = jnp.broadcast_to(squares, (4, table_mine.shape[1]))

    for hop_number, peer in enumerate((core_peer, y_peer, x_peer)):
        hop = send(table_mine, table_recv.at[hop_number], peer)
        hop.wait_recv()
        done_sending(hop)
        received = table_recv[hop_number]
        if hop_number == 1:
            table_mine[4:8, :] = table_mine[4:8, :] + received[4:8]
        else:
            table_mine[...] = table_mine[...] + received
    hops = [send(table_mine, table_recv.at[2 + k], z_peers[k - 1]) for k in (1, 2, 3)]
    for hop in hops:
        hop.wait_recv()
    parts = [table_mine[...], table_recv[3], table_recv[4], table_recv[5]]
    ordered = None
    for level in range(4):
        piece = parts[0]
        for k in (1, 2, 3):
            piece = jnp.where((level + k) % 4 == z, parts[k], piece)
        ordered = piece if ordered is None else ordered + piece
    table_out[...] = ordered

    given = [rows_0, rows_1]
    for item, copy in ((0, low_swap_0), (1, low_swap_1)):
        out_half[item] = (middle[item] + both(copy, send_b, swapped_low, item)).astype(BF16)
        given.append(give(out_half, output_h, item))
    for copy in given:
        copy.wait_recv()
    for store in stores:
        store.wait()
    for copy in list(pending):
        copy.wait_send()
    for wanted, copy in later:

        @pl.when(wanted)
        def _():
            copy.wait_send()


def update_kernel(
    place, output_h, grad_h, shards_h, table_h, norms_h, *refs
):
    params_h, results, scratch = refs[:14], refs[14:32], refs[32:]
    output_to, grad_to, norm_out = results[:3]
    targets = results[3:]
    output_in, grad_in, output_v, grad_v, shards, table, norms = scratch[:7]
    params = scratch[7:21]
    updated = scratch[21:36]
    load_sems, store_sems = scratch[36:]
    loads = [
        pltpu.make_async_copy(source, target, load_sems.at[i])
        for i, (source, target) in enumerate(
            zip(
                (table_h, grad_h, output_h, shards_h, norms_h) + params_h,
                (table, grad_in, output_in, shards, norms) + params,
            )
        )
    ]
    for load in loads:
        load.start()
    stores = []

    def store(source, target):
        copy = pltpu.make_async_copy(source, target, store_sems.at[len(stores)])
        copy.start()
        stores.append(copy)

    loads[0].wait()
    sums = table[0:4, :]
    total = table[4:5, 0:1] + jnp.sum(
        jnp.sum(sums * sums, axis=1, keepdims=True), axis=0, keepdims=True
    )
    grad_norm = jnp.sqrt(total)
    norm_out[...] = grad_norm
    clip = jnp.minimum(1.0, CLIP_NORM / (grad_norm + 1e-06))

    loads[1].wait()
    for item in range(2):
        grad_v[item] = grad_in[item, 0:SLOTS, :].astype(F32)
        store(grad_v.at[item], grad_to.at[item])
    loads[2].wait()
    output_v[...] = output_in[:, 0:SLOTS, :]
    store(output_v, output_to)
    loads[3].wait()
    loads[4].wait()

    def update(index, gradients, rate, decay, master_at=None):
        m_at, v_at = 4 + index, 9 + index
        for at in (m_at, v_at) if index == 4 else (index, m_at, v_at):
            loads[5 + at].wait()
        for part, gradient in enumerate(gradients):
            at = (lambda ref: ref.at[part]) if index == 0 else (lambda ref: ref)
            master = master_at if index == 4 else at(params[index])[...]
            values = adam_update(
                master, at(params[m_at])[...], at(params[v_at])[...], gradient, clip, rate, decay
            )
            for which, value in enumerate(values):
                at(updated[3 * index + which])[...] = value
        for which in range(3):
            store(updated[3 * index + which], targets[3 * index + which])

    part = params[0].shape[2]
    update(3, [shards[2]], RATE_DOWNWARD, WEIGHT_DECAY)
    update(2, [shards[1]], RATE_UPWARD, WEIGHT_DECAY)
    update(
        0, [shards[0, :, i * part : (i + 1) * part] for i in range(3)], RATE_INWARD, WEIGHT_DECAY
    )
    update(1, [shards[0, :, 3 * part :].T], RATE_OUTWARD, WEIGHT_DECAY)
    span = params[8].shape[1]
    own_sums = sums[:, 0:span]
    own_norms = norms[:, 0:span]
    for index in range(1, 8):
        here = place[0] == index
        columns = slice(index * span, (index + 1) * span)
        own_sums = jnp.where(here, sums[:, columns], own_sums)
        own_norms = jnp.where(here, norms[:, columns], own_norms)
    update(4, [own_sums], RATE_NORMS, 0.0, own_norms)
    for copy in stores:
        copy.wait()


def fused_body(
    tokens, cotangent, step_counts, wrist_flags,
    inward_weight, outward_weight, upward_weight, downward_weight, norm_table,
    momentum_inward, momentum_outward, momentum_upward, momentum_downward, momentum_norms,
    variance_inward, variance_outward, variance_upward, variance_downward, variance_norms,
):
    width = norm_table.shape[1]
    block = upward_weight.shape[0]
    any_spec = pl.BlockSpec(memory_space=pl.ANY)
    vmem = pl.BlockSpec(memory_space=pltpu.VMEM)
    smem = pl.BlockSpec(memory_space=pltpu.SMEM)
    rows = pltpu.VMEM((2, ROWS, width), BF16)
    halves = pltpu.VMEM((2, HALF, width), BF16)
    keep = pltpu.VMEM((2, HALF, width), F32)
    output, grads, shards, table = pl.pallas_call(
        fused_kernel,
        out_shape=(
            jax.ShapeDtypeStruct((2, ROWS, width), BF16),
            jax.ShapeDtypeStruct((2, ROWS, width), BF16),
            jax.ShapeDtypeStruct((3, block, width), F32),
            jax.ShapeDtypeStruct((8, width), F32),
        ),
        in_specs=[smem, smem, any_spec, any_spec, any_spec, any_spec, any_spec, any_spec, vmem],
        out_specs=(any_spec, any_spec, vmem, vmem),
        scratch_shapes=[
            pltpu.VMEM((3, width, width), BF16),
            pltpu.VMEM((2, SLOTS, width), BF16),
            pltpu.VMEM((2, SLOTS, width), BF16),
            rows,
            pltpu.VMEM((6, ROWS, HEAD_DIM), BF16),
            pltpu.VMEM((6, KEYS, HEAD_DIM), BF16),
            pltpu.VMEM((6, KEYS, HEAD_DIM), BF16),
            pltpu.VMEM((6, ROWS, KEYS), BF16),
            pltpu.VMEM((6, ROWS, HEAD_DIM), BF16),
            pltpu.VMEM((2, ROWS, 192), BF16),
            keep,
            rows,
            rows,
            rows,
            rows,
            halves,
            halves,
            keep,
            keep,
            halves,
            halves,
            halves,
            halves,
            halves,
            halves,
            halves,
            halves,
            keep,
            pltpu.VMEM((2, ROWS, 576), BF16),
            pltpu.VMEM((2, width, width), F32),
            pltpu.VMEM((3, 4, block, width), BF16),
            pltpu.VMEM((3, 4, block, width), BF16),
            pltpu.VMEM((3, 3, block, width), BF16),
            pltpu.VMEM((8, width), F32),
            pltpu.VMEM((6, 8, width), F32),
            pltpu.VMEM(inward_weight.shape, F32),
            pltpu.VMEM(outward_weight.shape, F32),
            pltpu.VMEM(upward_weight.shape, F32),
            pltpu.VMEM(upward_weight.shape, F32),
            pltpu.SemaphoreType.DMA((N_REMOTE,)),
            pltpu.SemaphoreType.DMA((N_REMOTE,)),
            pltpu.SemaphoreType.DMA((10,)),
        ],
        compiler_params=pltpu.CompilerParams(
            collective_id=0, has_side_effects=True, vmem_limit_bytes=VMEM_BYTES
        ),
        name="block_step",
    )(
        step_counts,
        wrist_flags,
        inward_weight,
        outward_weight,
        upward_weight,
        downward_weight.T,
        tokens,
        cotangent,
        norm_table,
    )
    place = jnp.reshape(lax.axis_index("dp"), (1,)).astype(jnp.int32)
    params = (
        inward_weight, outward_weight, upward_weight, downward_weight.T,
        momentum_inward, momentum_outward, momentum_upward, momentum_downward.T, momentum_norms,
        variance_inward, variance_outward, variance_upward, variance_downward.T, variance_norms,
    )
    shapes = [param.shape for param in params]
    updates = [shape for shape in shapes[:4] + shapes[8:9] for _ in range(3)]
    padded = pltpu.VMEM((2, ROWS, width), BF16)
    results = pl.pallas_call(
        update_kernel,
        out_shape=(
            jax.ShapeDtypeStruct((2, SLOTS, width), BF16),
            jax.ShapeDtypeStruct((2, SLOTS, width), F32),
            jax.ShapeDtypeStruct((1, 1), F32),
            *[jax.ShapeDtypeStruct(shape, F32) for shape in updates],
        ),
        in_specs=[smem] + [any_spec] * 19,
        out_specs=(any_spec, any_spec, vmem) + (any_spec,) * 15,
        scratch_shapes=[
            padded,
            padded,
            pltpu.VMEM((2, SLOTS, width), BF16),
            pltpu.VMEM((2, SLOTS, width), F32),
            pltpu.VMEM((3, block, width), F32),
            pltpu.VMEM((8, width), F32),
            pltpu.VMEM((4, width), F32),
            *[pltpu.VMEM(shape, F32) for shape in shapes],
            *[pltpu.VMEM(shape, F32) for shape in updates],
            pltpu.SemaphoreType.DMA((19,)),
            pltpu.SemaphoreType.DMA((18,)),
        ],
        compiler_params=pltpu.CompilerParams(vmem_limit_bytes=VMEM_BYTES),
        name="update_step",
    )(place, output, grads, shards, table, norm_table, *params)
    updated = list(results[3:])
    for index in (9, 10, 11):
        updated[index] = updated[index].T
    return (results[0], results[1], results[2][0, 0], *updated)


def solution(mesh):
    fits = mesh.shape["dp"] == 8 and mesh.shape["mp"] == 4
    return whole_program(mesh, fused_body if fits else body)
```

```python
import jax
import jax.numpy as jnp
from jax import lax
from jax.experimental import pallas as pl
from jax.experimental.pallas import tpu as pltpu
from jax.sharding import PartitionSpec as P

HEAD_DIM = 64
TASK = 16
PRIMARY = 256
WRIST = 64
READOUT = 4
SLOTS = 664
MB = 2
STEP = 10


NORM_EPSILON = 1e-06
CLIP_NORM = 1.0
BETA_ONE = 0.9
BETA_TWO = 0.999
ADAM_EPSILON = 1e-08
WEIGHT_DECAY = 0.1
NEGATIVE = -1e30
RATE_INWARD = 0.05
RATE_OUTWARD = 0.15
RATE_UPWARD = 0.04
RATE_DOWNWARD = 0.02
RATE_NORMS = 0.5


def slot_mask(live_steps, has_wrist):
    position = jnp.arange(SLOTS, dtype=jnp.int32)
    relative = position - TASK
    period = PRIMARY + WRIST + READOUT
    is_task = relative < 0
    forward_pos = jnp.maximum(relative, 0)
    stepno = forward_pos // period
    offset = forward_pos % period
    not_task = jnp.logical_not(is_task)
    is_read = jnp.logical_and(not_task, offset >= PRIMARY + WRIST)
    is_obs = jnp.logical_and(not_task, jnp.logical_not(is_read))
    is_wrist = jnp.logical_and(is_obs, offset >= PRIMARY)
    present = jnp.logical_or(
        is_task,
        jnp.logical_and(
            stepno < live_steps, jnp.logical_or(jnp.logical_not(is_wrist), has_wrist == 1)
        ),
    )
    see_obs = is_obs[None, :] & not_task[:, None] & (stepno[None, :] <= stepno[:, None])
    see_read = is_read[None, :] & is_read[:, None] & (stepno[None, :] == stepno[:, None])
    return present[None, :] & (is_task[None, :] | see_obs | see_read)


def layer_stats(values):
    centre = values - jnp.mean(values, axis=-1, keepdims=True)
    inverse = lax.rsqrt(jnp.mean(centre * centre, axis=-1, keepdims=True) + NORM_EPSILON)
    return (centre * inverse, inverse)


def layer_back(grad_result, normal, inverse, gain_row):
    scaled = grad_result * gain_row
    return inverse * (
        scaled
        - jnp.mean(scaled, axis=-1, keepdims=True)
        - normal * jnp.mean(scaled * normal, axis=-1, keepdims=True)
    )


def gelu_tanh(values):
    return (
        0.5
        * values
        * (1.0 + jnp.tanh(0.7978845608028654 * (values + 0.044715 * values * values * values)))
    )


def attention_scores(queries, key_heads, allowed, score_scale):
    dotted = (
        jnp.einsum("nqhd,nkhd->nhqk", queries, key_heads, preferred_element_type=jnp.float32)
        * score_scale
    )
    return jnp.where(allowed, dotted, NEGATIVE)


def adam_update(master, momentum, variance, gradient, clip_scale, step_rate, decay_rate):
    clipped = gradient * clip_scale
    moment_one = BETA_ONE * momentum + (1.0 - BETA_ONE) * clipped
    moment_two = BETA_TWO * variance + (1.0 - BETA_TWO) * clipped * clipped
    first_hat = moment_one / (1.0 - BETA_ONE**STEP)
    second_hat = moment_two / (1.0 - BETA_TWO**STEP)
    updated = master - step_rate * (
        first_hat / (jnp.sqrt(second_hat) + ADAM_EPSILON) + decay_rate * master
    )
    return (moment_one, moment_two, updated)


def body(
    tokens,
    cotangent,
    step_counts,
    wrist_flags,
    inward_weight,
    outward_weight,
    upward_weight,
    downward_weight,
    norm_table,
    momentum_inward,
    momentum_outward,
    momentum_upward,
    momentum_downward,
    momentum_norms,
    variance_inward,
    variance_outward,
    variance_upward,
    variance_downward,
    variance_norms,
):
    full_inward, full_outward, full_upward, full_downward = (
        lax.all_gather(inward_weight.astype(jnp.bfloat16), "dp", axis=1, tiled=True),
        lax.all_gather(outward_weight.astype(jnp.bfloat16), "dp", axis=1, tiled=True),
        lax.all_gather(upward_weight.astype(jnp.bfloat16), "dp", axis=0, tiled=True),
        lax.all_gather(downward_weight.astype(jnp.bfloat16), "dp", axis=1, tiled=True),
    )
    model_width = norm_table.shape[1]
    local_heads = full_inward.shape[2] // HEAD_DIM
    score_scale = HEAD_DIM ** (-0.5)
    per_batch = tokens.shape[0] // MB
    row_count = per_batch * SLOTS
    share_rows = row_count // lax.axis_size("mp")
    share_start = lax.axis_index("mp") * share_rows
    results = []
    input_grads = []
    local_sums = None
    for batch_index in range(MB):
        start_item = batch_index * per_batch
        block_tokens = (
            tokens[start_item : start_item + per_batch]
            .astype(jnp.float32)
            .reshape(row_count, model_width)
        )
        block_back = (
            cotangent[start_item : start_item + per_batch]
            .astype(jnp.float32)
            .reshape(row_count, model_width)
        )
        allowed = jax.vmap(slot_mask)(
            step_counts[start_item : start_item + per_batch],
            wrist_flags[start_item : start_item + per_batch],
        )[:, None]
        normal_one, inverse_one = layer_stats(block_tokens)
        normed_one = (normal_one * norm_table[0] + norm_table[1]).astype(jnp.bfloat16)
        projected = jnp.einsum(
            "rd,cdm->crm", normed_one, full_inward, preferred_element_type=jnp.float32
        ).astype(jnp.bfloat16)
        triple = projected.reshape(3, per_batch, SLOTS, local_heads, HEAD_DIM)
        queries = triple[0]
        key_heads = triple[1]
        value_heads = triple[2]
        scores = attention_scores(queries, key_heads, allowed, score_scale)
        highest = jnp.max(scores, axis=-1, keepdims=True)
        log_total = highest + jnp.log(jnp.sum(jnp.exp(scores - highest), axis=-1, keepdims=True))
        attention_low = jnp.exp(scores - log_total).astype(jnp.bfloat16)
        context = (
            jnp.einsum(
                "nhqk,nkhd->nqhd", attention_low, value_heads, preferred_element_type=jnp.float32
            )
            .astype(jnp.bfloat16)
            .reshape(row_count, -1)
        )
        attn_terms = jnp.dot(context, full_outward, preferred_element_type=jnp.float32)
        tokens_share = lax.dynamic_slice_in_dim(block_tokens, share_start, share_rows, 0)
        back_share = lax.dynamic_slice_in_dim(block_back, share_start, share_rows, 0)
        middle_share = tokens_share + lax.psum_scatter(
            attn_terms, "mp", scatter_dimension=0, tiled=True
        )
        normal_two, inverse_two = layer_stats(middle_share)
        normed_share = (normal_two * norm_table[2] + norm_table[3]).astype(jnp.bfloat16)
        normed_two = lax.all_gather(normed_share, "mp", axis=0, tiled=True)
        upper_pre = jnp.dot(normed_two, full_upward, preferred_element_type=jnp.float32)
        hidden = gelu_tanh(upper_pre).astype(jnp.bfloat16)
        lowered_share = lax.psum_scatter(
            jnp.dot(hidden, full_downward, preferred_element_type=jnp.float32).astype(jnp.bfloat16),
            "mp",
            scatter_dimension=0,
            tiled=True,
        ).astype(jnp.float32)
        output_share = (middle_share + lowered_share).astype(jnp.bfloat16)
        back_rows = block_back.astype(jnp.bfloat16)
        grad_down = jnp.einsum("rf,rd->fd", hidden, back_rows, preferred_element_type=jnp.float32)
        grad_hidden = jnp.einsum(
            "rd,fd->rf", back_rows, full_downward, preferred_element_type=jnp.float32
        )
        upper_pull = jax.vjp(gelu_tanh, upper_pre)[1]
        grad_upper = upper_pull(grad_hidden)[0].astype(jnp.bfloat16)
        grad_up = jnp.einsum(
            "rd,rf->df", normed_two, grad_upper, preferred_element_type=jnp.float32
        )
        normed_terms = jnp.einsum(
            "rf,df->rd", grad_upper, full_upward, preferred_element_type=jnp.float32
        )
        grad_normed_two = lax.psum_scatter(normed_terms, "mp", scatter_dimension=0, tiled=True)
        gain_two = jnp.sum(grad_normed_two * normal_two, axis=0)
        shift_two = jnp.sum(grad_normed_two, axis=0)
        grad_middle_share = back_share + layer_back(
            grad_normed_two, normal_two, inverse_two, norm_table[2]
        )
        middle_low, output_rows = (
            lax.all_gather(grad_middle_share.astype(jnp.bfloat16), "mp", axis=0, tiled=True),
            lax.all_gather(output_share, "mp", axis=0, tiled=True),
        )
        results.append(output_rows.reshape(per_batch, SLOTS, model_width))
        grad_out = jnp.einsum("rm,rd->md", context, middle_low, preferred_element_type=jnp.float32)
        grad_context = (
            jnp.einsum("rd,md->rm", middle_low, full_outward, preferred_element_type=jnp.float32)
            .astype(jnp.bfloat16)
            .reshape(per_batch, SLOTS, local_heads, HEAD_DIM)
        )
        scores_again = attention_scores(queries, key_heads, allowed, score_scale)
        attention_full = jnp.exp(scores_again - log_total)
        attention_again = attention_full.astype(jnp.bfloat16)
        grad_values = jnp.einsum(
            "nhqk,nqhd->nkhd", attention_again, grad_context, preferred_element_type=jnp.float32
        ).astype(jnp.bfloat16)
        grad_weights = jnp.einsum(
            "nqhd,nkhd->nhqk", grad_context, value_heads, preferred_element_type=jnp.float32
        )
        grad_scores = (
            attention_full
            * (grad_weights - jnp.sum(grad_weights * attention_full, axis=-1, keepdims=True))
        ).astype(jnp.bfloat16)
        grad_queries = (
            jnp.einsum(
                "nhqk,nkhd->nqhd", grad_scores, key_heads, preferred_element_type=jnp.float32
            )
            * score_scale
        ).astype(jnp.bfloat16)
        grad_keys = (
            jnp.einsum("nhqk,nqhd->nkhd", grad_scores, queries, preferred_element_type=jnp.float32)
            * score_scale
        ).astype(jnp.bfloat16)
        grad_triple = jnp.stack([grad_queries, grad_keys, grad_values]).reshape(3, row_count, -1)
        grad_in = jnp.einsum(
            "rd,crm->cdm", normed_one, grad_triple, preferred_element_type=jnp.float32
        )
        first_terms = jnp.einsum(
            "crm,cdm->rd", grad_triple, full_inward, preferred_element_type=jnp.float32
        )
        grad_normed_one = lax.psum_scatter(first_terms, "mp", scatter_dimension=0, tiled=True)
        normal_share = lax.dynamic_slice_in_dim(normal_one, share_start, share_rows, 0)
        inverse_share = lax.dynamic_slice_in_dim(inverse_one, share_start, share_rows, 0)
        gain_one = jnp.sum(grad_normed_one * normal_share, axis=0)
        shift_one = jnp.sum(grad_normed_one, axis=0)
        tokens_grad_share = grad_middle_share + layer_back(
            grad_normed_one, normal_share, inverse_share, norm_table[0]
        )
        table_terms = jnp.stack([gain_one, shift_one, gain_two, shift_two])[None]
        grad_tokens, gathered_tables = (
            lax.all_gather(tokens_grad_share, "mp", axis=0, tiled=True),
            lax.all_gather(table_terms, "mp", axis=0, tiled=True),
        )
        grad_table = jnp.sum(gathered_tables, axis=0)
        input_grads.append(grad_tokens.reshape(per_batch, SLOTS, model_width))
        batch_grads = (grad_in, grad_out, grad_up, grad_down, grad_table)
        if local_sums is None:
            local_sums = batch_grads
        else:
            local_sums = tuple((former + latter for former, latter in zip(local_sums, batch_grads)))
    shards = (
        lax.psum_scatter(local_sums[0], "dp", scatter_dimension=1, tiled=True),
        lax.psum_scatter(local_sums[1], "dp", scatter_dimension=1, tiled=True),
        lax.psum_scatter(local_sums[2], "dp", scatter_dimension=0, tiled=True),
        lax.psum_scatter(local_sums[3], "dp", scatter_dimension=1, tiled=True),
        lax.psum_scatter(local_sums[4], "dp", scatter_dimension=1, tiled=True),
    )
    mp_count = lax.axis_size("mp")
    squares = (
        sum((jnp.sum(piece * piece) for piece in shards[:4]))
        + jnp.sum(shards[4] * shards[4]) / mp_count
    )
    grad_norm = jnp.sqrt(lax.psum(squares, ("dp", "mp")))
    clip_scale = jnp.minimum(1.0, CLIP_NORM / (grad_norm + 1e-06))
    shard_width = shards[4].shape[1]
    own_table = lax.dynamic_slice_in_dim(
        norm_table, lax.axis_index("dp") * shard_width, shard_width, 1
    )
    inward_new = adam_update(
        inward_weight,
        momentum_inward,
        variance_inward,
        shards[0],
        clip_scale,
        RATE_INWARD,
        WEIGHT_DECAY,
    )
    outward_new = adam_update(
        outward_weight,
        momentum_outward,
        variance_outward,
        shards[1],
        clip_scale,
        RATE_OUTWARD,
        WEIGHT_DECAY,
    )
    upward_new = adam_update(
        upward_weight,
        momentum_upward,
        variance_upward,
        shards[2],
        clip_scale,
        RATE_UPWARD,
        WEIGHT_DECAY,
    )
    downward_new = adam_update(
        downward_weight,
        momentum_downward,
        variance_downward,
        shards[3],
        clip_scale,
        RATE_DOWNWARD,
        WEIGHT_DECAY,
    )
    norms_new = adam_update(
        own_table, momentum_norms, variance_norms, shards[4], clip_scale, RATE_NORMS, 0.0
    )
    output = jnp.concatenate(results, axis=0)
    input_grad = jnp.concatenate(input_grads, axis=0)
    return (
        output,
        input_grad,
        grad_norm,
        inward_new[0],
        inward_new[1],
        inward_new[2],
        outward_new[0],
        outward_new[1],
        outward_new[2],
        upward_new[0],
        upward_new[1],
        upward_new[2],
        downward_new[0],
        downward_new[1],
        downward_new[2],
        norms_new[0],
        norms_new[1],
        norms_new[2],
    )


def whole_program(mesh, function):
    placed = (
        P("dp", None, None),
        P("dp", None, None),
        P("dp"),
        P("dp"),
        P(None, "dp", "mp"),
        P("mp", "dp"),
        P("dp", "mp"),
        P("mp", "dp"),
        P(),
        P(None, "dp", "mp"),
        P("mp", "dp"),
        P("dp", "mp"),
        P("mp", "dp"),
        P(None, "dp"),
        P(None, "dp", "mp"),
        P("mp", "dp"),
        P("dp", "mp"),
        P("mp", "dp"),
        P(None, "dp"),
    )
    return jax.shard_map(
        function,
        mesh=mesh,
        in_specs=placed,
        out_specs=(
            P("dp", None, None),
            P("dp", None, None),
            P(),
            P(None, "dp", "mp"),
            P(None, "dp", "mp"),
            P(None, "dp", "mp"),
            P("mp", "dp"),
            P("mp", "dp"),
            P("mp", "dp"),
            P("dp", "mp"),
            P("dp", "mp"),
            P("dp", "mp"),
            P("mp", "dp"),
            P("mp", "dp"),
            P("mp", "dp"),
            P(None, "dp"),
            P(None, "dp"),
            P(None, "dp"),
        ),
        check_vma=False,
    )


NN = (((1,), (0,)), ((), ()))
NT = (((1,), (1,)), ((), ()))
TN = (((0,), (0,)), ((), ()))
MESH = pl.DeviceIdType.MESH
F32 = jnp.float32
BF16 = jnp.bfloat16
ROWS = 672
HALF = ROWS // 2
KEYS = 768
NEAR_KEYS = 384
FIRST_COLUMNS = 640
PERIOD = PRIMARY + WRIST + READOUT


def dot(left, right, dims=NN):
    return lax.dot_general(left, right, dims, preferred_element_type=F32)


def gelu_both(values):
    square = values * values
    inner = 0.7978845608028654 * values * (1.0 + 0.044715 * square)
    bend = jnp.tanh(inner)
    half_up = 0.5 + 0.5 * bend
    slope = half_up + 0.5 * values * (1.0 - bend * bend) * (
        0.7978845608028654 * (1.0 + 0.134145 * square)
    )
    return values * half_up, slope


def key_bits(live_steps, has_wrist):
    place = lax.broadcasted_iota(jnp.int32, (1, KEYS), 1)
    relative = place - TASK
    is_task = relative < 0
    later = relative >= PERIOD
    offset = jnp.where(later, relative - PERIOD, relative)
    is_read = offset >= PRIMARY + WRIST
    is_wrist = jnp.logical_and(offset >= PRIMARY, offset < PRIMARY + WRIST)
    step_of = jnp.where(later, 1, 0)
    alive = jnp.logical_and(
        step_of < live_steps, jnp.logical_or(jnp.logical_not(is_wrist), has_wrist == 1)
    )
    bits = jnp.where(is_read, jnp.where(later, 16, 8), jnp.where(later, 4, 2))
    bits = jnp.where(alive, bits, 0)
    bits = jnp.where(is_task, 1, bits)
    return jnp.where(place < SLOTS, bits, 0)


def query_bits(first):
    place = lax.broadcasted_iota(jnp.int32, (HALF, 1), 0) + first
    relative = place - TASK
    is_task = relative < 0
    later = relative >= PERIOD
    offset = jnp.where(later, relative - PERIOD, relative)
    is_read = offset >= PRIMARY + WRIST
    bits = jnp.where(later, 7, 3) + jnp.where(is_read, jnp.where(later, 16, 8), 0)
    return jnp.where(is_task, 1, bits)


N_REMOTE = 128
VMEM_BYTES = 64 * 1024 * 1024 - 65536


def fused_kernel(
    steps, flags, inward_h, outward_h, upward_h, downward_h, tokens_h, back_h, norms,
    output_h, grad_h, shards_out, table_out,
    weights, tokens, back, normed_one, queries, keys, values, probs, heads, context,
    middle, normed_two, hidden, grad_upper, middle_low, out_half, grad_half,
    keep, keep_low, send_a, send_b,
    recv_one, recv_mid, recv_low, swapped_one, swapped_mid, swapped_low,
    grad_mid, grad_triple, total, x_send, x_recv, z_recv,
    table_mine, table_recv, inward_f, outward_f, upward_f, downward_f,
    send_sems, recv_sems, local_sems,
):
    dp = lax.axis_index("dp")
    mp = lax.axis_index("mp")
    z, x = dp // 2, dp % 2
    y, c = mp // 2, mp % 2
    core_peer = (dp, y * 2 + 1 - c)
    y_peer = (dp, (1 - y) * 2 + c)
    x_peer = (z * 2 + 1 - x, mp)
    z_peers = [(((z + k) % 4) * 2 + x, mp) for k in (1, 2, 3)]
    xz_peers = [(((z + k) % 4) * 2 + 1 - x, mp) for k in (1, 2, 3)]
    diagonal_peer = (dp, (1 - y) * 2 + 1 - c)
    all_peers = [core_peer, y_peer, x_peer, diagonal_peer] + z_peers + xz_peers
    block = weights.shape[1] // 8
    used = []
    pending = []

    def describe(index, src, dst, peer):
        return pltpu.make_async_remote_copy(
            src_ref=src, dst_ref=dst, send_sem=send_sems.at[index], recv_sem=recv_sems.at[index],
            device_id=peer, device_id_type=MESH,
        )

    def send(src, dst, peer):
        used.append(0)
        copy = describe(len(used) - 1, src, dst, peer)
        copy.start()
        pending.append(copy)
        return copy

    def done_sending(*copies):
        for copy in copies:
            copy.wait_send()
            pending[:] = [other for other in pending if other is not copy]

    def block_rows(index):
        return pl.ds(pl.multiple_of(index * block, 32), block)

    def half_rows(half):
        return pl.ds(pl.multiple_of(half * HALF, 16), HALF)

    mine = half_rows(c)
    own_block = block_rows(dp)
    loads = [
        pltpu.make_async_copy(source, target, local_sems.at[4 + i])
        for i, (source, target) in enumerate(
            (
                (inward_h, inward_f),
                (outward_h, outward_f),
                (upward_h, upward_f),
                (downward_h, downward_f),
                (tokens_h, tokens),
                (back_h, back),
            )
        )
    ]
    for load in loads:
        load.start()

    barrier = pltpu.get_barrier_semaphore()
    for peer in all_peers:
        pl.semaphore_signal(barrier, inc=1, device_id=peer, device_id_type=MESH)
    loads[0].wait()
    loads[1].wait()
    weights[0, own_block, :] = jnp.concatenate(
        [inward_f[0], inward_f[1], inward_f[2], outward_f[...].T], axis=1
    ).astype(BF16)
    pl.semaphore_wait(barrier, len(all_peers))

    later = []
    z_index = {}
    for mat in (0,):
        for sign in (1, -1):
            for j in (1, 2, 3):
                z_index[mat, sign, j] = len(used)
                used.append(0)
                z_index[mat, sign, j, "x"] = len(used)
                used.append(0)
    own_x = {}

    def z_send_block(mat, sign, j):
        origin = z - sign * (j - 1)
        rows = weights.at[mat, block_rows(origin * 2 + x), 0:FIRST_COLUMNS]
        there = ((z + sign) * 2 + x, mp)
        copy = describe(z_index[mat, sign, j], rows, rows, there)
        wanted = jnp.logical_and(
            jnp.logical_and(origin >= 0, origin <= 3), z < 3 if sign == 1 else z > 0
        )

        @pl.when(wanted)
        def _():
            copy.start()

        later.append((wanted, copy))

    straight = {}
    onward = {}

    def part(mat, rows):
        if mat == 3:
            return weights.at[0, rows, FIRST_COLUMNS:]
        return weights.at[mat, rows, 0:FIRST_COLUMNS] if mat == 0 else weights.at[mat, rows]

    for mat in (3, 1, 2):
        for k in (1, 3, 2):
            rows = part(mat, block_rows(((z + 4 - k) % 4) * 2 + x))
            used.append(0)
            onward[mat, k] = describe(len(used) - 1, rows, rows, x_peer)

    def straight_out(mat):
        rows = part(mat, own_block)
        for k in (1, 3, 2):
            straight[mat, k] = send(rows, rows, z_peers[k - 1])

    def pass_x(mat, *places):
        for k in places:
            straight[mat, k].wait_recv()
            onward[mat, k].start()

    def straight_in(mat):
        own_x[mat].wait_recv()
        for k in (1, 3, 2):
            onward[mat, k].wait_recv()

    def z_sends_out(mat):
        for sign in (1, -1):
            z_send_block(mat, sign, 1)

    def own_out(mat):
        rows = part(mat, own_block)
        own_x[mat] = send(rows, rows, x_peer)

    def arrives(sign, j):
        return z >= j if sign == 1 else z <= 3 - j

    def block_at(mat, sign, j):
        return weights.at[mat, block_rows((z - sign * j) * 2 + x), 0:FIRST_COLUMNS]

    def weights_on(mat, j):
        for sign in (1, -1):
            here = arrives(sign, j)
            rows = block_at(mat, sign, j)
            onward = describe(z_index[mat, sign, j, "x"], rows, rows, x_peer)

            @pl.when(here)
            def _():
                describe(z_index[mat, sign, j], rows, rows, x_peer).wait_recv()

            if j < 3:
                z_send_block(mat, sign, j + 1)

            @pl.when(here)
            def _():
                onward.start()

            later.append((here, onward))

    def weights_in(mat):
        own_x[mat].wait_recv()
        for j in (1, 2, 3):
            for sign in (1, -1):
                rows = block_at(mat, sign, j)

                @pl.when(arrives(sign, j))
                def _():
                    describe(z_index[mat, sign, j, "x"], rows, rows, x_peer).wait_recv()

    def norm_stats(rows):
        centre = rows - jnp.mean(rows, axis=-1, keepdims=True)
        inverse = lax.rsqrt(jnp.mean(centre * centre, axis=-1, keepdims=True) + NORM_EPSILON)
        return centre * inverse, inverse

    def norm_back(grad_result, normal, inverse, gain_row):
        scaled = grad_result * gain_row
        return inverse * (
            scaled
            - jnp.mean(scaled, axis=-1, keepdims=True)
            - normal * jnp.mean(scaled * normal, axis=-1, keepdims=True)
        )

    def load_half(source, item, half):
        body = source[item, pl.ds(pl.multiple_of(half * HALF, 16), SLOTS - HALF), :].astype(F32)
        tail = source[item, SLOTS - HALF : HALF, :].astype(F32)
        return jnp.concatenate([body, jnp.where(half == 0, tail, 0.0)], axis=0)

    def first_norm(item, low, high):
        @pl.loop(low, min(high, 5))
        def _(index):
            rows = pl.ds(pl.multiple_of(index * 112, 16), 112)
            normal, _ = norm_stats(tokens[item, rows, :].astype(F32))
            normed_one[item, rows, :] = (normal * norms[0:1, :] + norms[1:2, :]).astype(BF16)

        if high == 6:
            normal, _ = norm_stats(tokens[item, 560:SLOTS, :].astype(F32))
            normed = normal * norms[0:1, :] + norms[1:2, :]
            none = jnp.zeros((ROWS - SLOTS, normed.shape[1]), F32)
            normed_one[item, 560:ROWS, :] = jnp.concatenate([normed, none], axis=0).astype(BF16)

    z_sends_out(0)
    own_out(0)
    loads[2].wait()
    loads[3].wait()
    weights[1, own_block, :] = upward_f[...].astype(BF16)
    weights[2, own_block, :] = downward_f[...].astype(BF16)
    loads[4].wait()
    first_norm(0, 0, 4)
    weights_on(0, 1)
    first_norm(0, 4, 6)
    first_norm(1, 0, 2)
    weights_on(0, 2)
    for mat in (3, 1, 2):
        straight_out(mat)
    first_norm(1, 2, 6)
    weights_on(0, 3)
    for mat in (3, 1, 2):
        own_out(mat)
    loads[5].wait()
    zero_rows = jnp.zeros((KEYS - ROWS, HEAD_DIM), BF16)
    for i in range(6):
        keys[i, ROWS:KEYS, :] = zero_rows
        values[i, ROWS:KEYS, :] = zero_rows
    weights_in(0)

    def project(item):
        @pl.loop(0, 2)
        def _(half):
            rows = half_rows(half)
            joined = dot(normed_one[item, rows, :], weights[0, :, 0:576])
            for head in range(3):
                low = head * HEAD_DIM
                queries[item * 3 + head, rows, :] = (
                    joined[:, low : low + HEAD_DIM].astype(BF16) * HEAD_DIM ** (-0.5)
                ).astype(BF16)
                low += 192
                keys[item * 3 + head, rows, :] = joined[:, low : low + HEAD_DIM].astype(BF16)
                low += 192
                values[item * 3 + head, rows, :] = joined[:, low : low + HEAD_DIM].astype(BF16)

    def attend(item):
        bits = key_bits(steps[item], flags[item])

        @pl.loop(0, 3)
        def _(head):
            at = item * 3 + head
            for half, extent in ((0, NEAR_KEYS), (1, KEYS)):
                first = half * HALF
                scores = dot(queries[at, first : first + HALF, :], keys[at, 0:extent, :], NT)
                seen = jnp.bitwise_and(bits[:, 0:extent], query_bits(first)) != 0
                scores = jnp.where(seen, scores, NEGATIVE)
                spread = jnp.exp(scores - jnp.max(scores, axis=-1, keepdims=True))
                scale = 1.0 / jnp.sum(spread, axis=-1, keepdims=True)
                low = (spread * scale).astype(BF16)
                probs[at, first : first + HALF, 0:extent] = low
                heads[at, first : first + HALF, :] = dot(low, values[at, 0:extent, :]).astype(BF16)

    def to_core(kind, item, source):
        return send(source.at[item], kind.at[item], core_peer)

    def to_swap(copy, kept, received, staged, swapped, item):
        done_sending(copy)
        copy.wait_recv()
        staged[item] = (kept[item] + received[item].astype(F32)).astype(BF16)
        return send(staged.at[item], swapped.at[item], y_peer)

    def both(copy, staged, swapped, item):
        copy.wait_recv()
        return staged[item].astype(F32) + swapped[item].astype(F32)

    def attention_out(item):
        for half in (0, 1):
            rows = slice(half * HALF, (half + 1) * HALF)
            context[item, rows, :] = jnp.concatenate(
                [heads[item * 3 + head, rows, :] for head in range(3)], axis=1
            )
        outward = weights[0, :, 576:768]
        send_a[item] = dot(context[item, half_rows(1 - c), :], outward, NT).astype(BF16)
        copy = to_core(recv_one, item, send_a)
        keep[item] = dot(context[item, mine, :], outward, NT)
        return copy

    project(0)
    pass_x(3, 1, 3, 2)
    attend(0)
    straight_in(3)
    attn_0 = attention_out(0)
    project(1)
    swap_0 = to_swap(attn_0, keep, recv_one, send_a, swapped_one, 0)
    pass_x(1, 1, 3)
    attend(1)
    pass_x(1, 2)
    attn_1 = attention_out(1)
    swap_1 = to_swap(attn_1, keep, recv_one, send_a, swapped_one, 1)
    pass_x(2, 1, 3)

    def share_rows(buffer, item):
        rows = buffer.at[item, mine]
        return send(rows, rows, core_peer)

    def second_norm(copy, item):
        rows = load_half(tokens, item, c) + both(copy, send_a, swapped_one, item)
        middle[item] = rows
        normal, _ = norm_stats(rows)
        normed_two[item, mine, :] = (normal * norms[2:3, :] + norms[3:4, :]).astype(BF16)
        return share_rows(normed_two, item)

    def feed_up(item, half):
        rows = half_rows(half)
        grown, slope = gelu_both(dot(normed_two[item, rows, :], weights[1]))
        hidden[item, rows, :] = grown.astype(BF16)
        total[item, rows, :] = slope

    def feed_down(item, half, keeps):
        rows = half_rows(half)
        grown = hidden[item, rows, :]
        pulled = dot(load_half(back, item, half).astype(BF16), weights[2])
        pull = (pulled * total[item, rows, :]).astype(BF16)
        grad_upper[item, rows, :] = pull
        terms = dot(pull, weights[1], NT)
        lowered = dot(grown, weights[2], NT)
        if keeps:
            keep[item] = terms
            keep_low[item] = lowered
            return None
        send_a[item] = terms.astype(BF16)
        first = to_core(recv_mid, item, send_a)
        send_b[item] = lowered.astype(BF16)
        return first, to_core(recv_low, item, send_b)

    two_0 = second_norm(swap_0, 0)
    done_sending(swap_0)
    straight_in(1)
    feed_up(0, c)
    pass_x(2, 2)
    two_0.wait_recv()
    feed_up(0, 1 - c)
    straight_in(2)
    mid_0, low_0 = feed_down(0, 1 - c, False)
    feed_down(0, c, True)
    swap_mid_0 = to_swap(mid_0, keep, recv_mid, send_a, swapped_mid, 0)
    two_1 = second_norm(swap_1, 1)
    done_sending(swap_1)
    feed_up(1, c)
    two_1.wait_recv()
    feed_up(1, 1 - c)
    mid_1, low_1 = feed_down(1, 1 - c, False)
    feed_down(1, c, True)

    def band_grad(slot, first, width, left_of, right_of):
        total[slot, :, first : first + width] = dot(left_of(0), right_of(0), TN) + dot(
            left_of(1), right_of(1), TN
        )

    x_copies = {}
    z_copies = {}

    def grads_out(mat, slot):
        for k in (2, 1, 3, 0):
            x_send[mat, k] = total[slot, block_rows(2 * ((z + k) % 4) + 1 - x), :].astype(BF16)
            x_copies[mat, k] = send(x_send.at[mat, k], x_recv.at[mat, k], x_peer)

    def grads_on(mat, slot):
        for k in (2, 1, 3):
            done_sending(x_copies[mat, k])
            x_copies[mat, k].wait_recv()
            x_send[mat, k] = (
                total[slot, block_rows(2 * ((z + k) % 4) + x), :] + x_recv[mat, k].astype(F32)
            ).astype(BF16)
            z_copies[mat, k] = send(x_send.at[mat, k], z_recv.at[mat, k - 1], z_peers[k - 1])
        x_copies[mat, 0].wait_recv()
        shards_out[mat] = total[slot, own_block, :] + x_recv[mat, 0].astype(F32)

    def grads_in(mat):
        summed = shards_out[mat]
        for k in (1, 3, 2):
            z_copies[mat, k].wait_recv()
            summed += z_recv[mat, k - 1].astype(F32)
        shards_out[mat] = summed
        return jnp.sum(summed * summed)

    swap_mid_1 = to_swap(mid_1, keep, recv_mid, send_a, swapped_mid, 1)
    for first in (0, 256, 512):
        band_grad(
            0, first, 256,
            lambda i: back[i], lambda i, f=first: hidden[i, 0:SLOTS, f : f + 256],
        )
    grads_out(2, 0)
    for first in (0, 256, 512):
        band_grad(
            1, first, 256,
            lambda i: normed_two[i], lambda i, f=first: grad_upper[i, :, f : f + 256],
        )
    grads_out(1, 1)

    def middle_back(copy, item):
        grad_two = both(copy, send_a, swapped_mid, item)
        normal, inverse = norm_stats(middle[item])
        sums = (
            jnp.sum(grad_two * normal, axis=0, keepdims=True),
            jnp.sum(grad_two, axis=0, keepdims=True),
        )
        for row, part in zip((2, 3), sums):
            table_mine[row : row + 1, :] = part if item == 0 else table_mine[row : row + 1, :] + part
        pulled = load_half(back, item, c) + norm_back(
            grad_two, normal, inverse, norms[2:3, :]
        )
        grad_mid[item] = pulled
        middle_low[item, mine, :] = pulled.astype(BF16)
        return share_rows(middle_low, item)

    def attend_back(item, shared):
        for half in (c, 1 - c):
            rows = half_rows(half)
            if half is not c:
                shared.wait_recv()
            pulled = dot(middle_low[item, rows, :], weights[0, :, 576:768]).astype(BF16)
            for head in range(3):
                heads[item * 3 + head, rows, :] = pulled[:, head * HEAD_DIM : (head + 1) * HEAD_DIM]

        @pl.loop(0, 3)
        def _(head):
            at = item * 3 + head
            grad_key = None
            grad_value = None
            key_rows = keys[at]
            value_rows = values[at]
            for half, extent in ((1, KEYS), (0, NEAR_KEYS)):
                first = half * HALF
                rows = slice(first, first + HALF)
                pulled = heads[at, rows, :]
                weight = dot(pulled, value_rows[0:extent], NT)
                low = probs[at, rows, 0:extent]
                wide = low.astype(F32)
                weight = wide * weight
                moved = (weight - wide * jnp.sum(weight, axis=-1, keepdims=True)).astype(BF16)
                asked = queries[at, rows, :]
                part_key = dot(moved, asked, TN)
                part_value = dot(low, pulled, TN)
                queries[at, rows, :] = (
                    dot(moved, key_rows[0:extent]) * HEAD_DIM ** (-0.5)
                ).astype(BF16)
                if grad_key is None:
                    grad_key, grad_value = part_key, part_value
                else:
                    keys[at, 0:extent, :] = (grad_key[0:extent] + part_key).astype(BF16)
                    values[at, 0:extent, :] = (grad_value[0:extent] + part_value).astype(BF16)
                    keys[at, extent:KEYS, :] = grad_key[extent:KEYS].astype(BF16)
                    values[at, extent:KEYS, :] = grad_value[extent:KEYS].astype(BF16)

        for half in (0, 1):
            rows = slice(half * HALF, (half + 1) * HALF)
            grad_triple[item, rows, :] = jnp.concatenate(
                [
                    source[item * 3 + head, rows, :]
                    for source in (queries, keys, values)
                    for head in range(3)
                ],
                axis=1,
            )

    def first_terms(item):
        inward = weights[0, :, 0:576]
        send_a[item] = dot(grad_triple[item, half_rows(1 - c), :], inward, NT).astype(BF16)
        copy = to_core(recv_one, item, send_a)
        keep[item] = dot(grad_triple[item, mine, :], inward, NT)
        return copy

    ml_0 = middle_back(swap_mid_0, 0)
    done_sending(swap_mid_0)
    attend_back(0, ml_0)
    low_swap_0 = to_swap(low_0, keep_low, recv_low, send_b, swapped_low, 0)
    first_0 = first_terms(0)
    ml_1 = middle_back(swap_mid_1, 1)
    done_sending(swap_mid_1)
    first_swap_0 = to_swap(first_0, keep, recv_one, send_a, swapped_one, 0)
    grads_on(2, 0)
    attend_back(1, ml_1)
    first_1 = first_terms(1)
    for first, width in ((0, 256), (256, 256), (512, 64)):
        band_grad(
            0, first, width,
            lambda i: normed_one[i], lambda i, f=first, w=width: grad_triple[i, :, f : f + w],
        )
        if first == 0:
            first_swap_1 = to_swap(first_1, keep, recv_one, send_a, swapped_one, 1)
            low_swap_1 = to_swap(low_1, keep_low, recv_low, send_b, swapped_low, 1)
    band_grad(0, 576, 192, lambda i: middle_low[i], lambda i: context[i])
    grads_out(0, 0)
    grads_on(1, 1)

    stores = []

    def give(half_buffer, result, item):
        here = result.at[item, mine]
        store = pltpu.make_async_copy(half_buffer.at[item], here, local_sems.at[len(stores)])
        store.start()
        stores.append(store)
        return send(half_buffer.at[item], here, core_peer)

    def first_back(copy, item):
        grad_one = both(copy, send_a, swapped_one, item)
        normal, inverse = norm_stats(load_half(tokens, item, c))
        sums = (
            jnp.sum(grad_one * normal, axis=0, keepdims=True),
            jnp.sum(grad_one, axis=0, keepdims=True),
        )
        for row, part in zip((0, 1), sums):
            table_mine[row : row + 1, :] = part if item == 0 else table_mine[row : row + 1, :] + part
        grad_half[item] = (
            grad_mid[item] + norm_back(grad_one, normal, inverse, norms[0:1, :])
        ).astype(BF16)
        return give(grad_half, grad_h, item)

    def outcome(copy, item):
        out_half[item] = (middle[item] + both(copy, send_b, swapped_low, item)).astype(BF16)
        return give(out_half, output_h, item)

    out_0 = outcome(low_swap_0, 0)
    grads_on(0, 0)
    rows_0 = first_back(first_swap_0, 0)
    squares = grads_in(2)
    rows_1 = first_back(first_swap_1, 1)
    squares += grads_in(1)
    squares += grads_in(0)
    table_mine[4:8, :] = jnp.broadcast_to(squares, (4, table_mine.shape[1]))

    hops = [
        send(table_mine, table_recv.at[at], peer)
        for at, peer in enumerate((core_peer, y_peer, diagonal_peer))
    ]
    out_1 = outcome(low_swap_1, 1)
    for hop in hops:
        hop.wait_recv()
    done_sending(*hops)
    beside = table_mine[...] + table_recv[0]
    table_mine[0:4, :] = beside[0:4]
    table_mine[4:8, :] = beside[4:8] + (table_recv[1, 4:8, :] + table_recv[2, 4:8, :])
    hops = [send(table_mine, table_recv.at[3], x_peer)]
    for k in (1, 2, 3):
        hops.append(send(table_mine, table_recv.at[3 + k], z_peers[k - 1]))
        hops.append(send(table_mine, table_recv.at[6 + k], xz_peers[k - 1]))
    for hop in hops:
        hop.wait_recv()
    parts = [table_mine[...] + table_recv[3]] + [
        table_recv[3 + k] + table_recv[6 + k] for k in (1, 2, 3)
    ]
    ordered = None
    for level in range(4):
        piece = parts[0]
        for k in (1, 2, 3):
            piece = jnp.where((level + k) % 4 == z, parts[k], piece)
        ordered = piece if ordered is None else ordered + piece
    table_out[...] = ordered

    given = [rows_0, rows_1, out_0, out_1]
    for copy in given:
        copy.wait_recv()
    for store in stores:
        store.wait()
    for copy in list(pending):
        copy.wait_send()
    for copy in onward.values():
        copy.wait_send()
    for wanted, copy in later:

        @pl.when(wanted)
        def _():
            copy.wait_send()


def update_kernel(
    place, output_h, grad_h, shards_h, table_h, norms_h, *refs
):
    params_h, results, scratch = refs[:14], refs[14:32], refs[32:]
    output_to, grad_to, norm_out = results[:3]
    targets = results[3:]
    output_in, grad_in, output_v, grad_v, shards, table, norms = scratch[:7]
    params = scratch[7:21]
    updated = scratch[21:36]
    load_sems, store_sems = scratch[36:]
    loads = [
        pltpu.make_async_copy(source, target, load_sems.at[i])
        for i, (source, target) in enumerate(
            zip(
                (table_h, grad_h, output_h, shards_h, norms_h) + params_h,
                (table, grad_in, output_in, shards, norms) + params,
            )
        )
    ]
    for load in loads:
        load.start()
    stores = []

    def store(source, target):
        copy = pltpu.make_async_copy(source, target, store_sems.at[len(stores)])
        copy.start()
        stores.append(copy)

    loads[0].wait()
    sums = table[0:4, :]
    total = table[4:5, 0:1] + jnp.sum(
        jnp.sum(sums * sums, axis=1, keepdims=True), axis=0, keepdims=True
    )
    grad_norm = jnp.sqrt(total)
    norm_out[...] = grad_norm
    clip = jnp.minimum(1.0, CLIP_NORM / (grad_norm + 1e-06))

    loads[1].wait()
    for item in range(2):
        grad_v[item] = grad_in[item, 0:SLOTS, :].astype(F32)
        store(grad_v.at[item], grad_to.at[item])
    loads[2].wait()
    output_v[...] = output_in[:, 0:SLOTS, :]
    store(output_v, output_to)
    loads[3].wait()
    loads[4].wait()

    def update(index, gradients, rate, decay, master_at=None):
        m_at, v_at = 4 + index, 9 + index
        for at in (m_at, v_at) if index == 4 else (index, m_at, v_at):
            loads[5 + at].wait()
        for part, gradient in enumerate(gradients):
            at = (lambda ref: ref.at[part]) if index == 0 else (lambda ref: ref)
            master = master_at if index == 4 else at(params[index])[...]
            values = adam_update(
                master, at(params[m_at])[...], at(params[v_at])[...], gradient, clip, rate, decay
            )
            for which, value in enumerate(values):
                at(updated[3 * index + which])[...] = value
        for which in range(3):
            store(updated[3 * index + which], targets[3 * index + which])

    part = params[0].shape[2]
    update(3, [shards[2]], RATE_DOWNWARD, WEIGHT_DECAY)
    update(2, [shards[1]], RATE_UPWARD, WEIGHT_DECAY)
    update(
        0, [shards[0, :, i * part : (i + 1) * part] for i in range(3)], RATE_INWARD, WEIGHT_DECAY
    )
    update(1, [shards[0, :, 3 * part :].T], RATE_OUTWARD, WEIGHT_DECAY)
    span = params[8].shape[1]
    own_sums = sums[:, 0:span]
    own_norms = norms[:, 0:span]
    for index in range(1, 8):
        here = place[0] == index
        columns = slice(index * span, (index + 1) * span)
        own_sums = jnp.where(here, sums[:, columns], own_sums)
        own_norms = jnp.where(here, norms[:, columns], own_norms)
    update(4, [own_sums], RATE_NORMS, 0.0, own_norms)
    for copy in stores:
        copy.wait()


def fused_body(
    tokens, cotangent, step_counts, wrist_flags,
    inward_weight, outward_weight, upward_weight, downward_weight, norm_table,
    momentum_inward, momentum_outward, momentum_upward, momentum_downward, momentum_norms,
    variance_inward, variance_outward, variance_upward, variance_downward, variance_norms,
):
    width = norm_table.shape[1]
    block = upward_weight.shape[0]
    any_spec = pl.BlockSpec(memory_space=pl.ANY)
    vmem = pl.BlockSpec(memory_space=pltpu.VMEM)
    smem = pl.BlockSpec(memory_space=pltpu.SMEM)
    rows = pltpu.VMEM((2, ROWS, width), BF16)
    halves = pltpu.VMEM((2, HALF, width), BF16)
    keep = pltpu.VMEM((2, HALF, width), F32)
    output, grads, shards, table = pl.pallas_call(
        fused_kernel,
        out_shape=(
            jax.ShapeDtypeStruct((2, ROWS, width), BF16),
            jax.ShapeDtypeStruct((2, ROWS, width), BF16),
            jax.ShapeDtypeStruct((3, block, width), F32),
            jax.ShapeDtypeStruct((8, width), F32),
        ),
        in_specs=[smem, smem, any_spec, any_spec, any_spec, any_spec, any_spec, any_spec, vmem],
        out_specs=(any_spec, any_spec, vmem, vmem),
        scratch_shapes=[
            pltpu.VMEM((3, width, width), BF16),
            pltpu.VMEM((2, SLOTS, width), BF16),
            pltpu.VMEM((2, SLOTS, width), BF16),
            rows,
            pltpu.VMEM((6, ROWS, HEAD_DIM), BF16),
            pltpu.VMEM((6, KEYS, HEAD_DIM), BF16),
            pltpu.VMEM((6, KEYS, HEAD_DIM), BF16),
            pltpu.VMEM((6, ROWS, KEYS), BF16),
            pltpu.VMEM((6, ROWS, HEAD_DIM), BF16),
            pltpu.VMEM((2, ROWS, 192), BF16),
            keep,
            rows,
            rows,
            rows,
            rows,
            halves,
            halves,
            keep,
            keep,
            halves,
            halves,
            halves,
            halves,
            halves,
            halves,
            halves,
            halves,
            keep,
            pltpu.VMEM((2, ROWS, 576), BF16),
            pltpu.VMEM((2, width, width), F32),
            pltpu.VMEM((3, 4, block, width), BF16),
            pltpu.VMEM((3, 4, block, width), BF16),
            pltpu.VMEM((3, 3, block, width), BF16),
            pltpu.VMEM((8, width), F32),
            pltpu.VMEM((10, 8, width), F32),
            pltpu.VMEM(inward_weight.shape, F32),
            pltpu.VMEM(outward_weight.shape, F32),
            pltpu.VMEM(upward_weight.shape, F32),
            pltpu.VMEM(upward_weight.shape, F32),
            pltpu.SemaphoreType.DMA((N_REMOTE,)),
            pltpu.SemaphoreType.DMA((N_REMOTE,)),
            pltpu.SemaphoreType.DMA((10,)),
        ],
        compiler_params=pltpu.CompilerParams(
            collective_id=0, has_side_effects=True, vmem_limit_bytes=VMEM_BYTES
        ),
        name="block_step",
    )(
        step_counts,
        wrist_flags,
        inward_weight,
        outward_weight,
        upward_weight,
        downward_weight.T,
        tokens,
        cotangent,
        norm_table,
    )
    place = jnp.reshape(lax.axis_index("dp"), (1,)).astype(jnp.int32)
    params = (
        inward_weight, outward_weight, upward_weight, downward_weight.T,
        momentum_inward, momentum_outward, momentum_upward, momentum_downward.T, momentum_norms,
        variance_inward, variance_outward, variance_upward, variance_downward.T, variance_norms,
    )
    shapes = [param.shape for param in params]
    updates = [shape for shape in shapes[:4] + shapes[8:9] for _ in range(3)]
    padded = pltpu.VMEM((2, ROWS, width), BF16)
    results = pl.pallas_call(
        update_kernel,
        out_shape=(
            jax.ShapeDtypeStruct((2, SLOTS, width), BF16),
            jax.ShapeDtypeStruct((2, SLOTS, width), F32),
            jax.ShapeDtypeStruct((1, 1), F32),
            *[jax.ShapeDtypeStruct(shape, F32) for shape in updates],
        ),
        in_specs=[smem] + [any_spec] * 19,
        out_specs=(any_spec, any_spec, vmem) + (any_spec,) * 15,
        scratch_shapes=[
            padded,
            padded,
            pltpu.VMEM((2, SLOTS, width), BF16),
            pltpu.VMEM((2, SLOTS, width), F32),
            pltpu.VMEM((3, block, width), F32),
            pltpu.VMEM((8, width), F32),
            pltpu.VMEM((4, width), F32),
            *[pltpu.VMEM(shape, F32) for shape in shapes],
            *[pltpu.VMEM(shape, F32) for shape in updates],
            pltpu.SemaphoreType.DMA((19,)),
            pltpu.SemaphoreType.DMA((18,)),
        ],
        compiler_params=pltpu.CompilerParams(vmem_limit_bytes=VMEM_BYTES),
        name="update_step",
    )(place, output, grads, shards, table, norm_table, *params)
    updated = list(results[3:])
    for index in (9, 10, 11):
        updated[index] = updated[index].T
    return (results[0], results[1], results[2][0, 0], *updated)


def solution(mesh):
    fits = mesh.shape["dp"] == 8 and mesh.shape["mp"] == 4
    return whole_program(mesh, fused_body if fits else body)
```

```python
import jax
import jax.numpy as jnp
from jax import lax
from jax.experimental import pallas as pl
from jax.experimental.pallas import tpu as pltpu
from jax.sharding import PartitionSpec as P

HEAD_DIM = 64
TASK = 16
PRIMARY = 256
WRIST = 64
READOUT = 4
SLOTS = 664
MB = 2
STEP = 10


NORM_EPSILON = 1e-06
CLIP_NORM = 1.0
BETA_ONE = 0.9
BETA_TWO = 0.999
ADAM_EPSILON = 1e-08
WEIGHT_DECAY = 0.1
NEGATIVE = -1e30
RATE_INWARD = 0.05
RATE_OUTWARD = 0.15
RATE_UPWARD = 0.04
RATE_DOWNWARD = 0.02
RATE_NORMS = 0.5


def slot_mask(live_steps, has_wrist):
    position = jnp.arange(SLOTS, dtype=jnp.int32)
    relative = position - TASK
    period = PRIMARY + WRIST + READOUT
    is_task = relative < 0
    forward_pos = jnp.maximum(relative, 0)
    stepno = forward_pos // period
    offset = forward_pos % period
    not_task = jnp.logical_not(is_task)
    is_read = jnp.logical_and(not_task, offset >= PRIMARY + WRIST)
    is_obs = jnp.logical_and(not_task, jnp.logical_not(is_read))
    is_wrist = jnp.logical_and(is_obs, offset >= PRIMARY)
    present = jnp.logical_or(
        is_task,
        jnp.logical_and(
            stepno < live_steps, jnp.logical_or(jnp.logical_not(is_wrist), has_wrist == 1)
        ),
    )
    see_obs = is_obs[None, :] & not_task[:, None] & (stepno[None, :] <= stepno[:, None])
    see_read = is_read[None, :] & is_read[:, None] & (stepno[None, :] == stepno[:, None])
    return present[None, :] & (is_task[None, :] | see_obs | see_read)


def layer_stats(values):
    centre = values - jnp.mean(values, axis=-1, keepdims=True)
    inverse = lax.rsqrt(jnp.mean(centre * centre, axis=-1, keepdims=True) + NORM_EPSILON)
    return (centre * inverse, inverse)


def layer_back(grad_result, normal, inverse, gain_row):
    scaled = grad_result * gain_row
    return inverse * (
        scaled
        - jnp.mean(scaled, axis=-1, keepdims=True)
        - normal * jnp.mean(scaled * normal, axis=-1, keepdims=True)
    )


def gelu_tanh(values):
    return (
        0.5
        * values
        * (1.0 + jnp.tanh(0.7978845608028654 * (values + 0.044715 * values * values * values)))
    )


def attention_scores(queries, key_heads, allowed, score_scale):
    dotted = (
        jnp.einsum("nqhd,nkhd->nhqk", queries, key_heads, preferred_element_type=jnp.float32)
        * score_scale
    )
    return jnp.where(allowed, dotted, NEGATIVE)


def adam_update(master, momentum, variance, gradient, clip_scale, step_rate, decay_rate):
    clipped = gradient * clip_scale
    moment_one = BETA_ONE * momentum + (1.0 - BETA_ONE) * clipped
    moment_two = BETA_TWO * variance + (1.0 - BETA_TWO) * clipped * clipped
    first_hat = moment_one / (1.0 - BETA_ONE**STEP)
    second_hat = moment_two / (1.0 - BETA_TWO**STEP)
    updated = master - step_rate * (
        first_hat / (jnp.sqrt(second_hat) + ADAM_EPSILON) + decay_rate * master
    )
    return (moment_one, moment_two, updated)


def body(
    tokens,
    cotangent,
    step_counts,
    wrist_flags,
    inward_weight,
    outward_weight,
    upward_weight,
    downward_weight,
    norm_table,
    momentum_inward,
    momentum_outward,
    momentum_upward,
    momentum_downward,
    momentum_norms,
    variance_inward,
    variance_outward,
    variance_upward,
    variance_downward,
    variance_norms,
):
    full_inward, full_outward, full_upward, full_downward = (
        lax.all_gather(inward_weight.astype(jnp.bfloat16), "dp", axis=1, tiled=True),
        lax.all_gather(outward_weight.astype(jnp.bfloat16), "dp", axis=1, tiled=True),
        lax.all_gather(upward_weight.astype(jnp.bfloat16), "dp", axis=0, tiled=True),
        lax.all_gather(downward_weight.astype(jnp.bfloat16), "dp", axis=1, tiled=True),
    )
    model_width = norm_table.shape[1]
    local_heads = full_inward.shape[2] // HEAD_DIM
    score_scale = HEAD_DIM ** (-0.5)
    per_batch = tokens.shape[0] // MB
    row_count = per_batch * SLOTS
    share_rows = row_count // lax.axis_size("mp")
    share_start = lax.axis_index("mp") * share_rows
    results = []
    input_grads = []
    local_sums = None
    for batch_index in range(MB):
        start_item = batch_index * per_batch
        block_tokens = (
            tokens[start_item : start_item + per_batch]
            .astype(jnp.float32)
            .reshape(row_count, model_width)
        )
        block_back = (
            cotangent[start_item : start_item + per_batch]
            .astype(jnp.float32)
            .reshape(row_count, model_width)
        )
        allowed = jax.vmap(slot_mask)(
            step_counts[start_item : start_item + per_batch],
            wrist_flags[start_item : start_item + per_batch],
        )[:, None]
        normal_one, inverse_one = layer_stats(block_tokens)
        normed_one = (normal_one * norm_table[0] + norm_table[1]).astype(jnp.bfloat16)
        projected = jnp.einsum(
            "rd,cdm->crm", normed_one, full_inward, preferred_element_type=jnp.float32
        ).astype(jnp.bfloat16)
        triple = projected.reshape(3, per_batch, SLOTS, local_heads, HEAD_DIM)
        queries = triple[0]
        key_heads = triple[1]
        value_heads = triple[2]
        scores = attention_scores(queries, key_heads, allowed, score_scale)
        highest = jnp.max(scores, axis=-1, keepdims=True)
        log_total = highest + jnp.log(jnp.sum(jnp.exp(scores - highest), axis=-1, keepdims=True))
        attention_low = jnp.exp(scores - log_total).astype(jnp.bfloat16)
        context = (
            jnp.einsum(
                "nhqk,nkhd->nqhd", attention_low, value_heads, preferred_element_type=jnp.float32
            )
            .astype(jnp.bfloat16)
            .reshape(row_count, -1)
        )
        attn_terms = jnp.dot(context, full_outward, preferred_element_type=jnp.float32)
        tokens_share = lax.dynamic_slice_in_dim(block_tokens, share_start, share_rows, 0)
        back_share = lax.dynamic_slice_in_dim(block_back, share_start, share_rows, 0)
        middle_share = tokens_share + lax.psum_scatter(
            attn_terms, "mp", scatter_dimension=0, tiled=True
        )
        normal_two, inverse_two = layer_stats(middle_share)
        normed_share = (normal_two * norm_table[2] + norm_table[3]).astype(jnp.bfloat16)
        normed_two = lax.all_gather(normed_share, "mp", axis=0, tiled=True)
        upper_pre = jnp.dot(normed_two, full_upward, preferred_element_type=jnp.float32)
        hidden = gelu_tanh(upper_pre).astype(jnp.bfloat16)
        lowered_share = lax.psum_scatter(
            jnp.dot(hidden, full_downward, preferred_element_type=jnp.float32).astype(jnp.bfloat16),
            "mp",
            scatter_dimension=0,
            tiled=True,
        ).astype(jnp.float32)
        output_share = (middle_share + lowered_share).astype(jnp.bfloat16)
        back_rows = block_back.astype(jnp.bfloat16)
        grad_down = jnp.einsum("rf,rd->fd", hidden, back_rows, preferred_element_type=jnp.float32)
        grad_hidden = jnp.einsum(
            "rd,fd->rf", back_rows, full_downward, preferred_element_type=jnp.float32
        )
        upper_pull = jax.vjp(gelu_tanh, upper_pre)[1]
        grad_upper = upper_pull(grad_hidden)[0].astype(jnp.bfloat16)
        grad_up = jnp.einsum(
            "rd,rf->df", normed_two, grad_upper, preferred_element_type=jnp.float32
        )
        normed_terms = jnp.einsum(
            "rf,df->rd", grad_upper, full_upward, preferred_element_type=jnp.float32
        )
        grad_normed_two = lax.psum_scatter(normed_terms, "mp", scatter_dimension=0, tiled=True)
        gain_two = jnp.sum(grad_normed_two * normal_two, axis=0)
        shift_two = jnp.sum(grad_normed_two, axis=0)
        grad_middle_share = back_share + layer_back(
            grad_normed_two, normal_two, inverse_two, norm_table[2]
        )
        middle_low, output_rows = (
            lax.all_gather(grad_middle_share.astype(jnp.bfloat16), "mp", axis=0, tiled=True),
            lax.all_gather(output_share, "mp", axis=0, tiled=True),
        )
        results.append(output_rows.reshape(per_batch, SLOTS, model_width))
        grad_out = jnp.einsum("rm,rd->md", context, middle_low, preferred_element_type=jnp.float32)
        grad_context = (
            jnp.einsum("rd,md->rm", middle_low, full_outward, preferred_element_type=jnp.float32)
            .astype(jnp.bfloat16)
            .reshape(per_batch, SLOTS, local_heads, HEAD_DIM)
        )
        scores_again = attention_scores(queries, key_heads, allowed, score_scale)
        attention_full = jnp.exp(scores_again - log_total)
        attention_again = attention_full.astype(jnp.bfloat16)
        grad_values = jnp.einsum(
            "nhqk,nqhd->nkhd", attention_again, grad_context, preferred_element_type=jnp.float32
        ).astype(jnp.bfloat16)
        grad_weights = jnp.einsum(
            "nqhd,nkhd->nhqk", grad_context, value_heads, preferred_element_type=jnp.float32
        )
        grad_scores = (
            attention_full
            * (grad_weights - jnp.sum(grad_weights * attention_full, axis=-1, keepdims=True))
        ).astype(jnp.bfloat16)
        grad_queries = (
            jnp.einsum(
                "nhqk,nkhd->nqhd", grad_scores, key_heads, preferred_element_type=jnp.float32
            )
            * score_scale
        ).astype(jnp.bfloat16)
        grad_keys = (
            jnp.einsum("nhqk,nqhd->nkhd", grad_scores, queries, preferred_element_type=jnp.float32)
            * score_scale
        ).astype(jnp.bfloat16)
        grad_triple = jnp.stack([grad_queries, grad_keys, grad_values]).reshape(3, row_count, -1)
        grad_in = jnp.einsum(
            "rd,crm->cdm", normed_one, grad_triple, preferred_element_type=jnp.float32
        )
        first_terms = jnp.einsum(
            "crm,cdm->rd", grad_triple, full_inward, preferred_element_type=jnp.float32
        )
        grad_normed_one = lax.psum_scatter(first_terms, "mp", scatter_dimension=0, tiled=True)
        normal_share = lax.dynamic_slice_in_dim(normal_one, share_start, share_rows, 0)
        inverse_share = lax.dynamic_slice_in_dim(inverse_one, share_start, share_rows, 0)
        gain_one = jnp.sum(grad_normed_one * normal_share, axis=0)
        shift_one = jnp.sum(grad_normed_one, axis=0)
        tokens_grad_share = grad_middle_share + layer_back(
            grad_normed_one, normal_share, inverse_share, norm_table[0]
        )
        table_terms = jnp.stack([gain_one, shift_one, gain_two, shift_two])[None]
        grad_tokens, gathered_tables = (
            lax.all_gather(tokens_grad_share, "mp", axis=0, tiled=True),
            lax.all_gather(table_terms, "mp", axis=0, tiled=True),
        )
        grad_table = jnp.sum(gathered_tables, axis=0)
        input_grads.append(grad_tokens.reshape(per_batch, SLOTS, model_width))
        batch_grads = (grad_in, grad_out, grad_up, grad_down, grad_table)
        if local_sums is None:
            local_sums = batch_grads
        else:
            local_sums = tuple((former + latter for former, latter in zip(local_sums, batch_grads)))
    shards = (
        lax.psum_scatter(local_sums[0], "dp", scatter_dimension=1, tiled=True),
        lax.psum_scatter(local_sums[1], "dp", scatter_dimension=1, tiled=True),
        lax.psum_scatter(local_sums[2], "dp", scatter_dimension=0, tiled=True),
        lax.psum_scatter(local_sums[3], "dp", scatter_dimension=1, tiled=True),
        lax.psum_scatter(local_sums[4], "dp", scatter_dimension=1, tiled=True),
    )
    mp_count = lax.axis_size("mp")
    squares = (
        sum((jnp.sum(piece * piece) for piece in shards[:4]))
        + jnp.sum(shards[4] * shards[4]) / mp_count
    )
    grad_norm = jnp.sqrt(lax.psum(squares, ("dp", "mp")))
    clip_scale = jnp.minimum(1.0, CLIP_NORM / (grad_norm + 1e-06))
    shard_width = shards[4].shape[1]
    own_table = lax.dynamic_slice_in_dim(
        norm_table, lax.axis_index("dp") * shard_width, shard_width, 1
    )
    inward_new = adam_update(
        inward_weight,
        momentum_inward,
        variance_inward,
        shards[0],
        clip_scale,
        RATE_INWARD,
        WEIGHT_DECAY,
    )
    outward_new = adam_update(
        outward_weight,
        momentum_outward,
        variance_outward,
        shards[1],
        clip_scale,
        RATE_OUTWARD,
        WEIGHT_DECAY,
    )
    upward_new = adam_update(
        upward_weight,
        momentum_upward,
        variance_upward,
        shards[2],
        clip_scale,
        RATE_UPWARD,
        WEIGHT_DECAY,
    )
    downward_new = adam_update(
        downward_weight,
        momentum_downward,
        variance_downward,
        shards[3],
        clip_scale,
        RATE_DOWNWARD,
        WEIGHT_DECAY,
    )
    norms_new = adam_update(
        own_table, momentum_norms, variance_norms, shards[4], clip_scale, RATE_NORMS, 0.0
    )
    output = jnp.concatenate(results, axis=0)
    input_grad = jnp.concatenate(input_grads, axis=0)
    return (
        output,
        input_grad,
        grad_norm,
        inward_new[0],
        inward_new[1],
        inward_new[2],
        outward_new[0],
        outward_new[1],
        outward_new[2],
        upward_new[0],
        upward_new[1],
        upward_new[2],
        downward_new[0],
        downward_new[1],
        downward_new[2],
        norms_new[0],
        norms_new[1],
        norms_new[2],
    )


def whole_program(mesh, function):
    placed = (
        P("dp", None, None),
        P("dp", None, None),
        P("dp"),
        P("dp"),
        P(None, "dp", "mp"),
        P("mp", "dp"),
        P("dp", "mp"),
        P("mp", "dp"),
        P(),
        P(None, "dp", "mp"),
        P("mp", "dp"),
        P("dp", "mp"),
        P("mp", "dp"),
        P(None, "dp"),
        P(None, "dp", "mp"),
        P("mp", "dp"),
        P("dp", "mp"),
        P("mp", "dp"),
        P(None, "dp"),
    )
    return jax.shard_map(
        function,
        mesh=mesh,
        in_specs=placed,
        out_specs=(
            P("dp", None, None),
            P("dp", None, None),
            P(),
            P(None, "dp", "mp"),
            P(None, "dp", "mp"),
            P(None, "dp", "mp"),
            P("mp", "dp"),
            P("mp", "dp"),
            P("mp", "dp"),
            P("dp", "mp"),
            P("dp", "mp"),
            P("dp", "mp"),
            P("mp", "dp"),
            P("mp", "dp"),
            P("mp", "dp"),
            P(None, "dp"),
            P(None, "dp"),
            P(None, "dp"),
        ),
        check_vma=False,
    )


NN = (((1,), (0,)), ((), ()))
NT = (((1,), (1,)), ((), ()))
TN = (((0,), (0,)), ((), ()))
MESH = pl.DeviceIdType.MESH
F32 = jnp.float32
BF16 = jnp.bfloat16
ROWS = 672
HALF = ROWS // 2
KEYS = 768
NEAR_KEYS = 384
FIRST_COLUMNS = 640
PERIOD = PRIMARY + WRIST + READOUT


def dot(left, right, dims=NN):
    return lax.dot_general(left, right, dims, preferred_element_type=F32)


def gelu_both(values):
    square = values * values
    inner = 0.7978845608028654 * values * (1.0 + 0.044715 * square)
    bend = jnp.tanh(inner)
    half_up = 0.5 + 0.5 * bend
    slope = half_up + 0.5 * values * (1.0 - bend * bend) * (
        0.7978845608028654 * (1.0 + 0.134145 * square)
    )
    return values * half_up, slope


def key_bits(live_steps, has_wrist):
    place = lax.broadcasted_iota(jnp.int32, (1, KEYS), 1)
    relative = place - TASK
    is_task = relative < 0
    later = relative >= PERIOD
    offset = jnp.where(later, relative - PERIOD, relative)
    is_read = offset >= PRIMARY + WRIST
    is_wrist = jnp.logical_and(offset >= PRIMARY, offset < PRIMARY + WRIST)
    step_of = jnp.where(later, 1, 0)
    alive = jnp.logical_and(
        step_of < live_steps, jnp.logical_or(jnp.logical_not(is_wrist), has_wrist == 1)
    )
    bits = jnp.where(is_read, jnp.where(later, 16, 8), jnp.where(later, 4, 2))
    bits = jnp.where(alive, bits, 0)
    bits = jnp.where(is_task, 1, bits)
    return jnp.where(place < SLOTS, bits, 0)


def query_bits(first):
    place = lax.broadcasted_iota(jnp.int32, (HALF, 1), 0) + first
    relative = place - TASK
    is_task = relative < 0
    later = relative >= PERIOD
    offset = jnp.where(later, relative - PERIOD, relative)
    is_read = offset >= PRIMARY + WRIST
    bits = jnp.where(later, 7, 3) + jnp.where(is_read, jnp.where(later, 16, 8), 0)
    return jnp.where(is_task, 1, bits)


N_REMOTE = 128
VMEM_BYTES = 64 * 1024 * 1024 - 65536


def fused_kernel(
    steps, flags, inward_h, outward_h, upward_h, downward_h, tokens_h, back_h, norms,
    output_h, grad_h, shards_out, table_out,
    weights, tokens, back, normed_one, queries, keys, values, probs, heads, context,
    middle, normed_two, hidden, grad_upper, middle_low, out_half, grad_half,
    keep, keep_low, send_a, send_b,
    recv_one, recv_mid, recv_low, swapped_one, swapped_mid, swapped_low,
    grad_mid, grad_triple, total, x_send, x_recv, z_recv,
    table_mine, early_mine, early_recv, late_mine, late_recv, inward_f, outward_f, upward_f, downward_f,
    send_sems, recv_sems, local_sems,
):
    dp = lax.axis_index("dp")
    mp = lax.axis_index("mp")
    z, x = dp // 2, dp % 2
    y, c = mp // 2, mp % 2
    core_peer = (dp, y * 2 + 1 - c)
    y_peer = (dp, (1 - y) * 2 + c)
    x_peer = (z * 2 + 1 - x, mp)
    z_peers = [(((z + k) % 4) * 2 + x, mp) for k in (1, 2, 3)]
    xz_peers = [(((z + k) % 4) * 2 + 1 - x, mp) for k in (1, 2, 3)]
    diagonal_peer = (dp, (1 - y) * 2 + 1 - c)
    all_peers = [core_peer, y_peer, x_peer, diagonal_peer] + z_peers + xz_peers
    block = weights.shape[1] // 8
    used = []
    pending = []

    def describe(index, src, dst, peer):
        return pltpu.make_async_remote_copy(
            src_ref=src, dst_ref=dst, send_sem=send_sems.at[index], recv_sem=recv_sems.at[index],
            device_id=peer, device_id_type=MESH,
        )

    def send(src, dst, peer):
        used.append(0)
        copy = describe(len(used) - 1, src, dst, peer)
        copy.start()
        pending.append(copy)
        return copy

    def done_sending(*copies):
        for copy in copies:
            copy.wait_send()
            pending[:] = [other for other in pending if other is not copy]

    def block_rows(index):
        return pl.ds(pl.multiple_of(index * block, 32), block)

    def half_rows(half):
        return pl.ds(pl.multiple_of(half * HALF, 16), HALF)

    mine = half_rows(c)
    own_block = block_rows(dp)
    loads = [
        pltpu.make_async_copy(source, target, local_sems.at[4 + i])
        for i, (source, target) in enumerate(
            (
                (inward_h, inward_f),
                (outward_h, outward_f),
                (upward_h, upward_f),
                (downward_h, downward_f),
                (tokens_h, tokens),
                (back_h, back),
            )
        )
    ]
    for load in loads:
        load.start()

    barrier = pltpu.get_barrier_semaphore()
    for peer in all_peers:
        pl.semaphore_signal(barrier, inc=1, device_id=peer, device_id_type=MESH)
    loads[0].wait()
    loads[1].wait()
    weights[0, own_block, :] = jnp.concatenate(
        [inward_f[0], inward_f[1], inward_f[2], outward_f[...].T], axis=1
    ).astype(BF16)
    pl.semaphore_wait(barrier, len(all_peers))

    later = []
    z_index = {}
    for mat in (0,):
        for sign in (1, -1):
            for j in (1, 2, 3):
                z_index[mat, sign, j] = len(used)
                used.append(0)
                z_index[mat, sign, j, "x"] = len(used)
                used.append(0)
    own_x = {}

    def z_send_block(mat, sign, j):
        origin = z - sign * (j - 1)
        rows = weights.at[mat, block_rows(origin * 2 + x), 0:FIRST_COLUMNS]
        there = ((z + sign) * 2 + x, mp)
        copy = describe(z_index[mat, sign, j], rows, rows, there)
        wanted = jnp.logical_and(
            jnp.logical_and(origin >= 0, origin <= 3), z < 3 if sign == 1 else z > 0
        )

        @pl.when(wanted)
        def _():
            copy.start()

        later.append((wanted, copy))

    straight = {}
    onward = {}

    def part(mat, rows):
        if mat == 3:
            return weights.at[0, rows, FIRST_COLUMNS:]
        return weights.at[mat, rows, 0:FIRST_COLUMNS] if mat == 0 else weights.at[mat, rows]

    for mat in (3, 1, 2):
        for k in (1, 3, 2):
            rows = part(mat, block_rows(((z + 4 - k) % 4) * 2 + x))
            used.append(0)
            onward[mat, k] = describe(len(used) - 1, rows, rows, x_peer)

    def straight_out(mat):
        rows = part(mat, own_block)
        for k in (1, 3, 2):
            straight[mat, k] = send(rows, rows, z_peers[k - 1])

    def pass_x(mat, *places):
        for k in places:
            straight[mat, k].wait_recv()
            onward[mat, k].start()

    def straight_in(mat):
        own_x[mat].wait_recv()
        for k in (1, 3, 2):
            onward[mat, k].wait_recv()

    def z_sends_out(mat):
        for sign in (1, -1):
            z_send_block(mat, sign, 1)

    def own_out(mat):
        rows = part(mat, own_block)
        own_x[mat] = send(rows, rows, x_peer)

    def arrives(sign, j):
        return z >= j if sign == 1 else z <= 3 - j

    def block_at(mat, sign, j):
        return weights.at[mat, block_rows((z - sign * j) * 2 + x), 0:FIRST_COLUMNS]

    def weights_on(mat, j):
        for sign in (1, -1):
            here = arrives(sign, j)
            rows = block_at(mat, sign, j)
            onward = describe(z_index[mat, sign, j, "x"], rows, rows, x_peer)

            @pl.when(here)
            def _():
                describe(z_index[mat, sign, j], rows, rows, x_peer).wait_recv()

            if j < 3:
                z_send_block(mat, sign, j + 1)

            @pl.when(here)
            def _():
                onward.start()

            later.append((here, onward))

    def weights_in(mat):
        own_x[mat].wait_recv()
        for j in (1, 2, 3):
            for sign in (1, -1):
                rows = block_at(mat, sign, j)

                @pl.when(arrives(sign, j))
                def _():
                    describe(z_index[mat, sign, j, "x"], rows, rows, x_peer).wait_recv()

    def norm_stats(rows):
        centre = rows - jnp.mean(rows, axis=-1, keepdims=True)
        inverse = lax.rsqrt(jnp.mean(centre * centre, axis=-1, keepdims=True) + NORM_EPSILON)
        return centre * inverse, inverse

    def norm_back(grad_result, normal, inverse, gain_row):
        scaled = grad_result * gain_row
        return inverse * (
            scaled
            - jnp.mean(scaled, axis=-1, keepdims=True)
            - normal * jnp.mean(scaled * normal, axis=-1, keepdims=True)
        )

    def load_half(source, item, half):
        body = source[item, pl.ds(pl.multiple_of(half * HALF, 16), SLOTS - HALF), :].astype(F32)
        tail = source[item, SLOTS - HALF : HALF, :].astype(F32)
        return jnp.concatenate([body, jnp.where(half == 0, tail, 0.0)], axis=0)

    def first_norm(item, low, high):
        @pl.loop(low, min(high, 5))
        def _(index):
            rows = pl.ds(pl.multiple_of(index * 112, 16), 112)
            normal, _ = norm_stats(tokens[item, rows, :].astype(F32))
            normed_one[item, rows, :] = (normal * norms[0:1, :] + norms[1:2, :]).astype(BF16)

        if high == 6:
            normal, _ = norm_stats(tokens[item, 560:SLOTS, :].astype(F32))
            normed = normal * norms[0:1, :] + norms[1:2, :]
            none = jnp.zeros((ROWS - SLOTS, normed.shape[1]), F32)
            normed_one[item, 560:ROWS, :] = jnp.concatenate([normed, none], axis=0).astype(BF16)

    z_sends_out(0)
    own_out(0)
    loads[2].wait()
    loads[3].wait()
    weights[1, own_block, :] = upward_f[...].astype(BF16)
    weights[2, own_block, :] = downward_f[...].astype(BF16)
    loads[4].wait()
    first_norm(0, 0, 4)
    weights_on(0, 1)
    first_norm(0, 4, 6)
    first_norm(1, 0, 2)
    weights_on(0, 2)
    for mat in (3, 1, 2):
        straight_out(mat)
    first_norm(1, 2, 6)
    weights_on(0, 3)
    for mat in (3, 1, 2):
        own_out(mat)
    loads[5].wait()
    zero_rows = jnp.zeros((KEYS - ROWS, HEAD_DIM), BF16)
    for i in range(6):
        keys[i, ROWS:KEYS, :] = zero_rows
        values[i, ROWS:KEYS, :] = zero_rows
    weights_in(0)

    def project(item):
        @pl.loop(0, 2)
        def _(half):
            rows = half_rows(half)
            joined = dot(normed_one[item, rows, :], weights[0, :, 0:576])
            for head in range(3):
                low = head * HEAD_DIM
                queries[item * 3 + head, rows, :] = (
                    joined[:, low : low + HEAD_DIM].astype(BF16) * HEAD_DIM ** (-0.5)
                ).astype(BF16)
                low += 192
                keys[item * 3 + head, rows, :] = joined[:, low : low + HEAD_DIM].astype(BF16)
                low += 192
                values[item * 3 + head, rows, :] = joined[:, low : low + HEAD_DIM].astype(BF16)

    def attend(item):
        bits = key_bits(steps[item], flags[item])

        @pl.loop(0, 3)
        def _(head):
            at = item * 3 + head
            for half, extent in ((0, NEAR_KEYS), (1, KEYS)):
                first = half * HALF
                scores = dot(queries[at, first : first + HALF, :], keys[at, 0:extent, :], NT)
                seen = jnp.bitwise_and(bits[:, 0:extent], query_bits(first)) != 0
                scores = jnp.where(seen, scores, NEGATIVE)
                spread = jnp.exp(scores - jnp.max(scores, axis=-1, keepdims=True))
                scale = 1.0 / jnp.sum(spread, axis=-1, keepdims=True)
                low = (spread * scale).astype(BF16)
                probs[at, first : first + HALF, 0:extent] = low
                heads[at, first : first + HALF, :] = dot(low, values[at, 0:extent, :]).astype(BF16)

    def to_core(kind, item, source):
        return send(source.at[item], kind.at[item], core_peer)

    def to_swap(copy, kept, received, staged, swapped, item):
        done_sending(copy)
        copy.wait_recv()
        staged[item] = (kept[item] + received[item].astype(F32)).astype(BF16)
        return send(staged.at[item], swapped.at[item], y_peer)

    def both(copy, staged, swapped, item):
        copy.wait_recv()
        return staged[item].astype(F32) + swapped[item].astype(F32)

    def attention_out(item):
        for half in (0, 1):
            rows = slice(half * HALF, (half + 1) * HALF)
            context[item, rows, :] = jnp.concatenate(
                [heads[item * 3 + head, rows, :] for head in range(3)], axis=1
            )
        outward = weights[0, :, 576:768]
        send_a[item] = dot(context[item, half_rows(1 - c), :], outward, NT).astype(BF16)
        copy = to_core(recv_one, item, send_a)
        keep[item] = dot(context[item, mine, :], outward, NT)
        return copy

    project(0)
    pass_x(3, 1, 3, 2)
    attend(0)
    straight_in(3)
    attn_0 = attention_out(0)
    project(1)
    swap_0 = to_swap(attn_0, keep, recv_one, send_a, swapped_one, 0)
    pass_x(1, 1, 3)
    attend(1)
    pass_x(1, 2)
    attn_1 = attention_out(1)
    swap_1 = to_swap(attn_1, keep, recv_one, send_a, swapped_one, 1)
    pass_x(2, 1, 3)

    def share_rows(buffer, item):
        rows = buffer.at[item, mine]
        return send(rows, rows, core_peer)

    def second_norm(copy, item):
        rows = load_half(tokens, item, c) + both(copy, send_a, swapped_one, item)
        middle[item] = rows
        normal, _ = norm_stats(rows)
        normed_two[item, mine, :] = (normal * norms[2:3, :] + norms[3:4, :]).astype(BF16)
        return share_rows(normed_two, item)

    def feed_up(item, half):
        rows = half_rows(half)
        grown, slope = gelu_both(dot(normed_two[item, rows, :], weights[1]))
        hidden[item, rows, :] = grown.astype(BF16)
        total[item, rows, :] = slope

    def feed_down(item, half, keeps):
        rows = half_rows(half)
        grown = hidden[item, rows, :]
        pulled = dot(load_half(back, item, half).astype(BF16), weights[2])
        pull = (pulled * total[item, rows, :]).astype(BF16)
        grad_upper[item, rows, :] = pull
        terms = dot(pull, weights[1], NT)
        lowered = dot(grown, weights[2], NT)
        if keeps:
            keep[item] = terms
            keep_low[item] = lowered
            return None
        send_a[item] = terms.astype(BF16)
        first = to_core(recv_mid, item, send_a)
        send_b[item] = lowered.astype(BF16)
        return first, to_core(recv_low, item, send_b)

    def band_grad(slot, first, width, left_of, right_of):
        total[slot, :, first : first + width] = dot(left_of(0), right_of(0), TN) + dot(
            left_of(1), right_of(1), TN
        )

    x_copies = {}
    z_copies = {}

    def grads_out(mat, slot):
        for k in (2, 1, 3, 0):
            x_send[mat, k] = total[slot, block_rows(2 * ((z + k) % 4) + 1 - x), :].astype(BF16)
            x_copies[mat, k] = send(x_send.at[mat, k], x_recv.at[mat, k], x_peer)

    def grads_on(mat, slot):
        for k in (2, 1, 3):
            done_sending(x_copies[mat, k])
            x_copies[mat, k].wait_recv()
            x_send[mat, k] = (
                total[slot, block_rows(2 * ((z + k) % 4) + x), :] + x_recv[mat, k].astype(F32)
            ).astype(BF16)
            z_copies[mat, k] = send(x_send.at[mat, k], z_recv.at[mat, k - 1], z_peers[k - 1])
        x_copies[mat, 0].wait_recv()
        shards_out[mat] = total[slot, own_block, :] + x_recv[mat, 0].astype(F32)

    def grads_in(mat):
        summed = shards_out[mat]
        for k in (1, 3, 2):
            z_copies[mat, k].wait_recv()
            summed += z_recv[mat, k - 1].astype(F32)
        shards_out[mat] = summed
        return jnp.sum(summed * summed)

    two_0 = second_norm(swap_0, 0)
    done_sending(swap_0)
    straight_in(1)
    feed_up(0, c)
    pass_x(2, 2)
    two_0.wait_recv()
    feed_up(0, 1 - c)
    straight_in(2)
    mid_0, low_0 = feed_down(0, 1 - c, False)
    feed_down(0, c, True)
    swap_mid_0 = to_swap(mid_0, keep, recv_mid, send_a, swapped_mid, 0)
    two_1 = second_norm(swap_1, 1)
    done_sending(swap_1)
    feed_up(1, c)
    two_1.wait_recv()
    feed_up(1, 1 - c)
    for first in (0, 256, 512):
        band_grad(
            0, first, 256,
            lambda i: back[i], lambda i, f=first: hidden[i, 0:SLOTS, f : f + 256],
        )
    grads_out(2, 0)
    mid_1, low_1 = feed_down(1, 1 - c, False)
    feed_down(1, c, True)

    swap_mid_1 = to_swap(mid_1, keep, recv_mid, send_a, swapped_mid, 1)
    low_swap_0 = to_swap(low_0, keep_low, recv_low, send_b, swapped_low, 0)
    for first in (0, 256, 512):
        band_grad(
            1, first, 256,
            lambda i: normed_two[i], lambda i, f=first: grad_upper[i, :, f : f + 256],
        )
    grads_out(1, 1)

    third = table_mine.shape[1] // 3

    def pack(buffer, first):
        for row in range(2):
            for piece in range(3):
                at = 3 * row + piece
                buffer[at : at + 1, :] = table_mine[
                    first + row : first + row + 1, piece * third : (piece + 1) * third
                ]

    def unpack(summed, first):
        for row in range(2):
            for piece in range(3):
                at = 3 * row + piece
                table_out[first + row : first + row + 1, piece * third : (piece + 1) * third] = (
                    summed[at : at + 1]
                )

    def to_group(buffer, received):
        copies = [send(buffer, received.at[3], x_peer)]
        for k in (2, 1, 3):
            copies.append(send(buffer, received.at[3 + k], z_peers[k - 1]))
            copies.append(send(buffer, received.at[6 + k], xz_peers[k - 1]))
        return copies

    def group_sum(copies, buffer, received):
        for copy in copies:
            copy.wait_recv()
        parts = [buffer[...] + received[3]] + [received[3 + k] + received[6 + k] for k in (1, 2, 3)]
        ordered = None
        for level in range(4):
            piece = parts[0]
            for k in (1, 2, 3):
                piece = jnp.where((level + k) % 4 == z, parts[k], piece)
            ordered = piece if ordered is None else ordered + piece
        return ordered

    def middle_back(copy, item):
        grad_two = both(copy, send_a, swapped_mid, item)
        normal, inverse = norm_stats(middle[item])
        sums = (
            jnp.sum(grad_two * normal, axis=0, keepdims=True),
            jnp.sum(grad_two, axis=0, keepdims=True),
        )
        for row, part in zip((2, 3), sums):
            table_mine[row : row + 1, :] = part if item == 0 else table_mine[row : row + 1, :] + part
        pulled = load_half(back, item, c) + norm_back(
            grad_two, normal, inverse, norms[2:3, :]
        )
        grad_mid[item] = pulled
        middle_low[item, mine, :] = pulled.astype(BF16)
        return share_rows(middle_low, item)

    def attend_back(item, shared):
        for half in (c, 1 - c):
            rows = half_rows(half)
            if half is not c:
                shared.wait_recv()
            pulled = dot(middle_low[item, rows, :], weights[0, :, 576:768]).astype(BF16)
            for head in range(3):
                heads[item * 3 + head, rows, :] = pulled[:, head * HEAD_DIM : (head + 1) * HEAD_DIM]

        @pl.loop(0, 3)
        def _(head):
            at = item * 3 + head
            grad_key = None
            grad_value = None
            key_rows = keys[at]
            value_rows = values[at]
            for half, extent in ((1, KEYS), (0, NEAR_KEYS)):
                first = half * HALF
                rows = slice(first, first + HALF)
                pulled = heads[at, rows, :]
                weight = dot(pulled, value_rows[0:extent], NT)
                low = probs[at, rows, 0:extent]
                wide = low.astype(F32)
                weight = wide * weight
                moved = (weight - wide * jnp.sum(weight, axis=-1, keepdims=True)).astype(BF16)
                asked = queries[at, rows, :]
                part_key = dot(moved, asked, TN)
                part_value = dot(low, pulled, TN)
                queries[at, rows, :] = (
                    dot(moved, key_rows[0:extent]) * HEAD_DIM ** (-0.5)
                ).astype(BF16)
                if grad_key is None:
                    grad_key, grad_value = part_key, part_value
                else:
                    keys[at, 0:extent, :] = (grad_key[0:extent] + part_key).astype(BF16)
                    values[at, 0:extent, :] = (grad_value[0:extent] + part_value).astype(BF16)
                    keys[at, extent:KEYS, :] = grad_key[extent:KEYS].astype(BF16)
                    values[at, extent:KEYS, :] = grad_value[extent:KEYS].astype(BF16)

        for half in (0, 1):
            rows = slice(half * HALF, (half + 1) * HALF)
            grad_triple[item, rows, :] = jnp.concatenate(
                [
                    source[item * 3 + head, rows, :]
                    for source in (queries, keys, values)
                    for head in range(3)
                ],
                axis=1,
            )

    def first_terms(item):
        inward = weights[0, :, 0:576]
        send_a[item] = dot(grad_triple[item, half_rows(1 - c), :], inward, NT).astype(BF16)
        copy = to_core(recv_one, item, send_a)
        keep[item] = dot(grad_triple[item, mine, :], inward, NT)
        return copy

    ml_0 = middle_back(swap_mid_0, 0)
    done_sending(swap_mid_0)
    grads_on(2, 0)
    attend_back(0, ml_0)
    first_0 = first_terms(0)
    ml_1 = middle_back(swap_mid_1, 1)
    pack(early_mine, 2)
    early_core = send(early_mine, early_recv.at[0], core_peer)
    done_sending(swap_mid_1)
    first_swap_0 = to_swap(first_0, keep, recv_one, send_a, swapped_one, 0)
    attend_back(1, ml_1)
    early_core.wait_recv()
    done_sending(early_core)
    early_mine[...] = early_mine[...] + early_recv[0]
    early_group = to_group(early_mine, early_recv)
    grads_on(1, 1)
    first_1 = first_terms(1)
    for first, width in ((0, 256), (256, 256), (512, 64)):
        band_grad(
            0, first, width,
            lambda i: normed_one[i], lambda i, f=first, w=width: grad_triple[i, :, f : f + w],
        )
        if first == 0:
            first_swap_1 = to_swap(first_1, keep, recv_one, send_a, swapped_one, 1)
            low_swap_1 = to_swap(low_1, keep_low, recv_low, send_b, swapped_low, 1)
    band_grad(0, 576, 192, lambda i: middle_low[i], lambda i: context[i])
    grads_out(0, 0)

    stores = []

    def give(half_buffer, result, item):
        here = result.at[item, mine]
        store = pltpu.make_async_copy(half_buffer.at[item], here, local_sems.at[len(stores)])
        store.start()
        stores.append(store)
        return send(half_buffer.at[item], here, core_peer)

    def first_back(copy, item):
        grad_one = both(copy, send_a, swapped_one, item)
        normal, inverse = norm_stats(load_half(tokens, item, c))
        sums = (
            jnp.sum(grad_one * normal, axis=0, keepdims=True),
            jnp.sum(grad_one, axis=0, keepdims=True),
        )
        for row, part in zip((0, 1), sums):
            table_mine[row : row + 1, :] = part if item == 0 else table_mine[row : row + 1, :] + part
        grad_half[item] = (
            grad_mid[item] + norm_back(grad_one, normal, inverse, norms[0:1, :])
        ).astype(BF16)
        return give(grad_half, grad_h, item)

    def outcome(copy, item):
        out_half[item] = (middle[item] + both(copy, send_b, swapped_low, item)).astype(BF16)
        return give(out_half, output_h, item)

    out_0 = outcome(low_swap_0, 0)
    grads_on(0, 0)
    rows_0 = first_back(first_swap_0, 0)
    squares = grads_in(2)
    rows_1 = first_back(first_swap_1, 1)
    squares += grads_in(1)
    squares += grads_in(0)
    unpack(group_sum(early_group, early_mine, early_recv), 2)
    pack(late_mine, 0)
    late_mine[6:8, :] = jnp.broadcast_to(squares, (2, third))

    hops = [
        send(late_mine, late_recv.at[at], peer)
        for at, peer in enumerate((core_peer, y_peer, diagonal_peer))
    ]
    out_1 = outcome(low_swap_1, 1)
    for hop in hops:
        hop.wait_recv()
    done_sending(*hops)
    beside = late_mine[...] + late_recv[0]
    late_mine[0:6, :] = beside[0:6]
    late_mine[6:8, :] = beside[6:8] + (late_recv[1, 6:8, :] + late_recv[2, 6:8, :])
    summed = group_sum(to_group(late_mine, late_recv), late_mine, late_recv)
    unpack(summed, 0)
    table_out[4:8, :] = jnp.broadcast_to(summed[6:7, 0:1], (4, table_out.shape[1]))

    given = [rows_0, rows_1, out_0, out_1]
    for copy in given:
        copy.wait_recv()
    for store in stores:
        store.wait()
    for copy in list(pending):
        copy.wait_send()
    for copy in onward.values():
        copy.wait_send()
    for wanted, copy in later:

        @pl.when(wanted)
        def _():
            copy.wait_send()


def update_kernel(
    place, output_h, grad_h, shards_h, table_h, norms_h, *refs
):
    params_h, results, scratch = refs[:14], refs[14:32], refs[32:]
    output_to, grad_to, norm_out = results[:3]
    targets = results[3:]
    output_in, grad_in, output_v, grad_v, shards, table, norms = scratch[:7]
    params = scratch[7:21]
    updated = scratch[21:36]
    load_sems, store_sems = scratch[36:]
    loads = [
        pltpu.make_async_copy(source, target, load_sems.at[i])
        for i, (source, target) in enumerate(
            zip(
                (table_h, grad_h, output_h, shards_h, norms_h) + params_h,
                (table, grad_in, output_in, shards, norms) + params,
            )
        )
    ]
    for load in loads:
        load.start()
    stores = []

    def store(source, target):
        copy = pltpu.make_async_copy(source, target, store_sems.at[len(stores)])
        copy.start()
        stores.append(copy)

    loads[0].wait()
    sums = table[0:4, :]
    total = table[4:5, 0:1] + jnp.sum(
        jnp.sum(sums * sums, axis=1, keepdims=True), axis=0, keepdims=True
    )
    grad_norm = jnp.sqrt(total)
    norm_out[...] = grad_norm
    clip = jnp.minimum(1.0, CLIP_NORM / (grad_norm + 1e-06))

    loads[1].wait()
    for item in range(2):
        grad_v[item] = grad_in[item, 0:SLOTS, :].astype(F32)
        store(grad_v.at[item], grad_to.at[item])
    loads[2].wait()
    output_v[...] = output_in[:, 0:SLOTS, :]
    store(output_v, output_to)
    loads[3].wait()
    loads[4].wait()

    def update(index, gradients, rate, decay, master_at=None):
        m_at, v_at = 4 + index, 9 + index
        for at in (m_at, v_at) if index == 4 else (index, m_at, v_at):
            loads[5 + at].wait()
        for part, gradient in enumerate(gradients):
            at = (lambda ref: ref.at[part]) if index == 0 else (lambda ref: ref)
            master = master_at if index == 4 else at(params[index])[...]
            values = adam_update(
                master, at(params[m_at])[...], at(params[v_at])[...], gradient, clip, rate, decay
            )
            for which, value in enumerate(values):
                at(updated[3 * index + which])[...] = value
        for which in range(3):
            store(updated[3 * index + which], targets[3 * index + which])

    part = params[0].shape[2]
    update(3, [shards[2]], RATE_DOWNWARD, WEIGHT_DECAY)
    update(2, [shards[1]], RATE_UPWARD, WEIGHT_DECAY)
    update(
        0, [shards[0, :, i * part : (i + 1) * part] for i in range(3)], RATE_INWARD, WEIGHT_DECAY
    )
    update(1, [shards[0, :, 3 * part :].T], RATE_OUTWARD, WEIGHT_DECAY)
    span = params[8].shape[1]
    own_sums = sums[:, 0:span]
    own_norms = norms[:, 0:span]
    for index in range(1, 8):
        here = place[0] == index
        columns = slice(index * span, (index + 1) * span)
        own_sums = jnp.where(here, sums[:, columns], own_sums)
        own_norms = jnp.where(here, norms[:, columns], own_norms)
    update(4, [own_sums], RATE_NORMS, 0.0, own_norms)
    for copy in stores:
        copy.wait()


def fused_body(
    tokens, cotangent, step_counts, wrist_flags,
    inward_weight, outward_weight, upward_weight, downward_weight, norm_table,
    momentum_inward, momentum_outward, momentum_upward, momentum_downward, momentum_norms,
    variance_inward, variance_outward, variance_upward, variance_downward, variance_norms,
):
    width = norm_table.shape[1]
    block = upward_weight.shape[0]
    any_spec = pl.BlockSpec(memory_space=pl.ANY)
    vmem = pl.BlockSpec(memory_space=pltpu.VMEM)
    smem = pl.BlockSpec(memory_space=pltpu.SMEM)
    rows = pltpu.VMEM((2, ROWS, width), BF16)
    halves = pltpu.VMEM((2, HALF, width), BF16)
    keep = pltpu.VMEM((2, HALF, width), F32)
    output, grads, shards, table = pl.pallas_call(
        fused_kernel,
        out_shape=(
            jax.ShapeDtypeStruct((2, ROWS, width), BF16),
            jax.ShapeDtypeStruct((2, ROWS, width), BF16),
            jax.ShapeDtypeStruct((3, block, width), F32),
            jax.ShapeDtypeStruct((8, width), F32),
        ),
        in_specs=[smem, smem, any_spec, any_spec, any_spec, any_spec, any_spec, any_spec, vmem],
        out_specs=(any_spec, any_spec, vmem, vmem),
        scratch_shapes=[
            pltpu.VMEM((3, width, width), BF16),
            pltpu.VMEM((2, SLOTS, width), BF16),
            pltpu.VMEM((2, SLOTS, width), BF16),
            rows,
            pltpu.VMEM((6, ROWS, HEAD_DIM), BF16),
            pltpu.VMEM((6, KEYS, HEAD_DIM), BF16),
            pltpu.VMEM((6, KEYS, HEAD_DIM), BF16),
            pltpu.VMEM((6, ROWS, KEYS), BF16),
            pltpu.VMEM((6, ROWS, HEAD_DIM), BF16),
            pltpu.VMEM((2, ROWS, 192), BF16),
            keep,
            rows,
            rows,
            rows,
            rows,
            halves,
            halves,
            keep,
            keep,
            halves,
            halves,
            halves,
            halves,
            halves,
            halves,
            halves,
            halves,
            keep,
            pltpu.VMEM((2, ROWS, 576), BF16),
            pltpu.VMEM((2, width, width), F32),
            pltpu.VMEM((3, 4, block, width), BF16),
            pltpu.VMEM((3, 4, block, width), BF16),
            pltpu.VMEM((3, 3, block, width), BF16),
            pltpu.VMEM((8, width), F32),
            pltpu.VMEM((8, width // 3), F32),
            pltpu.VMEM((10, 8, width // 3), F32),
            pltpu.VMEM((8, width // 3), F32),
            pltpu.VMEM((10, 8, width // 3), F32),
            pltpu.VMEM(inward_weight.shape, F32),
            pltpu.VMEM(outward_weight.shape, F32),
            pltpu.VMEM(upward_weight.shape, F32),
            pltpu.VMEM(upward_weight.shape, F32),
            pltpu.SemaphoreType.DMA((N_REMOTE,)),
            pltpu.SemaphoreType.DMA((N_REMOTE,)),
            pltpu.SemaphoreType.DMA((10,)),
        ],
        compiler_params=pltpu.CompilerParams(
            collective_id=0, has_side_effects=True, vmem_limit_bytes=VMEM_BYTES
        ),
        name="block_step",
    )(
        step_counts,
        wrist_flags,
        inward_weight,
        outward_weight,
        upward_weight,
        downward_weight.T,
        tokens,
        cotangent,
        norm_table,
    )
    place = jnp.reshape(lax.axis_index("dp"), (1,)).astype(jnp.int32)
    params = (
        inward_weight, outward_weight, upward_weight, downward_weight.T,
        momentum_inward, momentum_outward, momentum_upward, momentum_downward.T, momentum_norms,
        variance_inward, variance_outward, variance_upward, variance_downward.T, variance_norms,
    )
    shapes = [param.shape for param in params]
    updates = [shape for shape in shapes[:4] + shapes[8:9] for _ in range(3)]
    padded = pltpu.VMEM((2, ROWS, width), BF16)
    results = pl.pallas_call(
        update_kernel,
        out_shape=(
            jax.ShapeDtypeStruct((2, SLOTS, width), BF16),
            jax.ShapeDtypeStruct((2, SLOTS, width), F32),
            jax.ShapeDtypeStruct((1, 1), F32),
            *[jax.ShapeDtypeStruct(shape, F32) for shape in updates],
        ),
        in_specs=[smem] + [any_spec] * 19,
        out_specs=(any_spec, any_spec, vmem) + (any_spec,) * 15,
        scratch_shapes=[
            padded,
            padded,
            pltpu.VMEM((2, SLOTS, width), BF16),
            pltpu.VMEM((2, SLOTS, width), F32),
            pltpu.VMEM((3, block, width), F32),
            pltpu.VMEM((8, width), F32),
            pltpu.VMEM((4, width), F32),
            *[pltpu.VMEM(shape, F32) for shape in shapes],
            *[pltpu.VMEM(shape, F32) for shape in updates],
            pltpu.SemaphoreType.DMA((19,)),
            pltpu.SemaphoreType.DMA((18,)),
        ],
        compiler_params=pltpu.CompilerParams(vmem_limit_bytes=VMEM_BYTES),
        name="update_step",
    )(place, output, grads, shards, table, norm_table, *params)
    updated = list(results[3:])
    for index in (9, 10, 11):
        updated[index] = updated[index].T
    return (results[0], results[1], results[2][0, 0], *updated)


def solution(mesh):
    fits = mesh.shape["dp"] == 8 and mesh.shape["mp"] == 4
    return whole_program(mesh, fused_body if fits else body)
```

```python
import jax
import jax.numpy as jnp
from jax import lax
from jax.experimental import pallas as pl
from jax.experimental.pallas import tpu as pltpu
from jax.sharding import PartitionSpec as P

HEAD_DIM = 64
TASK = 16
PRIMARY = 256
WRIST = 64
READOUT = 4
SLOTS = 664
MB = 2
STEP = 10


NORM_EPSILON = 1e-06
CLIP_NORM = 1.0
BETA_ONE = 0.9
BETA_TWO = 0.999
ADAM_EPSILON = 1e-08
WEIGHT_DECAY = 0.1
NEGATIVE = -1e30
RATE_INWARD = 0.05
RATE_OUTWARD = 0.15
RATE_UPWARD = 0.04
RATE_DOWNWARD = 0.02
RATE_NORMS = 0.5


def slot_mask(live_steps, has_wrist):
    position = jnp.arange(SLOTS, dtype=jnp.int32)
    relative = position - TASK
    period = PRIMARY + WRIST + READOUT
    is_task = relative < 0
    forward_pos = jnp.maximum(relative, 0)
    stepno = forward_pos // period
    offset = forward_pos % period
    not_task = jnp.logical_not(is_task)
    is_read = jnp.logical_and(not_task, offset >= PRIMARY + WRIST)
    is_obs = jnp.logical_and(not_task, jnp.logical_not(is_read))
    is_wrist = jnp.logical_and(is_obs, offset >= PRIMARY)
    present = jnp.logical_or(
        is_task,
        jnp.logical_and(
            stepno < live_steps, jnp.logical_or(jnp.logical_not(is_wrist), has_wrist == 1)
        ),
    )
    see_obs = is_obs[None, :] & not_task[:, None] & (stepno[None, :] <= stepno[:, None])
    see_read = is_read[None, :] & is_read[:, None] & (stepno[None, :] == stepno[:, None])
    return present[None, :] & (is_task[None, :] | see_obs | see_read)


def layer_stats(values):
    centre = values - jnp.mean(values, axis=-1, keepdims=True)
    inverse = lax.rsqrt(jnp.mean(centre * centre, axis=-1, keepdims=True) + NORM_EPSILON)
    return (centre * inverse, inverse)


def layer_back(grad_result, normal, inverse, gain_row):
    scaled = grad_result * gain_row
    return inverse * (
        scaled
        - jnp.mean(scaled, axis=-1, keepdims=True)
        - normal * jnp.mean(scaled * normal, axis=-1, keepdims=True)
    )


def gelu_tanh(values):
    return (
        0.5
        * values
        * (1.0 + jnp.tanh(0.7978845608028654 * (values + 0.044715 * values * values * values)))
    )


def attention_scores(queries, key_heads, allowed, score_scale):
    dotted = (
        jnp.einsum("nqhd,nkhd->nhqk", queries, key_heads, preferred_element_type=jnp.float32)
        * score_scale
    )
    return jnp.where(allowed, dotted, NEGATIVE)


def adam_update(master, momentum, variance, gradient, clip_scale, step_rate, decay_rate):
    clipped = gradient * clip_scale
    moment_one = BETA_ONE * momentum + (1.0 - BETA_ONE) * clipped
    moment_two = BETA_TWO * variance + (1.0 - BETA_TWO) * clipped * clipped
    first_hat = moment_one / (1.0 - BETA_ONE**STEP)
    second_hat = moment_two / (1.0 - BETA_TWO**STEP)
    updated = master - step_rate * (
        first_hat / (jnp.sqrt(second_hat) + ADAM_EPSILON) + decay_rate * master
    )
    return (moment_one, moment_two, updated)


def body(
    tokens,
    cotangent,
    step_counts,
    wrist_flags,
    inward_weight,
    outward_weight,
    upward_weight,
    downward_weight,
    norm_table,
    momentum_inward,
    momentum_outward,
    momentum_upward,
    momentum_downward,
    momentum_norms,
    variance_inward,
    variance_outward,
    variance_upward,
    variance_downward,
    variance_norms,
):
    full_inward, full_outward, full_upward, full_downward = (
        lax.all_gather(inward_weight.astype(jnp.bfloat16), "dp", axis=1, tiled=True),
        lax.all_gather(outward_weight.astype(jnp.bfloat16), "dp", axis=1, tiled=True),
        lax.all_gather(upward_weight.astype(jnp.bfloat16), "dp", axis=0, tiled=True),
        lax.all_gather(downward_weight.astype(jnp.bfloat16), "dp", axis=1, tiled=True),
    )
    model_width = norm_table.shape[1]
    local_heads = full_inward.shape[2] // HEAD_DIM
    score_scale = HEAD_DIM ** (-0.5)
    per_batch = tokens.shape[0] // MB
    row_count = per_batch * SLOTS
    share_rows = row_count // lax.axis_size("mp")
    share_start = lax.axis_index("mp") * share_rows
    results = []
    input_grads = []
    local_sums = None
    for batch_index in range(MB):
        start_item = batch_index * per_batch
        block_tokens = (
            tokens[start_item : start_item + per_batch]
            .astype(jnp.float32)
            .reshape(row_count, model_width)
        )
        block_back = (
            cotangent[start_item : start_item + per_batch]
            .astype(jnp.float32)
            .reshape(row_count, model_width)
        )
        allowed = jax.vmap(slot_mask)(
            step_counts[start_item : start_item + per_batch],
            wrist_flags[start_item : start_item + per_batch],
        )[:, None]
        normal_one, inverse_one = layer_stats(block_tokens)
        normed_one = (normal_one * norm_table[0] + norm_table[1]).astype(jnp.bfloat16)
        projected = jnp.einsum(
            "rd,cdm->crm", normed_one, full_inward, preferred_element_type=jnp.float32
        ).astype(jnp.bfloat16)
        triple = projected.reshape(3, per_batch, SLOTS, local_heads, HEAD_DIM)
        queries = triple[0]
        key_heads = triple[1]
        value_heads = triple[2]
        scores = attention_scores(queries, key_heads, allowed, score_scale)
        highest = jnp.max(scores, axis=-1, keepdims=True)
        log_total = highest + jnp.log(jnp.sum(jnp.exp(scores - highest), axis=-1, keepdims=True))
        attention_low = jnp.exp(scores - log_total).astype(jnp.bfloat16)
        context = (
            jnp.einsum(
                "nhqk,nkhd->nqhd", attention_low, value_heads, preferred_element_type=jnp.float32
            )
            .astype(jnp.bfloat16)
            .reshape(row_count, -1)
        )
        attn_terms = jnp.dot(context, full_outward, preferred_element_type=jnp.float32)
        tokens_share = lax.dynamic_slice_in_dim(block_tokens, share_start, share_rows, 0)
        back_share = lax.dynamic_slice_in_dim(block_back, share_start, share_rows, 0)
        middle_share = tokens_share + lax.psum_scatter(
            attn_terms, "mp", scatter_dimension=0, tiled=True
        )
        normal_two, inverse_two = layer_stats(middle_share)
        normed_share = (normal_two * norm_table[2] + norm_table[3]).astype(jnp.bfloat16)
        normed_two = lax.all_gather(normed_share, "mp", axis=0, tiled=True)
        upper_pre = jnp.dot(normed_two, full_upward, preferred_element_type=jnp.float32)
        hidden = gelu_tanh(upper_pre).astype(jnp.bfloat16)
        lowered_share = lax.psum_scatter(
            jnp.dot(hidden, full_downward, preferred_element_type=jnp.float32).astype(jnp.bfloat16),
            "mp",
            scatter_dimension=0,
            tiled=True,
        ).astype(jnp.float32)
        output_share = (middle_share + lowered_share).astype(jnp.bfloat16)
        back_rows = block_back.astype(jnp.bfloat16)
        grad_down = jnp.einsum("rf,rd->fd", hidden, back_rows, preferred_element_type=jnp.float32)
        grad_hidden = jnp.einsum(
            "rd,fd->rf", back_rows, full_downward, preferred_element_type=jnp.float32
        )
        upper_pull = jax.vjp(gelu_tanh, upper_pre)[1]
        grad_upper = upper_pull(grad_hidden)[0].astype(jnp.bfloat16)
        grad_up = jnp.einsum(
            "rd,rf->df", normed_two, grad_upper, preferred_element_type=jnp.float32
        )
        normed_terms = jnp.einsum(
            "rf,df->rd", grad_upper, full_upward, preferred_element_type=jnp.float32
        )
        grad_normed_two = lax.psum_scatter(normed_terms, "mp", scatter_dimension=0, tiled=True)
        gain_two = jnp.sum(grad_normed_two * normal_two, axis=0)
        shift_two = jnp.sum(grad_normed_two, axis=0)
        grad_middle_share = back_share + layer_back(
            grad_normed_two, normal_two, inverse_two, norm_table[2]
        )
        middle_low, output_rows = (
            lax.all_gather(grad_middle_share.astype(jnp.bfloat16), "mp", axis=0, tiled=True),
            lax.all_gather(output_share, "mp", axis=0, tiled=True),
        )
        results.append(output_rows.reshape(per_batch, SLOTS, model_width))
        grad_out = jnp.einsum("rm,rd->md", context, middle_low, preferred_element_type=jnp.float32)
        grad_context = (
            jnp.einsum("rd,md->rm", middle_low, full_outward, preferred_element_type=jnp.float32)
            .astype(jnp.bfloat16)
            .reshape(per_batch, SLOTS, local_heads, HEAD_DIM)
        )
        scores_again = attention_scores(queries, key_heads, allowed, score_scale)
        attention_full = jnp.exp(scores_again - log_total)
        attention_again = attention_full.astype(jnp.bfloat16)
        grad_values = jnp.einsum(
            "nhqk,nqhd->nkhd", attention_again, grad_context, preferred_element_type=jnp.float32
        ).astype(jnp.bfloat16)
        grad_weights = jnp.einsum(
            "nqhd,nkhd->nhqk", grad_context, value_heads, preferred_element_type=jnp.float32
        )
        grad_scores = (
            attention_full
            * (grad_weights - jnp.sum(grad_weights * attention_full, axis=-1, keepdims=True))
        ).astype(jnp.bfloat16)
        grad_queries = (
            jnp.einsum(
                "nhqk,nkhd->nqhd", grad_scores, key_heads, preferred_element_type=jnp.float32
            )
            * score_scale
        ).astype(jnp.bfloat16)
        grad_keys = (
            jnp.einsum("nhqk,nqhd->nkhd", grad_scores, queries, preferred_element_type=jnp.float32)
            * score_scale
        ).astype(jnp.bfloat16)
        grad_triple = jnp.stack([grad_queries, grad_keys, grad_values]).reshape(3, row_count, -1)
        grad_in = jnp.einsum(
            "rd,crm->cdm", normed_one, grad_triple, preferred_element_type=jnp.float32
        )
        first_terms = jnp.einsum(
            "crm,cdm->rd", grad_triple, full_inward, preferred_element_type=jnp.float32
        )
        grad_normed_one = lax.psum_scatter(first_terms, "mp", scatter_dimension=0, tiled=True)
        normal_share = lax.dynamic_slice_in_dim(normal_one, share_start, share_rows, 0)
        inverse_share = lax.dynamic_slice_in_dim(inverse_one, share_start, share_rows, 0)
        gain_one = jnp.sum(grad_normed_one * normal_share, axis=0)
        shift_one = jnp.sum(grad_normed_one, axis=0)
        tokens_grad_share = grad_middle_share + layer_back(
            grad_normed_one, normal_share, inverse_share, norm_table[0]
        )
        table_terms = jnp.stack([gain_one, shift_one, gain_two, shift_two])[None]
        grad_tokens, gathered_tables = (
            lax.all_gather(tokens_grad_share, "mp", axis=0, tiled=True),
            lax.all_gather(table_terms, "mp", axis=0, tiled=True),
        )
        grad_table = jnp.sum(gathered_tables, axis=0)
        input_grads.append(grad_tokens.reshape(per_batch, SLOTS, model_width))
        batch_grads = (grad_in, grad_out, grad_up, grad_down, grad_table)
        if local_sums is None:
            local_sums = batch_grads
        else:
            local_sums = tuple((former + latter for former, latter in zip(local_sums, batch_grads)))
    shards = (
        lax.psum_scatter(local_sums[0], "dp", scatter_dimension=1, tiled=True),
        lax.psum_scatter(local_sums[1], "dp", scatter_dimension=1, tiled=True),
        lax.psum_scatter(local_sums[2], "dp", scatter_dimension=0, tiled=True),
        lax.psum_scatter(local_sums[3], "dp", scatter_dimension=1, tiled=True),
        lax.psum_scatter(local_sums[4], "dp", scatter_dimension=1, tiled=True),
    )
    mp_count = lax.axis_size("mp")
    squares = (
        sum((jnp.sum(piece * piece) for piece in shards[:4]))
        + jnp.sum(shards[4] * shards[4]) / mp_count
    )
    grad_norm = jnp.sqrt(lax.psum(squares, ("dp", "mp")))
    clip_scale = jnp.minimum(1.0, CLIP_NORM / (grad_norm + 1e-06))
    shard_width = shards[4].shape[1]
    own_table = lax.dynamic_slice_in_dim(
        norm_table, lax.axis_index("dp") * shard_width, shard_width, 1
    )
    inward_new = adam_update(
        inward_weight,
        momentum_inward,
        variance_inward,
        shards[0],
        clip_scale,
        RATE_INWARD,
        WEIGHT_DECAY,
    )
    outward_new = adam_update(
        outward_weight,
        momentum_outward,
        variance_outward,
        shards[1],
        clip_scale,
        RATE_OUTWARD,
        WEIGHT_DECAY,
    )
    upward_new = adam_update(
        upward_weight,
        momentum_upward,
        variance_upward,
        shards[2],
        clip_scale,
        RATE_UPWARD,
        WEIGHT_DECAY,
    )
    downward_new = adam_update(
        downward_weight,
        momentum_downward,
        variance_downward,
        shards[3],
        clip_scale,
        RATE_DOWNWARD,
        WEIGHT_DECAY,
    )
    norms_new = adam_update(
        own_table, momentum_norms, variance_norms, shards[4], clip_scale, RATE_NORMS, 0.0
    )
    output = jnp.concatenate(results, axis=0)
    input_grad = jnp.concatenate(input_grads, axis=0)
    return (
        output,
        input_grad,
        grad_norm,
        inward_new[0],
        inward_new[1],
        inward_new[2],
        outward_new[0],
        outward_new[1],
        outward_new[2],
        upward_new[0],
        upward_new[1],
        upward_new[2],
        downward_new[0],
        downward_new[1],
        downward_new[2],
        norms_new[0],
        norms_new[1],
        norms_new[2],
    )


def whole_program(mesh, function):
    placed = (
        P("dp", None, None),
        P("dp", None, None),
        P("dp"),
        P("dp"),
        P(None, "dp", "mp"),
        P("mp", "dp"),
        P("dp", "mp"),
        P("mp", "dp"),
        P(),
        P(None, "dp", "mp"),
        P("mp", "dp"),
        P("dp", "mp"),
        P("mp", "dp"),
        P(None, "dp"),
        P(None, "dp", "mp"),
        P("mp", "dp"),
        P("dp", "mp"),
        P("mp", "dp"),
        P(None, "dp"),
    )
    return jax.shard_map(
        function,
        mesh=mesh,
        in_specs=placed,
        out_specs=(
            P("dp", None, None),
            P("dp", None, None),
            P(),
            P(None, "dp", "mp"),
            P(None, "dp", "mp"),
            P(None, "dp", "mp"),
            P("mp", "dp"),
            P("mp", "dp"),
            P("mp", "dp"),
            P("dp", "mp"),
            P("dp", "mp"),
            P("dp", "mp"),
            P("mp", "dp"),
            P("mp", "dp"),
            P("mp", "dp"),
            P(None, "dp"),
            P(None, "dp"),
            P(None, "dp"),
        ),
        check_vma=False,
    )


NN = (((1,), (0,)), ((), ()))
NT = (((1,), (1,)), ((), ()))
TN = (((0,), (0,)), ((), ()))
MESH = pl.DeviceIdType.MESH
F32 = jnp.float32
BF16 = jnp.bfloat16
ROWS = 672
HALF = ROWS // 2
KEYS = 768
NEAR_KEYS = 384
FIRST_COLUMNS = 640
PERIOD = PRIMARY + WRIST + READOUT


def dot(left, right, dims=NN):
    return lax.dot_general(left, right, dims, preferred_element_type=F32)


def gelu_both(values):
    square = values * values
    inner = 0.7978845608028654 * values * (1.0 + 0.044715 * square)
    bend = jnp.tanh(inner)
    half_up = 0.5 + 0.5 * bend
    slope = half_up + 0.5 * values * (1.0 - bend * bend) * (
        0.7978845608028654 * (1.0 + 0.134145 * square)
    )
    return values * half_up, slope


def key_bits(live_steps, has_wrist):
    place = lax.broadcasted_iota(jnp.int32, (1, KEYS), 1)
    relative = place - TASK
    is_task = relative < 0
    later = relative >= PERIOD
    offset = jnp.where(later, relative - PERIOD, relative)
    is_read = offset >= PRIMARY + WRIST
    is_wrist = jnp.logical_and(offset >= PRIMARY, offset < PRIMARY + WRIST)
    step_of = jnp.where(later, 1, 0)
    alive = jnp.logical_and(
        step_of < live_steps, jnp.logical_or(jnp.logical_not(is_wrist), has_wrist == 1)
    )
    bits = jnp.where(is_read, jnp.where(later, 16, 8), jnp.where(later, 4, 2))
    bits = jnp.where(alive, bits, 0)
    bits = jnp.where(is_task, 1, bits)
    return jnp.where(place < SLOTS, bits, 0)


def query_bits(first):
    place = lax.broadcasted_iota(jnp.int32, (HALF, 1), 0) + first
    relative = place - TASK
    is_task = relative < 0
    later = relative >= PERIOD
    offset = jnp.where(later, relative - PERIOD, relative)
    is_read = offset >= PRIMARY + WRIST
    bits = jnp.where(later, 7, 3) + jnp.where(is_read, jnp.where(later, 16, 8), 0)
    return jnp.where(is_task, 1, bits)


N_REMOTE = 128
VMEM_BYTES = 64 * 1024 * 1024 - 65536


def fused_kernel(
    steps, flags, inward_h, outward_h, upward_h, downward_h, tokens_h, back_h, norms,
    output_h, grad_h, shards_out, table_out,
    weights, tokens, back, normed_one, queries, keys, values, probs, heads, context,
    middle, normed_two, hidden, grad_upper, middle_low, out_half, grad_half,
    keep, keep_low, send_a, send_b,
    recv_one, recv_mid, recv_low, swapped_one, swapped_mid, swapped_low,
    grad_mid, grad_triple, total, x_send, x_recv, z_recv,
    table_mine, early_mine, early_recv, late_mine, late_recv, inward_f, outward_f, upward_f, downward_f,
    send_sems, recv_sems, local_sems,
):
    dp = lax.axis_index("dp")
    mp = lax.axis_index("mp")
    z, x = dp // 2, dp % 2
    y, c = mp // 2, mp % 2
    core_peer = (dp, y * 2 + 1 - c)
    y_peer = (dp, (1 - y) * 2 + c)
    x_peer = (z * 2 + 1 - x, mp)
    z_peers = [(((z + k) % 4) * 2 + x, mp) for k in (1, 2, 3)]
    xz_peers = [(((z + k) % 4) * 2 + 1 - x, mp) for k in (1, 2, 3)]
    diagonal_peer = (dp, (1 - y) * 2 + 1 - c)
    all_peers = [core_peer, y_peer, x_peer, diagonal_peer] + z_peers + xz_peers
    block = weights.shape[1] // 8
    used = []
    pending = []

    def describe(index, src, dst, peer):
        return pltpu.make_async_remote_copy(
            src_ref=src, dst_ref=dst, send_sem=send_sems.at[index], recv_sem=recv_sems.at[index],
            device_id=peer, device_id_type=MESH,
        )

    def send(src, dst, peer):
        used.append(0)
        copy = describe(len(used) - 1, src, dst, peer)
        copy.start()
        pending.append(copy)
        return copy

    def done_sending(*copies):
        for copy in copies:
            copy.wait_send()
            pending[:] = [other for other in pending if other is not copy]

    def block_rows(index):
        return pl.ds(pl.multiple_of(index * block, 32), block)

    def half_rows(half):
        return pl.ds(pl.multiple_of(half * HALF, 16), HALF)

    mine = half_rows(c)
    own_block = block_rows(dp)
    loads = [
        pltpu.make_async_copy(source, target, local_sems.at[4 + i])
        for i, (source, target) in enumerate(
            (
                (inward_h, inward_f),
                (outward_h, outward_f),
                (upward_h, upward_f),
                (downward_h, downward_f),
                (tokens_h, tokens),
                (back_h, back),
            )
        )
    ]
    for load in loads:
        load.start()

    barrier = pltpu.get_barrier_semaphore()
    for peer in all_peers:
        pl.semaphore_signal(barrier, inc=1, device_id=peer, device_id_type=MESH)
    loads[0].wait()
    loads[1].wait()
    weights[0, own_block, :] = jnp.concatenate(
        [inward_f[0], inward_f[1], inward_f[2], outward_f[...].T], axis=1
    ).astype(BF16)
    pl.semaphore_wait(barrier, len(all_peers))

    later = []
    z_index = {}
    for mat in (0,):
        for sign in (1, -1):
            for j in (1, 2, 3):
                z_index[mat, sign, j] = len(used)
                used.append(0)
                z_index[mat, sign, j, "x"] = len(used)
                used.append(0)
    own_x = {}

    def z_send_block(mat, sign, j):
        origin = z - sign * (j - 1)
        rows = weights.at[mat, block_rows(origin * 2 + x), 0:FIRST_COLUMNS]
        there = ((z + sign) * 2 + x, mp)
        copy = describe(z_index[mat, sign, j], rows, rows, there)
        wanted = jnp.logical_and(
            jnp.logical_and(origin >= 0, origin <= 3), z < 3 if sign == 1 else z > 0
        )

        @pl.when(wanted)
        def _():
            copy.start()

        later.append((wanted, copy))

    straight = {}
    onward = {}

    def part(mat, rows):
        if mat == 3:
            return weights.at[0, rows, FIRST_COLUMNS:]
        return weights.at[mat, rows, 0:FIRST_COLUMNS] if mat == 0 else weights.at[mat, rows]

    for mat in (3, 1, 2):
        for k in (1, 3, 2):
            rows = part(mat, block_rows(((z + 4 - k) % 4) * 2 + x))
            used.append(0)
            onward[mat, k] = describe(len(used) - 1, rows, rows, x_peer)

    def straight_out(mat):
        rows = part(mat, own_block)
        for k in (1, 3, 2):
            straight[mat, k] = send(rows, rows, z_peers[k - 1])

    def pass_x(mat, *places):
        for k in places:
            straight[mat, k].wait_recv()
            onward[mat, k].start()

    def straight_in(mat):
        own_x[mat].wait_recv()
        for k in (1, 3, 2):
            onward[mat, k].wait_recv()

    def z_sends_out(mat):
        for sign in (1, -1):
            z_send_block(mat, sign, 1)

    def own_out(mat):
        rows = part(mat, own_block)
        own_x[mat] = send(rows, rows, x_peer)

    def arrives(sign, j):
        return z >= j if sign == 1 else z <= 3 - j

    def block_at(mat, sign, j):
        return weights.at[mat, block_rows((z - sign * j) * 2 + x), 0:FIRST_COLUMNS]

    def weights_on(mat, j):
        for sign in (1, -1):
            here = arrives(sign, j)
            rows = block_at(mat, sign, j)
            onward = describe(z_index[mat, sign, j, "x"], rows, rows, x_peer)

            @pl.when(here)
            def _():
                describe(z_index[mat, sign, j], rows, rows, x_peer).wait_recv()

            if j < 3:
                z_send_block(mat, sign, j + 1)

            @pl.when(here)
            def _():
                onward.start()

            later.append((here, onward))

    def weights_in(mat):
        own_x[mat].wait_recv()
        for j in (1, 2, 3):
            for sign in (1, -1):
                rows = block_at(mat, sign, j)

                @pl.when(arrives(sign, j))
                def _():
                    describe(z_index[mat, sign, j, "x"], rows, rows, x_peer).wait_recv()

    def norm_stats(rows):
        centre = rows - jnp.mean(rows, axis=-1, keepdims=True)
        inverse = lax.rsqrt(jnp.mean(centre * centre, axis=-1, keepdims=True) + NORM_EPSILON)
        return centre * inverse, inverse

    def norm_back(grad_result, normal, inverse, gain_row):
        scaled = grad_result * gain_row
        return inverse * (
            scaled
            - jnp.mean(scaled, axis=-1, keepdims=True)
            - normal * jnp.mean(scaled * normal, axis=-1, keepdims=True)
        )

    def load_half(source, item, half):
        body = source[item, pl.ds(pl.multiple_of(half * HALF, 16), SLOTS - HALF), :].astype(F32)
        tail = source[item, SLOTS - HALF : HALF, :].astype(F32)
        return jnp.concatenate([body, jnp.where(half == 0, tail, 0.0)], axis=0)

    def first_norm(item, low, high):
        @pl.loop(low, min(high, 5))
        def _(index):
            rows = pl.ds(pl.multiple_of(index * 112, 16), 112)
            normal, _ = norm_stats(tokens[item, rows, :].astype(F32))
            normed_one[item, rows, :] = (normal * norms[0:1, :] + norms[1:2, :]).astype(BF16)

        if high == 6:
            normal, _ = norm_stats(tokens[item, 560:SLOTS, :].astype(F32))
            normed = normal * norms[0:1, :] + norms[1:2, :]
            none = jnp.zeros((ROWS - SLOTS, normed.shape[1]), F32)
            normed_one[item, 560:ROWS, :] = jnp.concatenate([normed, none], axis=0).astype(BF16)

    z_sends_out(0)
    own_out(0)
    loads[2].wait()
    loads[3].wait()
    weights[1, own_block, :] = upward_f[...].astype(BF16)
    weights[2, own_block, :] = downward_f[...].astype(BF16)
    loads[4].wait()
    first_norm(0, 0, 4)
    weights_on(0, 1)
    first_norm(0, 4, 6)
    first_norm(1, 0, 2)
    weights_on(0, 2)
    for mat in (3, 1, 2):
        straight_out(mat)
    first_norm(1, 2, 6)
    weights_on(0, 3)
    for mat in (3, 1, 2):
        own_out(mat)
    loads[5].wait()
    zero_rows = jnp.zeros((KEYS - ROWS, HEAD_DIM), BF16)
    for i in range(6):
        keys[i, ROWS:KEYS, :] = zero_rows
        values[i, ROWS:KEYS, :] = zero_rows
    weights_in(0)

    def project(item):
        @pl.loop(0, 2)
        def _(half):
            rows = half_rows(half)
            joined = dot(normed_one[item, rows, :], weights[0, :, 0:576])
            for head in range(3):
                low = head * HEAD_DIM
                queries[item * 3 + head, rows, :] = (
                    joined[:, low : low + HEAD_DIM].astype(BF16) * HEAD_DIM ** (-0.5)
                ).astype(BF16)
                low += 192
                keys[item * 3 + head, rows, :] = joined[:, low : low + HEAD_DIM].astype(BF16)
                low += 192
                values[item * 3 + head, rows, :] = joined[:, low : low + HEAD_DIM].astype(BF16)

    def attend(item):
        bits = key_bits(steps[item], flags[item])

        @pl.loop(0, 3)
        def _(head):
            at = item * 3 + head
            for half, extent in ((0, NEAR_KEYS), (1, KEYS)):
                first = half * HALF
                scores = dot(queries[at, first : first + HALF, :], keys[at, 0:extent, :], NT)
                seen = jnp.bitwise_and(bits[:, 0:extent], query_bits(first)) != 0
                scores = jnp.where(seen, scores, NEGATIVE)
                spread = jnp.exp(scores - jnp.max(scores, axis=-1, keepdims=True))
                scale = 1.0 / jnp.sum(spread, axis=-1, keepdims=True)
                low = (spread * scale).astype(BF16)
                probs[at, first : first + HALF, 0:extent] = low
                heads[at, first : first + HALF, :] = dot(low, values[at, 0:extent, :]).astype(BF16)

    def to_core(kind, item, source):
        return send(source.at[item], kind.at[item], core_peer)

    def to_swap(copy, kept, received, staged, swapped, item):
        done_sending(copy)
        copy.wait_recv()
        staged[item] = (kept[item] + received[item].astype(F32)).astype(BF16)
        return send(staged.at[item], swapped.at[item], y_peer)

    def both(copy, staged, swapped, item):
        copy.wait_recv()
        return staged[item].astype(F32) + swapped[item].astype(F32)

    def attention_out(item):
        for half in (0, 1):
            rows = slice(half * HALF, (half + 1) * HALF)
            context[item, rows, :] = jnp.concatenate(
                [heads[item * 3 + head, rows, :] for head in range(3)], axis=1
            )
        outward = weights[0, :, 576:768]
        send_a[item] = dot(context[item, half_rows(1 - c), :], outward, NT).astype(BF16)
        copy = to_core(recv_one, item, send_a)
        keep[item] = dot(context[item, mine, :], outward, NT)
        return copy

    project(0)
    pass_x(3, 1, 3, 2)
    attend(0)
    straight_in(3)
    attn_0 = attention_out(0)
    project(1)
    swap_0 = to_swap(attn_0, keep, recv_one, send_a, swapped_one, 0)
    pass_x(1, 1, 3)
    attend(1)
    pass_x(1, 2)
    attn_1 = attention_out(1)
    swap_1 = to_swap(attn_1, keep, recv_one, send_a, swapped_one, 1)
    pass_x(2, 1, 3)

    def share_rows(buffer, item):
        rows = buffer.at[item, mine]
        return send(rows, rows, core_peer)

    def second_norm(copy, item):
        rows = load_half(tokens, item, c) + both(copy, send_a, swapped_one, item)
        middle[item] = rows
        normal, _ = norm_stats(rows)
        normed_two[item, mine, :] = (normal * norms[2:3, :] + norms[3:4, :]).astype(BF16)
        return share_rows(normed_two, item)

    def feed_up(item, half):
        rows = half_rows(half)
        grown, slope = gelu_both(dot(normed_two[item, rows, :], weights[1]))
        hidden[item, rows, :] = grown.astype(BF16)
        total[item, rows, :] = slope

    def feed_mid(item, half, keeps):
        rows = half_rows(half)
        pulled = dot(load_half(back, item, half).astype(BF16), weights[2])
        pull = (pulled * total[item, rows, :]).astype(BF16)
        grad_upper[item, rows, :] = pull
        terms = dot(pull, weights[1], NT)
        if keeps:
            keep[item] = terms
            return None
        send_a[item] = terms.astype(BF16)
        return to_core(recv_mid, item, send_a)

    def feed_low(item, half, keeps):
        lowered = dot(hidden[item, half_rows(half), :], weights[2], NT)
        if keeps:
            keep_low[item] = lowered
            return None
        send_b[item] = lowered.astype(BF16)
        return to_core(recv_low, item, send_b)

    def band_grad(slot, first, width, left_of, right_of):
        total[slot, :, first : first + width] = dot(left_of(0), right_of(0), TN) + dot(
            left_of(1), right_of(1), TN
        )

    x_copies = {}
    z_copies = {}

    def grads_out(mat, slot):
        for k in (2, 1, 3, 0):
            x_send[mat, k] = total[slot, block_rows(2 * ((z + k) % 4) + 1 - x), :].astype(BF16)
            x_copies[mat, k] = send(x_send.at[mat, k], x_recv.at[mat, k], x_peer)

    def grads_on(mat, slot):
        for k in (2, 1, 3):
            done_sending(x_copies[mat, k])
            x_copies[mat, k].wait_recv()
            x_send[mat, k] = (
                total[slot, block_rows(2 * ((z + k) % 4) + x), :] + x_recv[mat, k].astype(F32)
            ).astype(BF16)
            z_copies[mat, k] = send(x_send.at[mat, k], z_recv.at[mat, k - 1], z_peers[k - 1])
        x_copies[mat, 0].wait_recv()
        shards_out[mat] = total[slot, own_block, :] + x_recv[mat, 0].astype(F32)

    def grads_in(mat):
        summed = shards_out[mat]
        for k in (1, 3, 2):
            z_copies[mat, k].wait_recv()
            summed += z_recv[mat, k - 1].astype(F32)
        shards_out[mat] = summed
        return jnp.sum(summed * summed)

    two_0 = second_norm(swap_0, 0)
    done_sending(swap_0)
    straight_in(1)
    feed_up(0, c)
    pass_x(2, 2)
    two_0.wait_recv()
    feed_up(0, 1 - c)
    straight_in(2)
    mid_0 = feed_mid(0, 1 - c, False)
    feed_mid(0, c, True)
    low_0 = feed_low(0, 1 - c, False)
    swap_mid_0 = to_swap(mid_0, keep, recv_mid, send_a, swapped_mid, 0)
    two_1 = second_norm(swap_1, 1)
    done_sending(swap_1)
    feed_low(0, c, True)
    feed_up(1, c)
    two_1.wait_recv()
    feed_up(1, 1 - c)
    for first in (0, 256, 512):
        band_grad(
            0, first, 256,
            lambda i: back[i], lambda i, f=first: hidden[i, 0:SLOTS, f : f + 256],
        )
    grads_out(2, 0)
    mid_1 = feed_mid(1, 1 - c, False)
    feed_mid(1, c, True)
    low_1 = feed_low(1, 1 - c, False)
    swap_mid_1 = to_swap(mid_1, keep, recv_mid, send_a, swapped_mid, 1)
    feed_low(1, c, True)
    low_swap_0 = to_swap(low_0, keep_low, recv_low, send_b, swapped_low, 0)
    for first in (0, 256, 512):
        band_grad(
            1, first, 256,
            lambda i: normed_two[i], lambda i, f=first: grad_upper[i, :, f : f + 256],
        )
    grads_out(1, 1)

    third = table_mine.shape[1] // 3

    def pack(buffer, first):
        for row in range(2):
            for piece in range(3):
                at = 3 * row + piece
                buffer[at : at + 1, :] = table_mine[
                    first + row : first + row + 1, piece * third : (piece + 1) * third
                ]

    def unpack(summed, first):
        for row in range(2):
            for piece in range(3):
                at = 3 * row + piece
                table_out[first + row : first + row + 1, piece * third : (piece + 1) * third] = (
                    summed[at : at + 1]
                )

    def to_group(buffer, received):
        copies = [send(buffer, received.at[3], x_peer)]
        for k in (2, 1, 3):
            copies.append(send(buffer, received.at[3 + k], z_peers[k - 1]))
            copies.append(send(buffer, received.at[6 + k], xz_peers[k - 1]))
        return copies

    def group_sum(copies, buffer, received):
        for copy in copies:
            copy.wait_recv()
        parts = [buffer[...] + received[3]] + [received[3 + k] + received[6 + k] for k in (1, 2, 3)]
        ordered = None
        for level in range(4):
            piece = parts[0]
            for k in (1, 2, 3):
                piece = jnp.where((level + k) % 4 == z, parts[k], piece)
            ordered = piece if ordered is None else ordered + piece
        return ordered

    def middle_back(copy, item):
        grad_two = both(copy, send_a, swapped_mid, item)
        normal, inverse = norm_stats(middle[item])
        sums = (
            jnp.sum(grad_two * normal, axis=0, keepdims=True),
            jnp.sum(grad_two, axis=0, keepdims=True),
        )
        for row, part in zip((2, 3), sums):
            table_mine[row : row + 1, :] = part if item == 0 else table_mine[row : row + 1, :] + part
        pulled = load_half(back, item, c) + norm_back(
            grad_two, normal, inverse, norms[2:3, :]
        )
        grad_mid[item] = pulled
        middle_low[item, mine, :] = pulled.astype(BF16)
        return share_rows(middle_low, item)

    def attend_back(item, shared):
        for half in (c, 1 - c):
            rows = half_rows(half)
            if half is not c:
                shared.wait_recv()
            pulled = dot(middle_low[item, rows, :], weights[0, :, 576:768]).astype(BF16)
            for head in range(3):
                heads[item * 3 + head, rows, :] = pulled[:, head * HEAD_DIM : (head + 1) * HEAD_DIM]

        @pl.loop(0, 3)
        def _(head):
            at = item * 3 + head
            grad_key = None
            grad_value = None
            key_rows = keys[at]
            value_rows = values[at]
            for half, extent in ((1, KEYS), (0, NEAR_KEYS)):
                first = half * HALF
                rows = slice(first, first + HALF)
                pulled = heads[at, rows, :]
                weight = dot(pulled, value_rows[0:extent], NT)
                low = probs[at, rows, 0:extent]
                wide = low.astype(F32)
                weight = wide * weight
                moved = (weight - wide * jnp.sum(weight, axis=-1, keepdims=True)).astype(BF16)
                asked = queries[at, rows, :]
                part_key = dot(moved, asked, TN)
                part_value = dot(low, pulled, TN)
                queries[at, rows, :] = (
                    dot(moved, key_rows[0:extent]) * HEAD_DIM ** (-0.5)
                ).astype(BF16)
                if grad_key is None:
                    grad_key, grad_value = part_key, part_value
                else:
                    keys[at, 0:extent, :] = (grad_key[0:extent] + part_key).astype(BF16)
                    values[at, 0:extent, :] = (grad_value[0:extent] + part_value).astype(BF16)
                    keys[at, extent:KEYS, :] = grad_key[extent:KEYS].astype(BF16)
                    values[at, extent:KEYS, :] = grad_value[extent:KEYS].astype(BF16)

        for half in (0, 1):
            rows = slice(half * HALF, (half + 1) * HALF)
            grad_triple[item, rows, :] = jnp.concatenate(
                [
                    source[item * 3 + head, rows, :]
                    for source in (queries, keys, values)
                    for head in range(3)
                ],
                axis=1,
            )

    def first_terms(item):
        inward = weights[0, :, 0:576]
        send_a[item] = dot(grad_triple[item, half_rows(1 - c), :], inward, NT).astype(BF16)
        copy = to_core(recv_one, item, send_a)
        keep[item] = dot(grad_triple[item, mine, :], inward, NT)
        return copy

    ml_0 = middle_back(swap_mid_0, 0)
    done_sending(swap_mid_0)
    attend_back(0, ml_0)
    first_0 = first_terms(0)
    grads_on(2, 0)
    ml_1 = middle_back(swap_mid_1, 1)
    pack(early_mine, 2)
    early_core = send(early_mine, early_recv.at[0], core_peer)
    done_sending(swap_mid_1)
    first_swap_0 = to_swap(first_0, keep, recv_one, send_a, swapped_one, 0)
    attend_back(1, ml_1)
    early_core.wait_recv()
    done_sending(early_core)
    early_mine[...] = early_mine[...] + early_recv[0]
    early_group = to_group(early_mine, early_recv)
    grads_on(1, 1)
    first_1 = first_terms(1)
    for first, width in ((0, 256), (256, 256), (512, 64)):
        band_grad(
            0, first, width,
            lambda i: normed_one[i], lambda i, f=first, w=width: grad_triple[i, :, f : f + w],
        )
        if first == 0:
            first_swap_1 = to_swap(first_1, keep, recv_one, send_a, swapped_one, 1)
            low_swap_1 = to_swap(low_1, keep_low, recv_low, send_b, swapped_low, 1)
    band_grad(0, 576, 192, lambda i: middle_low[i], lambda i: context[i])
    grads_out(0, 0)

    stores = []

    def give(half_buffer, result, item):
        here = result.at[item, mine]
        store = pltpu.make_async_copy(half_buffer.at[item], here, local_sems.at[len(stores)])
        store.start()
        stores.append(store)
        return send(half_buffer.at[item], here, core_peer)

    def first_back(copy, item):
        grad_one = both(copy, send_a, swapped_one, item)
        normal, inverse = norm_stats(load_half(tokens, item, c))
        sums = (
            jnp.sum(grad_one * normal, axis=0, keepdims=True),
            jnp.sum(grad_one, axis=0, keepdims=True),
        )
        for row, part in zip((0, 1), sums):
            table_mine[row : row + 1, :] = part if item == 0 else table_mine[row : row + 1, :] + part
        grad_half[item] = (
            grad_mid[item] + norm_back(grad_one, normal, inverse, norms[0:1, :])
        ).astype(BF16)
        return give(grad_half, grad_h, item)

    def outcome(copy, item):
        out_half[item] = (middle[item] + both(copy, send_b, swapped_low, item)).astype(BF16)
        return give(out_half, output_h, item)

    out_0 = outcome(low_swap_0, 0)
    grads_on(0, 0)
    rows_0 = first_back(first_swap_0, 0)
    squares = grads_in(2)
    rows_1 = first_back(first_swap_1, 1)
    squares += grads_in(1)
    squares += grads_in(0)
    unpack(group_sum(early_group, early_mine, early_recv), 2)
    pack(late_mine, 0)
    late_mine[6:8, :] = jnp.broadcast_to(squares, (2, third))

    hops = [
        send(late_mine, late_recv.at[at], peer)
        for at, peer in enumerate((core_peer, y_peer, diagonal_peer))
    ]
    out_1 = outcome(low_swap_1, 1)
    for hop in hops:
        hop.wait_recv()
    done_sending(*hops)
    beside = late_mine[...] + late_recv[0]
    late_mine[0:6, :] = beside[0:6]
    late_mine[6:8, :] = beside[6:8] + (late_recv[1, 6:8, :] + late_recv[2, 6:8, :])
    summed = group_sum(to_group(late_mine, late_recv), late_mine, late_recv)
    unpack(summed, 0)
    table_out[4:8, :] = jnp.broadcast_to(summed[6:7, 0:1], (4, table_out.shape[1]))

    given = [rows_0, rows_1, out_0, out_1]
    for copy in given:
        copy.wait_recv()
    for store in stores:
        store.wait()
    for copy in list(pending):
        copy.wait_send()
    for copy in onward.values():
        copy.wait_send()
    for wanted, copy in later:

        @pl.when(wanted)
        def _():
            copy.wait_send()


def update_kernel(
    place, output_h, grad_h, shards_h, table_h, norms_h, *refs
):
    params_h, results, scratch = refs[:14], refs[14:32], refs[32:]
    output_to, grad_to, norm_out = results[:3]
    targets = results[3:]
    output_in, grad_in, output_v, grad_v, shards, table, norms = scratch[:7]
    params = scratch[7:21]
    updated = scratch[21:36]
    load_sems, store_sems = scratch[36:]
    loads = [
        pltpu.make_async_copy(source, target, load_sems.at[i])
        for i, (source, target) in enumerate(
            zip(
                (table_h, grad_h, output_h, shards_h, norms_h) + params_h,
                (table, grad_in, output_in, shards, norms) + params,
            )
        )
    ]
    for load in loads:
        load.start()
    stores = []

    def store(source, target):
        copy = pltpu.make_async_copy(source, target, store_sems.at[len(stores)])
        copy.start()
        stores.append(copy)

    loads[0].wait()
    sums = table[0:4, :]
    total = table[4:5, 0:1] + jnp.sum(
        jnp.sum(sums * sums, axis=1, keepdims=True), axis=0, keepdims=True
    )
    grad_norm = jnp.sqrt(total)
    norm_out[...] = grad_norm
    clip = jnp.minimum(1.0, CLIP_NORM / (grad_norm + 1e-06))

    loads[1].wait()
    for item in range(2):
        grad_v[item] = grad_in[item, 0:SLOTS, :].astype(F32)
        store(grad_v.at[item], grad_to.at[item])
    loads[2].wait()
    output_v[...] = output_in[:, 0:SLOTS, :]
    store(output_v, output_to)
    loads[3].wait()
    loads[4].wait()

    def update(index, gradients, rate, decay, master_at=None):
        m_at, v_at = 4 + index, 9 + index
        for at in (m_at, v_at) if index == 4 else (index, m_at, v_at):
            loads[5 + at].wait()
        for part, gradient in enumerate(gradients):
            at = (lambda ref: ref.at[part]) if index == 0 else (lambda ref: ref)
            master = master_at if index == 4 else at(params[index])[...]
            values = adam_update(
                master, at(params[m_at])[...], at(params[v_at])[...], gradient, clip, rate, decay
            )
            for which, value in enumerate(values):
                at(updated[3 * index + which])[...] = value
        for which in range(3):
            store(updated[3 * index + which], targets[3 * index + which])

    part = params[0].shape[2]
    update(3, [shards[2]], RATE_DOWNWARD, WEIGHT_DECAY)
    update(2, [shards[1]], RATE_UPWARD, WEIGHT_DECAY)
    update(
        0, [shards[0, :, i * part : (i + 1) * part] for i in range(3)], RATE_INWARD, WEIGHT_DECAY
    )
    update(1, [shards[0, :, 3 * part :].T], RATE_OUTWARD, WEIGHT_DECAY)
    span = params[8].shape[1]
    own_sums = sums[:, 0:span]
    own_norms = norms[:, 0:span]
    for index in range(1, 8):
        here = place[0] == index
        columns = slice(index * span, (index + 1) * span)
        own_sums = jnp.where(here, sums[:, columns], own_sums)
        own_norms = jnp.where(here, norms[:, columns], own_norms)
    update(4, [own_sums], RATE_NORMS, 0.0, own_norms)
    for copy in stores:
        copy.wait()


def fused_body(
    tokens, cotangent, step_counts, wrist_flags,
    inward_weight, outward_weight, upward_weight, downward_weight, norm_table,
    momentum_inward, momentum_outward, momentum_upward, momentum_downward, momentum_norms,
    variance_inward, variance_outward, variance_upward, variance_downward, variance_norms,
):
    width = norm_table.shape[1]
    block = upward_weight.shape[0]
    any_spec = pl.BlockSpec(memory_space=pl.ANY)
    vmem = pl.BlockSpec(memory_space=pltpu.VMEM)
    smem = pl.BlockSpec(memory_space=pltpu.SMEM)
    rows = pltpu.VMEM((2, ROWS, width), BF16)
    halves = pltpu.VMEM((2, HALF, width), BF16)
    keep = pltpu.VMEM((2, HALF, width), F32)
    output, grads, shards, table = pl.pallas_call(
        fused_kernel,
        out_shape=(
            jax.ShapeDtypeStruct((2, ROWS, width), BF16),
            jax.ShapeDtypeStruct((2, ROWS, width), BF16),
            jax.ShapeDtypeStruct((3, block, width), F32),
            jax.ShapeDtypeStruct((8, width), F32),
        ),
        in_specs=[smem, smem, any_spec, any_spec, any_spec, any_spec, any_spec, any_spec, vmem],
        out_specs=(any_spec, any_spec, vmem, vmem),
        scratch_shapes=[
            pltpu.VMEM((3, width, width), BF16),
            pltpu.VMEM((2, SLOTS, width), BF16),
            pltpu.VMEM((2, SLOTS, width), BF16),
            rows,
            pltpu.VMEM((6, ROWS, HEAD_DIM), BF16),
            pltpu.VMEM((6, KEYS, HEAD_DIM), BF16),
            pltpu.VMEM((6, KEYS, HEAD_DIM), BF16),
            pltpu.VMEM((6, ROWS, KEYS), BF16),
            pltpu.VMEM((6, ROWS, HEAD_DIM), BF16),
            pltpu.VMEM((2, ROWS, 192), BF16),
            keep,
            rows,
            rows,
            rows,
            rows,
            halves,
            halves,
            keep,
            keep,
            halves,
            halves,
            halves,
            halves,
            halves,
            halves,
            halves,
            halves,
            keep,
            pltpu.VMEM((2, ROWS, 576), BF16),
            pltpu.VMEM((2, width, width), F32),
            pltpu.VMEM((3, 4, block, width), BF16),
            pltpu.VMEM((3, 4, block, width), BF16),
            pltpu.VMEM((3, 3, block, width), BF16),
            pltpu.VMEM((8, width), F32),
            pltpu.VMEM((8, width // 3), F32),
            pltpu.VMEM((10, 8, width // 3), F32),
            pltpu.VMEM((8, width // 3), F32),
            pltpu.VMEM((10, 8, width // 3), F32),
            pltpu.VMEM(inward_weight.shape, F32),
            pltpu.VMEM(outward_weight.shape, F32),
            pltpu.VMEM(upward_weight.shape, F32),
            pltpu.VMEM(upward_weight.shape, F32),
            pltpu.SemaphoreType.DMA((N_REMOTE,)),
            pltpu.SemaphoreType.DMA((N_REMOTE,)),
            pltpu.SemaphoreType.DMA((10,)),
        ],
        compiler_params=pltpu.CompilerParams(
            collective_id=0, has_side_effects=True, vmem_limit_bytes=VMEM_BYTES
        ),
        name="block_step",
    )(
        step_counts,
        wrist_flags,
        inward_weight,
        outward_weight,
        upward_weight,
        downward_weight.T,
        tokens,
        cotangent,
        norm_table,
    )
    place = jnp.reshape(lax.axis_index("dp"), (1,)).astype(jnp.int32)
    params = (
        inward_weight, outward_weight, upward_weight, downward_weight.T,
        momentum_inward, momentum_outward, momentum_upward, momentum_downward.T, momentum_norms,
        variance_inward, variance_outward, variance_upward, variance_downward.T, variance_norms,
    )
    shapes = [param.shape for param in params]
    updates = [shape for shape in shapes[:4] + shapes[8:9] for _ in range(3)]
    padded = pltpu.VMEM((2, ROWS, width), BF16)
    results = pl.pallas_call(
        update_kernel,
        out_shape=(
            jax.ShapeDtypeStruct((2, SLOTS, width), BF16),
            jax.ShapeDtypeStruct((2, SLOTS, width), F32),
            jax.ShapeDtypeStruct((1, 1), F32),
            *[jax.ShapeDtypeStruct(shape, F32) for shape in updates],
        ),
        in_specs=[smem] + [any_spec] * 19,
        out_specs=(any_spec, any_spec, vmem) + (any_spec,) * 15,
        scratch_shapes=[
            padded,
            padded,
            pltpu.VMEM((2, SLOTS, width), BF16),
            pltpu.VMEM((2, SLOTS, width), F32),
            pltpu.VMEM((3, block, width), F32),
            pltpu.VMEM((8, width), F32),
            pltpu.VMEM((4, width), F32),
            *[pltpu.VMEM(shape, F32) for shape in shapes],
            *[pltpu.VMEM(shape, F32) for shape in updates],
            pltpu.SemaphoreType.DMA((19,)),
            pltpu.SemaphoreType.DMA((18,)),
        ],
        compiler_params=pltpu.CompilerParams(vmem_limit_bytes=VMEM_BYTES),
        name="update_step",
    )(place, output, grads, shards, table, norm_table, *params)
    updated = list(results[3:])
    for index in (9, 10, 11):
        updated[index] = updated[index].T
    return (results[0], results[1], results[2][0, 0], *updated)


def solution(mesh):
    fits = mesh.shape["dp"] == 8 and mesh.shape["mp"] == 4
    return whole_program(mesh, fused_body if fits else body)
```
